128 devices in a mesh: owner: 32 (over y, z, core), split: 4 (over x).
Axes of the slice: x: 4, y: 4, z: 4, core: 2. Of those that a mesh axis runs over, the one named last changes fastest.
Arguments:
- embeddings: bfloat16 [131072, 768], P(('owner', 'split')), may hold values from -6 to 6
- cluster: int32 [131072], P(('owner', 'split')), may hold values from 0 to 31, as said below
- order: int32 [131072], P(('owner', 'split')), may hold values from 0 to 131071, each once
Outputs:
- max_cosine: float32 [131072], P(('owner', 'split'))
The draws below stay inside these ranges and needn't reach their ends.
Inputs may be any that keep to these rules, and one draw needn't show every extreme that they name: Cluster c belongs to owner c. Of one device's rows at most 64 lie in clusters of one owner and at most 64 in one cluster; on every device some owner receives exactly 64 and each of its clusters exactly 64. `order`: all ranks are distinct.
All inputs are finite; a program needn't handle non-finite values.
Results may differ from the reference program's by a relative error of at most 0.0013.
Values may be sent and summed in bfloat16 or wider, within the bound.
No kernel may reach another device: no remote copies, remote signals or barrier semaphores. Data moves between devices by JAX's collectives and lax.ppermute only.
A program may use at most 64 MiB of HBM per device.

```python
import jax
import jax.numpy as jnp
from jax import lax

D = 768
ROWS_DEV = 1024
CLUS_OWN = 1
CAP = 64
SLOTS = 64
ROWS = 131072
CLUSTERS = 32
MEMBERS_MAX = 8192
N_OWNER = 32


def draw_cluster(key, part):
    key = jax.random.fold_in(key, 7)
    block_keys = jax.random.split(key, ROWS // ROWS_DEV)

    def one_block(block_key):
        first_key, second_key, third_key = jax.random.split(block_key, 3)
        full_owner = jax.random.randint(first_key, (), 0, N_OWNER)
        priority = jax.random.permutation(second_key, 2 * ROWS_DEV).astype(jnp.int32)
        slot_ids = jnp.arange(2 * ROWS_DEV, dtype=jnp.int32)
        priority = jnp.where(slot_ids // CAP == full_owner, priority - 2 * ROWS_DEV, priority)
        chosen = jnp.argsort(priority)[:ROWS_DEV].astype(jnp.int32)
        chosen = jax.random.permutation(third_key, chosen)
        return (chosen // CAP * CLUS_OWN + chosen % CAP // SLOTS).astype(jnp.int32)
    return jax.vmap(one_block)(block_keys).reshape(-1).astype(jnp.int32)


def levels(stream_key, dims, cuts, least, largest):
    def one(axis_at, parts):
        heights = jax.random.uniform(jax.random.fold_in(jax.random.fold_in(stream_key, 6), axis_at), (parts,), jnp.float32, least / len(cuts), largest / len(cuts))
        return jnp.repeat(jnp.exp(heights), dims[axis_at] // parts).reshape((-1,) + (1,) * (len(dims) - axis_at - 1))

    loudness = one(*cuts[0])
    for cut in cuts[1:]:
        loudness = loudness * one(*cut)
    return loudness


def gaussian(own_key, dims, width, reach, cuts=(), held_as=jnp.bfloat16):
    level = levels(own_key, dims, cuts, -0.22, 0.18) if cuts else 1.0
    values = jax.random.normal(own_key, dims, jnp.float32) * width * level
    return jnp.minimum(jnp.maximum(values, -reach), reach).astype(held_as)


def setup_inputs(seed: int = 0) -> dict:
    arg_keys = jax.random.split(jax.random.key(seed), 4)
    return {
        "embeddings": gaussian(arg_keys[0], (ROWS, D), 1.0, 6.0, ((0, 128),)),
        "cluster": draw_cluster(jax.random.fold_in(arg_keys[3], 71), 0),
        "order": jax.random.permutation(arg_keys[2], ROWS).astype(jnp.int32),
    }


def reference(embeddings, cluster, order):
    values = embeddings.astype(jnp.float32)
    unit_rows = (values * lax.rsqrt(lax.optimization_barrier(jnp.sum(values * values, axis=1, keepdims=True)) + 1e-06)).astype(jnp.bfloat16)
    sort_key = cluster * ROWS + order
    ordering = jnp.argsort(sort_key).astype(jnp.int32)
    sorted_units = unit_rows[ordering]
    sorted_labels = cluster[ordering]
    sorted_ranks = order[ordering]
    cluster_size = lax.optimization_barrier(jnp.sum((cluster[:, None] == jnp.arange(CLUSTERS, dtype=jnp.int32)[None, :]).astype(jnp.int32), axis=0))
    cluster_start = (jnp.cumsum(cluster_size) - cluster_size).astype(jnp.int32)
    padded_units = jnp.concatenate([sorted_units, jnp.zeros((MEMBERS_MAX, D), sorted_units.dtype)], axis=0)
    padded_labels = jnp.concatenate([sorted_labels, jnp.full((MEMBERS_MAX,), -1, jnp.int32)], axis=0)
    padded_ranks = jnp.concatenate([sorted_ranks, jnp.zeros((MEMBERS_MAX,), jnp.int32)], axis=0)

    def per_cluster(label):
        begin = cluster_start[label].astype(jnp.int32)
        members = lax.dynamic_slice(padded_units, (begin, jnp.int32(0)), (MEMBERS_MAX, D))
        labels = lax.dynamic_slice(padded_labels, (begin,), (MEMBERS_MAX,))
        ranks = lax.dynamic_slice(padded_ranks, (begin,), (MEMBERS_MAX,))
        member = labels == label
        scores = jnp.dot(members, members.T, preferred_element_type=jnp.float32)
        earlier = member[:, None] & member[None, :] & (ranks[None, :] < ranks[:, None])
        best_score = lax.optimization_barrier(jnp.max(jnp.where(earlier, scores, -1.0), axis=1))
        targets = jnp.where(member, begin + jnp.arange(MEMBERS_MAX, dtype=jnp.int32), ROWS)
        return (best_score, targets)
    best_all, target_all = lax.map(per_cluster, jnp.arange(CLUSTERS, dtype=jnp.int32))
    sorted_best = jnp.zeros((ROWS,), jnp.float32).at[target_all.reshape(-1)].set(best_all.reshape(-1), mode='drop')
    return jnp.zeros((ROWS,), jnp.float32).at[ordering].set(sorted_best)
```

```python
import jax
import jax.numpy as jnp
from jax import lax
from jax.experimental import pallas as pl
from jax.experimental.pallas import tpu as pltpu
from jax.sharding import PartitionSpec as P

D = 768
LANES = 128
BLOCKS = D // LANES
SLOTS = 16
DATA = SLOTS * BLOCKS
MSG = DATA + 8
CLUSTERS = 32
PEERS = 128
ROWS = PEERS * SLOTS
LATE = 320
FAR = float(2**20)
AXES = ("owner", "split")
VMEM = 56 * 2**20


def place_of(cluster, index):
    late = index >> 5
    core = index & 1
    chip = cluster >> 1
    column = 2 * (cluster & 1) + late
    return (chip * 2 + core) * 4 + column, (index & 31) >> 1


def iota(shape, axis):
    return lax.broadcasted_iota(jnp.int32, shape, axis)


def ones_where(mask):
    return jnp.where(mask, 1.0, 0.0).astype(jnp.bfloat16)


def dot_nt(a, b, **kw):
    return lax.dot_general(a, b, (((1,), (1,)), ((), ())), preferred_element_type=jnp.float32, **kw)


def dot_nn(a, b, **kw):
    return lax.dot_general(a, b, (((1,), (0,)), ((), ())), preferred_element_type=jnp.float32, **kw)


def exact_nt(a, b):
    return dot_nt(a, b, precision=lax.Precision.HIGHEST)


def exact_nn(a, b):
    return dot_nn(a, b, precision=lax.Precision.HIGHEST)


def pack_kernel(emb_ref, cluster_ref, order_ref, out_ref, index_ref, unit_ref, target_ref, meta_ref):
    step = pl.program_id(0)
    rows = emb_ref.shape[0]
    tile = PEERS // pl.num_programs(0)

    @pl.when(step == 0)
    def _():
        values = emb_ref[...].astype(jnp.float32)
        total = jnp.sum(values * values, axis=1, keepdims=True)
        unit_ref[...] = (values * lax.rsqrt(total + 1e-06)).astype(jnp.bfloat16)
        cluster = cluster_ref[...]
        rank = order_ref[...]
        hit = iota((CLUSTERS, rows), 0) == cluster
        hits = ones_where(hit)
        upper = ones_where(iota((LANES, LANES), 0) <= iota((LANES, LANES), 1))
        running = jnp.zeros((CLUSTERS, 1), jnp.float32)
        parts = []
        for block in range(rows // LANES):
            part = dot_nn(hits[:, block * LANES:(block + 1) * LANES], upper) + running
            running = part[:, LANES - 1:LANES]
            parts.append(part)
        counted = jnp.concatenate(parts, axis=1)
        index = jnp.sum(jnp.where(hit, counted, 0.0), axis=0, keepdims=True).astype(jnp.int32) - 1
        index_ref[...] = index
        peer, slot = place_of(cluster, index)
        target_ref[...] = peer * SLOTS + slot
        to_peer = jnp.where(iota((PEERS, rows), 0) == peer, 1.0, 0.0)
        high = (rank >> 9).astype(jnp.float32)
        low = ((rank & 511) - 256).astype(jnp.float32)
        lane = iota((LANES, rows), 0)
        meta = dot_nt((to_peer * high).astype(jnp.bfloat16), ones_where(lane == slot))
        meta += dot_nt((to_peer * low).astype(jnp.bfloat16), ones_where(lane == slot + SLOTS))
        meta += dot_nt(to_peer.astype(jnp.bfloat16), ones_where(lane == slot + 2 * SLOTS))
        meta += dot_nt(jnp.ones((PEERS, rows), jnp.bfloat16), ones_where(lane == cluster + 64))
        meta_ref[...] = meta

    chosen = ones_where(iota((tile * SLOTS, rows), 0) + step * tile * SLOTS == target_ref[...])
    packed = dot_nn(chosen, unit_ref[...]).astype(jnp.bfloat16)
    for block in range(BLOCKS):
        out_ref[:, block * SLOTS:(block + 1) * SLOTS, :] = packed[
            :, block * LANES:(block + 1) * LANES
        ].reshape(tile, SLOTS, LANES)
    start = pl.multiple_of(step * tile, tile)
    meta = meta_ref[pl.ds(start, tile), :]
    out_ref[:, DATA:MSG, :] = jnp.broadcast_to(meta[:, None, :], (tile, 8, LANES)).astype(jnp.bfloat16)


def pack(embeddings, cluster, order):
    rows = embeddings.shape[0]
    steps = 4
    return pl.pallas_call(
        pack_kernel,
        grid=(steps,),
        in_specs=[
            pl.BlockSpec((rows, D), lambda i: (0, 0)),
            pl.BlockSpec((1, rows), lambda i: (0, 0)),
            pl.BlockSpec((1, rows), lambda i: (0, 0)),
        ],
        out_specs=[
            pl.BlockSpec((PEERS // steps, MSG, LANES), lambda i: (i, 0, 0)),
            pl.BlockSpec((1, rows), lambda i: (0, 0)),
        ],
        out_shape=[
            jax.ShapeDtypeStruct((PEERS, MSG, LANES), jnp.bfloat16),
            jax.ShapeDtypeStruct((1, rows), jnp.int32),
        ],
        scratch_shapes=[
            pltpu.VMEM((rows, D), jnp.bfloat16),
            pltpu.VMEM((1, rows), jnp.int32),
            pltpu.VMEM((PEERS, LANES), jnp.float32),
        ],
        compiler_params=pltpu.CompilerParams(vmem_limit_bytes=VMEM),
        name="pack",
    )(embeddings, cluster.reshape(1, rows), order.reshape(1, rows))


def units_of(ref, start, count):
    first, peers = start // SLOTS, count // SLOTS
    return jnp.concatenate(
        [
            ref[first:first + peers, b * SLOTS:(b + 1) * SLOTS, :].reshape(count, LANES)
            for b in range(BLOCKS)
        ],
        axis=1,
    )


def meta_of(ref):
    whole = ref[:, DATA:MSG, :].astype(jnp.float32).reshape(PEERS * 8, LANES).astype(jnp.bfloat16)
    pick = ones_where(iota((PEERS, PEERS * 8), 1) == iota((PEERS, PEERS * 8), 0) * 8)
    return dot_nn(pick, whole)


def rank_weight(place, slot):
    weight = jnp.where(place == slot, 512.0, 0.0) + jnp.where(place == slot + SLOTS, 1.0, 0.0)
    return weight - jnp.where(place == slot + 2 * SLOTS, FAR, 0.0)


def rank_column(meta):
    spread = ones_where(iota((ROWS, PEERS), 0) >> 4 == iota((ROWS, PEERS), 1))
    wide = dot_nn(spread, meta.astype(jnp.bfloat16))
    weight = rank_weight(iota((ROWS, LANES), 1), iota((ROWS, LANES), 0) & 15)
    return jnp.sum(wide * weight, axis=1, keepdims=True) + (256.0 + FAR)


def rank_row(meta):
    spread = ones_where(iota((PEERS, ROWS), 1) >> 4 == iota((PEERS, ROWS), 0))
    wide = dot_nn(meta.T.astype(jnp.bfloat16), spread)
    weight = rank_weight(iota((LANES, ROWS), 0), iota((LANES, ROWS), 1) & 15)
    return jnp.sum(wide * weight, axis=0, keepdims=True) + (256.0 + FAR)


def table_of_column(best, base):
    spread = jnp.where(iota((PEERS, ROWS), 1) >> 4 == iota((PEERS, ROWS), 0), 1.0, 0.0)
    placed = jnp.where(iota((ROWS, LANES), 1) == (iota((ROWS, LANES), 0) & 15) + base, best, 0.0)
    return exact_nn(spread, placed)


def table_of_row(best, base):
    spread = jnp.where(iota((PEERS, ROWS), 1) >> 4 == iota((PEERS, ROWS), 0), 1.0, 0.0)
    placed = jnp.where(iota((LANES, ROWS), 0) == (iota((LANES, ROWS), 1) & 15) + base, best, 0.0)
    return exact_nt(spread, placed)


def late_kernel(round_ref, msg_ref, out_ref, most_ref):
    meta = meta_of(msg_ref)
    counts = meta[:, 64:64 + CLUSTERS]
    extra = jnp.maximum(counts - 32.0, 0.0)
    half = jnp.floor((extra + 1.0) * 0.5)
    most_ref[...] = jnp.max(jnp.sum(half, axis=0, keepdims=True), axis=1, keepdims=True).astype(jnp.int32)

    held = jnp.sum(
        jnp.where((iota((PEERS, LANES), 1) >> 4) == 2, meta, 0.0), axis=1, keepdims=True
    )
    before = ones_where(iota((PEERS, PEERS), 1) < iota((PEERS, PEERS), 0))
    begin = dot_nn(before, jnp.broadcast_to(held, (PEERS, LANES)).astype(jnp.bfloat16))
    both = jnp.where(iota((PEERS, LANES), 1) == 0, begin, jnp.where(iota((PEERS, LANES), 1) == 1, held, 0.0))
    spread = jnp.where(iota((PEERS, ROWS), 1) >> 4 == iota((PEERS, ROWS), 0), 1.0, 0.0)
    wide = exact_nn(both.T, spread)
    slot = iota((1, ROWS), 1) & 15
    begin_row = (wide[0:1, :] + 0.5).astype(jnp.int32)
    held_row = (wide[1:2, :] + 0.5).astype(jnp.int32)
    position = jnp.where(slot < held_row, begin_row + slot - round_ref[0] * LATE, -1)
    chosen = ones_where(iota((LATE, ROWS), 0) == position)
    wide_meta = dot_nn(
        ones_where(iota((ROWS, PEERS), 0) >> 4 == iota((ROWS, PEERS), 1)), meta.astype(jnp.bfloat16)
    )
    lane = iota((ROWS, LANES), 1)
    slot_col = iota((ROWS, LANES), 0) & 15
    peer_col = iota((ROWS, LANES), 0) >> 4
    high = jnp.sum(jnp.where(lane == slot_col, wide_meta, 0.0), axis=1, keepdims=True)
    low = jnp.sum(jnp.where(lane == slot_col + SLOTS, wide_meta, 0.0), axis=1, keepdims=True)
    facts = jnp.where(lane == 0, high, 0.0) + jnp.where(lane == 1, low, 0.0)
    facts += jnp.where(lane == 2, 1.0, 0.0)
    facts += jnp.where(lane == 3, peer_col.astype(jnp.float32), 0.0)
    facts += jnp.where(lane == 4, slot_col.astype(jnp.float32), 0.0)
    data = jnp.concatenate([units_of(msg_ref, 0, ROWS), facts.astype(jnp.bfloat16)], axis=1)
    out_ref[...] = dot_nn(chosen, data).astype(jnp.bfloat16)


def gather_late(round_at, msg):
    return pl.pallas_call(
        late_kernel,
        in_specs=[
            pl.BlockSpec(memory_space=pltpu.SMEM),
            pl.BlockSpec(memory_space=pltpu.VMEM),
        ],
        out_specs=[pl.BlockSpec(memory_space=pltpu.VMEM)] * 2,
        out_shape=[
            jax.ShapeDtypeStruct((LATE, D + LANES), jnp.bfloat16),
            jax.ShapeDtypeStruct((1, 1), jnp.int32),
        ],
        compiler_params=pltpu.CompilerParams(vmem_limit_bytes=VMEM),
        name="late",
    )(round_at, msg)


BLOCK = 512


def pairs_kernel(core_ref, own_ref, other_ref, out_ref, rows_ref, cols_ref):
    core = core_ref[0]
    own_meta = meta_of(own_ref)
    other_meta = meta_of(other_ref)
    column = rank_column(own_meta)
    row = rank_row(own_meta)
    count = ROWS // BLOCK
    rows_ref[...] = jnp.full((ROWS, LANES), -1.0, jnp.float32)
    cols_ref[...] = jnp.full((8, ROWS), -1.0, jnp.float32)
    tiles = [units_of(own_ref, i * BLOCK, BLOCK) for i in range(count)]

    def narrow_rows(x):
        best = x[:, :LANES]
        for b in range(1, x.shape[1] // LANES):
            best = jnp.maximum(best, x[:, b * LANES:(b + 1) * LANES])
        return best

    def narrow_cols(x):
        return jnp.max(x.reshape(x.shape[0] // 8, 8, x.shape[1]), axis=0)

    def score(left, right, left_rank, right_rank, rows_at, cols_at, both):
        scores = dot_nt(left, right)
        earlier = right_rank < left_rank
        kept = narrow_rows(jnp.where(earlier, scores, -1.0))
        rows_ref[rows_at, :] = jnp.maximum(rows_ref[rows_at, :], kept)
        if both:
            kept = narrow_cols(jnp.where(earlier, -1.0, scores))
            cols_ref[:, cols_at] = jnp.maximum(cols_ref[:, cols_at], kept)

    def span(i):
        return slice(i * BLOCK, (i + 1) * BLOCK)

    for i in range(count):
        for j in range(i, count):
            score(tiles[i], tiles[j], column[span(i), :], row[:, span(j)], span(i), span(j), i != j)
    own_column = jnp.max(rows_ref[...], axis=1, keepdims=True)
    own_row = jnp.max(cols_ref[...], axis=0, keepdims=True)
    own_table = jnp.maximum(table_of_column(own_column, 0), table_of_row(own_row, 0))

    rows_ref[...] = jnp.full((ROWS, LANES), -1.0, jnp.float32)
    cols_ref[...] = jnp.full((8, ROWS), -1.0, jnp.float32)

    def across(big_ref, small_ref, big_meta, small_meta, half):
        big_column = rank_column(big_meta)
        small_row = rank_row(small_meta)
        for j in range(half * count // 2, (half + 1) * count // 2):
            right = units_of(small_ref, j * BLOCK, BLOCK)
            for i in range(count):
                left = units_of(big_ref, i * BLOCK, BLOCK)
                score(left, right, big_column[span(i), :], small_row[:, span(j)], span(i), span(j), True)

    @pl.when(core == 0)
    def _():
        across(own_ref, other_ref, own_meta, other_meta, 0)

    @pl.when(core == 1)
    def _():
        across(other_ref, own_ref, other_meta, own_meta, 1)

    first = table_of_column(jnp.max(rows_ref[...], axis=1, keepdims=True), 0)
    second = table_of_row(jnp.max(cols_ref[...], axis=0, keepdims=True), SLOTS)
    lane = iota((PEERS, LANES), 1)
    own_at_first = jnp.where(lane < SLOTS, own_table, -1.0)
    own_at_second = jnp.where(lane >> 4 == 1, pltpu.roll(own_table, SLOTS, 1), -1.0)
    across_table = jnp.where(lane < SLOTS, first, jnp.where(lane < 2 * SLOTS, second, -1.0))
    out_ref[...] = jnp.maximum(across_table, jnp.where(core == 0, own_at_first, own_at_second))


def score_pairs(core, own, other):
    return pl.pallas_call(
        pairs_kernel,
        in_specs=[
            pl.BlockSpec(memory_space=pltpu.SMEM),
            pl.BlockSpec(memory_space=pltpu.VMEM),
            pl.BlockSpec(memory_space=pltpu.VMEM),
        ],
        out_specs=pl.BlockSpec(memory_space=pltpu.VMEM),
        out_shape=jax.ShapeDtypeStruct((PEERS, LANES), jnp.float32),
        scratch_shapes=[
            pltpu.VMEM((ROWS, LANES), jnp.float32),
            pltpu.VMEM((8, ROWS), jnp.float32),
        ],
        compiler_params=pltpu.CompilerParams(vmem_limit_bytes=VMEM),
        name="pairs",
    )(core, own, other)


def late_pairs_kernel(core_ref, late_ref, own_ref, other_ref, table_ref, out_ref):
    core = core_ref[0]
    late = late_ref[:, :D]
    facts = late_ref[:, D:].astype(jnp.float32)
    late_rank = facts[:, 0:1] * 512.0 + facts[:, 1:2] - facts[:, 2:3] * FAR + (256.0 + FAR)
    late_best = jnp.full((LATE, LANES), -1.0, jnp.float32)
    tables = []
    for ref in (own_ref, other_ref):
        row = rank_row(meta_of(ref))
        parts = []
        for j in range(ROWS // BLOCK):
            scores = dot_nt(late, units_of(ref, j * BLOCK, BLOCK))
            earlier = row[:, j * BLOCK:(j + 1) * BLOCK] < late_rank
            kept = jnp.where(earlier, scores, -1.0)
            for b in range(BLOCK // LANES):
                late_best = jnp.maximum(late_best, kept[:, b * LANES:(b + 1) * LANES])
            parts.append(jnp.max(jnp.where(earlier, -1.0, scores), axis=0, keepdims=True))
        tables.append(table_of_row(jnp.concatenate(parts, axis=1), 0))
    best = jnp.max(late_best, axis=1, keepdims=True)
    lane = iota((LATE, LANES), 1)
    here = lane == facts[:, 4:5].astype(jnp.int32) + 2 * SLOTS
    peers = jnp.where(
        (lane == facts[:, 3:4].astype(jnp.int32)) & (facts[:, 2:3] > 0.5), 1.0, 0.0
    )
    filled = dot_nn(peers.T.astype(jnp.bfloat16), ones_where(here))
    late_table = jnp.where(filled > 0.5, exact_nn(peers.T, jnp.where(here, best, 0.0)), -1.0)
    lane = iota((PEERS, LANES), 1)
    moved = [pltpu.roll(t, SLOTS, 1) for t in tables]
    first = jnp.where(core == 0, tables[0], tables[1])
    second = jnp.where(core == 0, moved[1], moved[0])
    table = jnp.where(lane < SLOTS, first, jnp.where(lane < 2 * SLOTS, second, late_table))
    out_ref[...] = jnp.maximum(table_ref[...], table)


def score_late(core, late, own, other, table):
    return pl.pallas_call(
        late_pairs_kernel,
        in_specs=[pl.BlockSpec(memory_space=pltpu.SMEM)] + [pl.BlockSpec(memory_space=pltpu.VMEM)] * 4,
        out_specs=pl.BlockSpec(memory_space=pltpu.VMEM),
        out_shape=jax.ShapeDtypeStruct((PEERS, LANES), jnp.float32),
        compiler_params=pltpu.CompilerParams(vmem_limit_bytes=VMEM),
        name="late_pairs",
    )(core, late, own, other, table)


def reply_kernel(table_ref, cluster_ref, index_ref, out_ref):
    cluster = cluster_ref[...]
    index = index_ref[...]
    rows = cluster.shape[1]
    peer, slot = place_of(cluster, index)
    core = index & 1
    late = index >> 5
    table = table_ref[...].T
    at = iota((PEERS, rows), 0)
    first = exact_nn(table, jnp.where(at == peer - 4 * core, 1.0, 0.0))
    second = exact_nn(table, jnp.where(at == peer - 4 * core + 4, 1.0, 0.0))
    beside = exact_nn(table, jnp.where(at == peer - 1, 1.0, 0.0))
    lane = iota((LANES, rows), 0)
    best = jnp.where(lane == core * SLOTS + slot, jnp.maximum(first, second), -1.0)
    best = jnp.maximum(best, jnp.where((lane == 2 * SLOTS + slot) & (late == 1), beside, -1.0))
    out_ref[...] = jnp.max(best, axis=0, keepdims=True)


def read_reply(table, cluster, index):
    rows = cluster.shape[0]
    best = pl.pallas_call(
        reply_kernel,
        in_specs=[pl.BlockSpec(memory_space=pltpu.VMEM)] * 3,
        out_specs=pl.BlockSpec(memory_space=pltpu.VMEM),
        out_shape=jax.ShapeDtypeStruct((1, rows), jnp.float32),
        compiler_params=pltpu.CompilerParams(vmem_limit_bytes=VMEM),
        name="reply",
    )(table, cluster.reshape(1, rows), index)
    return best.reshape(rows)


def device(chip, core, column):
    return (chip * 2 + core) * 4 + column


SWAP = [
    (device(chip, core, column), device(chip, 1 - core, column))
    for chip in range(16)
    for core in range(2)
    for column in range(4)
]
LATE_TO_EARLY = [
    (device(chip, core, 2 * pair + 1), device(chip, core, 2 * pair))
    for chip in range(16)
    for core in range(2)
    for pair in range(2)
]


def shards(embeddings, cluster, order):
    message, index = pack(embeddings, cluster, order)
    own = lax.all_to_all(message, AXES, split_axis=0, concat_axis=0, tiled=True)
    other = lax.ppermute(own, AXES, SWAP)
    core = (lax.axis_index("owner") % 2).astype(jnp.int32).reshape(1)
    rows, most = gather_late(jnp.zeros((1,), jnp.int32), own)
    late = lax.ppermute(rows, AXES, LATE_TO_EARLY)
    table = score_pairs(core, own, other)
    table = score_late(core, late, own, other, table)

    def more(state):
        return state[0] * LATE < most[0, 0]

    def one_round(state):
        rows, _ = gather_late(state[0].reshape(1), own)
        late = lax.ppermute(rows, AXES, LATE_TO_EARLY)
        return state[0] + 1, score_late(core, late, own, other, state[1])

    table = lax.while_loop(more, one_round, (jnp.int32(1), table))[1]
    replies = lax.all_to_all(table, AXES, split_axis=0, concat_axis=0, tiled=True)
    return read_reply(replies, cluster, index)


def solution(mesh):
    placed = (P(AXES, None), P(AXES), P(AXES))
    return jax.shard_map(
        shards, mesh=mesh, in_specs=placed, out_specs=P(AXES), check_vma=False
    )
```

```python
import jax
import jax.numpy as jnp
from jax import lax
from jax.experimental import pallas as pl
from jax.experimental.pallas import tpu as pltpu
from jax.sharding import PartitionSpec as P

D = 768
LANES = 128
BLOCKS = D // LANES
SLOTS = 16
DATA = SLOTS * BLOCKS
MSG = DATA + 8
CLUSTERS = 32
PEERS = 128
ROWS = PEERS * SLOTS
GROUPS = ROWS // LANES
GROUP = LANES // SLOTS
LATE = 256
FACTS = 16
FAR = float(2**20)
BLOCK = 512
AXES = ("owner", "split")
VMEM = 56 * 2**20


def place_of(cluster, index):
    late = index >> 5
    core = index & 1
    chip = cluster >> 1
    column = 2 * (cluster & 1) + late
    return (chip * 2 + core) * 4 + column, (index & 31) >> 1


def iota(shape, axis):
    return lax.broadcasted_iota(jnp.int32, shape, axis)


def ones_where(mask):
    return jnp.where(mask, 1.0, 0.0).astype(jnp.bfloat16)


def dot_nt(a, b):
    return lax.dot_general(a, b, (((1,), (1,)), ((), ())), preferred_element_type=jnp.float32)


def dot_nn(a, b):
    return lax.dot_general(a, b, (((1,), (0,)), ((), ())), preferred_element_type=jnp.float32)


def thirds(x):
    first = x.astype(jnp.bfloat16)
    left = x - first.astype(jnp.float32)
    second = left.astype(jnp.bfloat16)
    return first, second, (left - second.astype(jnp.float32)).astype(jnp.bfloat16)


def pack_kernel(emb_ref, cluster_ref, order_ref, out_ref, index_ref, unit_ref, target_ref, meta_ref):
    step = pl.program_id(0)
    rows = emb_ref.shape[0]
    tile = PEERS // pl.num_programs(0)

    @pl.when(step == 0)
    def _():
        values = emb_ref[...].astype(jnp.float32)
        total = jnp.sum(values * values, axis=1, keepdims=True)
        unit_ref[...] = (values * lax.rsqrt(total + 1e-06)).astype(jnp.bfloat16)
        cluster = cluster_ref[...]
        rank = order_ref[...]
        hit = iota((CLUSTERS, rows), 0) == cluster
        hits = ones_where(hit)
        upper = ones_where(iota((LANES, LANES), 0) <= iota((LANES, LANES), 1))
        running = jnp.zeros((CLUSTERS, 1), jnp.float32)
        parts = []
        for block in range(rows // LANES):
            part = dot_nn(hits[:, block * LANES:(block + 1) * LANES], upper) + running
            running = part[:, LANES - 1:LANES]
            parts.append(part)
        counted = jnp.concatenate(parts, axis=1)
        index = jnp.sum(jnp.where(hit, counted, 0.0), axis=0, keepdims=True).astype(jnp.int32) - 1
        index_ref[...] = index
        peer, slot = place_of(cluster, index)
        target_ref[...] = peer * SLOTS + slot
        to_peer = iota((PEERS, rows), 0) == peer
        high = ((rank >> 9) + 1).astype(jnp.float32)
        low = ((rank & 511) - 256).astype(jnp.float32)
        lane = iota((LANES, rows), 0)
        at_slot = ones_where((lane & (SLOTS - 1)) == slot)
        meta_ref[0] = dot_nt(jnp.where(to_peer, high, 0.0).astype(jnp.bfloat16), at_slot)
        meta_ref[1] = dot_nt(jnp.where(to_peer, low, 0.0).astype(jnp.bfloat16), at_slot)
        counts = dot_nt(jnp.ones((8, rows), jnp.bfloat16), ones_where(lane == cluster))
        meta_ref[2] = jnp.broadcast_to(counts[0:1, :], (PEERS, LANES))

    chosen = ones_where(iota((tile * SLOTS, rows), 0) + step * tile * SLOTS == target_ref[...])
    packed = dot_nn(chosen, unit_ref[...]).astype(jnp.bfloat16)
    for block in range(BLOCKS):
        out_ref[:, block * SLOTS:(block + 1) * SLOTS, :] = packed[
            :, block * LANES:(block + 1) * LANES
        ].reshape(tile, SLOTS, LANES)
    start = pl.multiple_of(step * tile, tile)
    high, low, counts = (meta_ref[i, pl.ds(start, tile), :][:, None, :] for i in range(3))
    at = iota((tile, 8, LANES), 1)
    meta = jnp.where(at == 0, high, jnp.where(at == 1, low, jnp.where(at == 2, counts, 0.0)))
    out_ref[:, DATA:MSG, :] = meta.astype(jnp.bfloat16)


def pack(embeddings, cluster, order):
    rows = embeddings.shape[0]
    steps = 4
    return pl.pallas_call(
        pack_kernel,
        grid=(steps,),
        in_specs=[
            pl.BlockSpec((rows, D), lambda i: (0, 0)),
            pl.BlockSpec((1, rows), lambda i: (0, 0)),
            pl.BlockSpec((1, rows), lambda i: (0, 0)),
        ],
        out_specs=[
            pl.BlockSpec((PEERS // steps, MSG, LANES), lambda i: (i, 0, 0)),
            pl.BlockSpec((1, rows), lambda i: (0, 0)),
        ],
        out_shape=[
            jax.ShapeDtypeStruct((PEERS, MSG, LANES), jnp.bfloat16),
            jax.ShapeDtypeStruct((1, rows), jnp.int32),
        ],
        scratch_shapes=[
            pltpu.VMEM((rows, D), jnp.bfloat16),
            pltpu.VMEM((1, rows), jnp.int32),
            pltpu.VMEM((3, PEERS, LANES), jnp.float32),
        ],
        compiler_params=pltpu.CompilerParams(vmem_limit_bytes=VMEM),
        name="pack",
    )(embeddings, cluster.reshape(1, rows), order.reshape(1, rows))


def units_of(ref, start, count):
    first, peers = start // SLOTS, count // SLOTS
    return jnp.concatenate(
        [
            ref[first:first + peers, b * SLOTS:(b + 1) * SLOTS, :].reshape(count, LANES)
            for b in range(BLOCKS)
        ],
        axis=1,
    )


def digits_of(ref):
    meta = ref[:, DATA:MSG, :].astype(jnp.float32).reshape(GROUPS, GROUP, 8, LANES)
    mine = iota((1, GROUP, 8, LANES), 3) >> 4 == iota((1, GROUP, 8, LANES), 1)
    held = jnp.sum(jnp.where(mine, meta, 0.0), axis=1)
    return held[:, 0:1, :], held[:, 1:2, :], meta


def rank_from(high, low):
    return jnp.where(high > 0.5, high * 512.0 + low, FAR)


def ranks_of(ref):
    high, low, _ = digits_of(ref)
    return rank_from(high, low)


def as_row(blocks):
    return jnp.concatenate([blocks[b] for b in range(GROUPS)], axis=1)


def as_columns(blocks, out_ref):
    for b in range(GROUPS):
        out_ref[b * LANES:(b + 1) * LANES, :] = jnp.broadcast_to(blocks[b], (LANES, LANES)).T


def row_of_best(ref):
    return jnp.concatenate(
        [
            jnp.max(ref[b * LANES:(b + 1) * LANES, :].T, axis=0, keepdims=True)
            for b in range(ref.shape[0] // LANES)
        ],
        axis=1,
    )


def late_kernel(round_ref, msg_ref, out_ref, most_ref):
    high, low, meta = digits_of(msg_ref)
    extra = jnp.maximum(meta[:, :, 2, :] - 32.0, 0.0)
    half = jnp.floor((extra + 1.0) * 0.5)
    most = jnp.sum(jnp.sum(half, axis=0), axis=0, keepdims=True)
    most = jnp.where(iota((1, LANES), 1) < CLUSTERS, most, 0.0)
    most_ref[...] = jnp.max(most, axis=1, keepdims=True).astype(jnp.int32)

    filled = jnp.concatenate([high[b] for b in range(GROUPS)], axis=0) > 0.5
    upper = ones_where(iota((LANES, LANES), 0) <= iota((LANES, LANES), 1))
    counted = dot_nn(ones_where(filled), upper)
    whole = jnp.broadcast_to(counted[:, LANES - 1:LANES], (GROUPS, LANES)).astype(jnp.bfloat16)
    below = ones_where(iota((GROUPS, GROUPS), 1) < iota((GROUPS, GROUPS), 0))
    position = (counted + dot_nn(below, whole)).astype(jnp.int32) - 1 - round_ref[0] * LATE
    position = jnp.where(filled, position, -1)
    position = jnp.concatenate([position[b:b + 1, :] for b in range(GROUPS)], axis=1)
    chosen = ones_where(iota((LATE, ROWS), 0) == position)
    out_ref[:LATE, :] = dot_nn(chosen, units_of(msg_ref, 0, ROWS)).astype(jnp.bfloat16)
    at = iota((FACTS, ROWS), 0)
    row = iota((FACTS, ROWS), 1)
    facts = jnp.where(at == 2, row >> 4, jnp.where(at == 3, row & 15, 0)).astype(jnp.float32)
    facts = jnp.where(at == 0, as_row(high), jnp.where(at == 1, as_row(low), facts))
    facts = dot_nt(facts.astype(jnp.bfloat16), chosen).astype(jnp.bfloat16)
    out_ref[LATE:, :LATE] = facts
    out_ref[LATE:, LATE:] = jnp.zeros((FACTS, D - LATE), jnp.bfloat16)


def gather_late(round_at, msg):
    return pl.pallas_call(
        late_kernel,
        in_specs=[
            pl.BlockSpec(memory_space=pltpu.SMEM),
            pl.BlockSpec(memory_space=pltpu.VMEM),
        ],
        out_specs=[pl.BlockSpec(memory_space=pltpu.VMEM)] * 2,
        out_shape=[
            jax.ShapeDtypeStruct((LATE + FACTS, D), jnp.bfloat16),
            jax.ShapeDtypeStruct((1, 1), jnp.int32),
        ],
        compiler_params=pltpu.CompilerParams(vmem_limit_bytes=VMEM),
        name="late",
    )(round_at, msg)


def narrow_rows(x):
    best = x[:, :LANES]
    for b in range(1, x.shape[1] // LANES):
        best = jnp.maximum(best, x[:, b * LANES:(b + 1) * LANES])
    return best


def narrow_cols(x):
    return jnp.max(x.reshape(x.shape[0] // 8, 8, x.shape[1]), axis=0)


def wide(column, count):
    return jnp.concatenate([column] * (count // LANES), axis=1)


def span(i):
    return slice(i * BLOCK, (i + 1) * BLOCK)


def pairs_kernel(core_ref, own_ref, other_ref, out_ref, rank_ref, rows_ref, cols_ref):
    core = core_ref[0]
    own_ranks = ranks_of(own_ref)
    other_ranks = ranks_of(other_ref)
    count = ROWS // BLOCK

    def score(left, right, left_rank, right_rank, rows_at, cols_at, both):
        scores = dot_nt(left, right)
        earlier = right_rank < wide(left_rank, BLOCK)
        kept = narrow_rows(jnp.where(earlier, scores, -1.0))
        rows_ref[rows_at, :] = jnp.maximum(rows_ref[rows_at, :], kept)
        if both:
            kept = narrow_cols(jnp.where(earlier, -1.0, scores))
            cols_ref[:, cols_at] = jnp.maximum(cols_ref[:, cols_at], kept)

    def clear():
        rows_ref[...] = jnp.full((ROWS, LANES), -1.0, jnp.float32)
        cols_ref[...] = jnp.full((8, ROWS), -1.0, jnp.float32)

    clear()
    as_columns(own_ranks, rank_ref)
    row = as_row(own_ranks)
    for i in range(count):
        left = units_of(own_ref, i * BLOCK, BLOCK)
        for j in range(i, count):
            right = units_of(own_ref, j * BLOCK, BLOCK)
            score(left, right, rank_ref[span(i), :], row[:, span(j)], span(i), span(j), i != j)
    own_best = jnp.maximum(row_of_best(rows_ref), jnp.max(cols_ref[...], axis=0, keepdims=True))

    clear()

    def across(big_ref, small_ref, big_ranks, small_ranks, half):
        as_columns(big_ranks, rank_ref)
        row = as_row(small_ranks)
        for j in range(half * count // 2, (half + 1) * count // 2):
            right = units_of(small_ref, j * BLOCK, BLOCK)
            for i in range(count):
                left = units_of(big_ref, i * BLOCK, BLOCK)
                score(left, right, rank_ref[span(i), :], row[:, span(j)], span(i), span(j), True)

    @pl.when(core == 0)
    def _():
        across(own_ref, other_ref, own_ranks, other_ranks, 0)

    @pl.when(core == 1)
    def _():
        across(other_ref, own_ref, other_ranks, own_ranks, 1)

    first = row_of_best(rows_ref)
    second = jnp.max(cols_ref[...], axis=0, keepdims=True)
    out_ref[0:1, :] = jnp.where(core == 0, jnp.maximum(own_best, first), first)
    out_ref[1:2, :] = jnp.where(core == 1, jnp.maximum(own_best, second), second)


def score_pairs(core, own, other):
    return pl.pallas_call(
        pairs_kernel,
        in_specs=[
            pl.BlockSpec(memory_space=pltpu.SMEM),
            pl.BlockSpec(memory_space=pltpu.VMEM),
            pl.BlockSpec(memory_space=pltpu.VMEM),
        ],
        out_specs=pl.BlockSpec(memory_space=pltpu.VMEM),
        out_shape=jax.ShapeDtypeStruct((2, ROWS), jnp.float32),
        scratch_shapes=[
            pltpu.VMEM((ROWS, LANES), jnp.float32),
            pltpu.VMEM((ROWS, LANES), jnp.float32),
            pltpu.VMEM((8, ROWS), jnp.float32),
        ],
        compiler_params=pltpu.CompilerParams(vmem_limit_bytes=VMEM),
        name="pairs",
    )(core, own, other)


def as_table(row):
    mine = iota((GROUP, LANES), 1) >> 4 == iota((GROUP, LANES), 0)
    parts = []
    for b in range(GROUPS):
        part = jnp.where(mine, row[:, b * LANES:(b + 1) * LANES], 0.0)
        for shift in (64, 32, 16):
            part = part + pltpu.roll(part, shift, 1)
        parts.append(part)
    return jnp.concatenate(parts, axis=0)


def late_pairs_kernel(core_ref, late_ref, own_ref, other_ref, best_ref, out_ref, rank_ref, rows_ref):
    core = core_ref[0]
    late = late_ref[:LATE, :]
    facts = late_ref[LATE:, :LATE].astype(jnp.float32)
    late_rank = rank_from(facts[0:1, :], facts[1:2, :])
    late_best = jnp.full((8, LATE), -1.0, jnp.float32)
    found = []
    for ref in (own_ref, other_ref):
        as_columns(ranks_of(ref), rank_ref)
        for i in range(ROWS // BLOCK):
            scores = dot_nt(units_of(ref, i * BLOCK, BLOCK), late)
            earlier = late_rank < wide(rank_ref[span(i), :], LATE)
            rows_ref[span(i), :] = narrow_rows(jnp.where(earlier, scores, -1.0))
            late_best = jnp.maximum(late_best, narrow_cols(jnp.where(earlier, -1.0, scores)))
        found.append(row_of_best(rows_ref))
    best = jnp.max(late_best, axis=0, keepdims=True)
    first = jnp.maximum(best_ref[0:1, :], jnp.where(core == 0, found[0], found[1]))
    second = jnp.maximum(best_ref[1:2, :], jnp.where(core == 0, found[1], found[0]))
    peer = jnp.where(facts[0:1, :] > 0.5, facts[2:3, :].astype(jnp.int32), -1)
    slot = facts[3:4, :].astype(jnp.int32)
    at_peer = ones_where(iota((PEERS, LATE), 0) == peer)
    lane = iota((LANES, LATE), 0)
    at_slot = (lane & 15) == slot
    late_table = dot_nt(at_peer, ones_where(at_slot))
    parts = thirds(best)
    late_best = sum(dot_nt(at_peer, jnp.where(at_slot, p.astype(jnp.float32), 0.0).astype(jnp.bfloat16)) for p in parts)
    late_table = jnp.where(late_table > 0.5, late_best, -1.0)
    lane = iota((PEERS, LANES), 1)
    out_ref[...] = jnp.where(
        lane < SLOTS, as_table(first), jnp.where(lane < 2 * SLOTS, as_table(second), late_table)
    )


def score_late(core, late, own, other, best):
    return pl.pallas_call(
        late_pairs_kernel,
        in_specs=[pl.BlockSpec(memory_space=pltpu.SMEM)] + [pl.BlockSpec(memory_space=pltpu.VMEM)] * 4,
        out_specs=pl.BlockSpec(memory_space=pltpu.VMEM),
        out_shape=jax.ShapeDtypeStruct((PEERS, LANES), jnp.float32),
        scratch_shapes=[
            pltpu.VMEM((ROWS, LANES), jnp.float32),
            pltpu.VMEM((ROWS, LANES), jnp.float32),
        ],
        compiler_params=pltpu.CompilerParams(vmem_limit_bytes=VMEM),
        name="late_pairs",
    )(core, late, own, other, best)


def reply_kernel(table_ref, cluster_ref, index_ref, out_ref):
    cluster = cluster_ref[...]
    index = index_ref[...]
    rows = cluster.shape[1]
    peer, slot = place_of(cluster, index)
    core = index & 1
    table = table_ref[...]
    lane = iota((PEERS, LANES), 1)
    row = iota((PEERS, LANES), 0)
    best = jnp.maximum(table, pltpu.roll(table, PEERS - 4, 0))
    beside = jnp.where(
        lane < SLOTS,
        pltpu.roll(pltpu.roll(table, 1, 0), LANES - 2 * SLOTS, 1),
        pltpu.roll(pltpu.roll(table, PEERS - 3, 0), LANES - SLOTS, 1),
    )
    best = jnp.where((row & 1) == 1, jnp.maximum(best, beside), best)
    chosen = ones_where(iota((PEERS, rows), 0) == peer - 4 * core)
    picked = sum(dot_nn(p, chosen) for p in thirds(best.T[:2 * SLOTS, :]))
    here = iota((2 * SLOTS, rows), 0) == core * SLOTS + slot
    out_ref[...] = jnp.max(jnp.where(here, picked, -1.0), axis=0, keepdims=True)


def read_reply(table, cluster, index):
    rows = cluster.shape[0]
    best = pl.pallas_call(
        reply_kernel,
        in_specs=[pl.BlockSpec(memory_space=pltpu.VMEM)] * 3,
        out_specs=pl.BlockSpec(memory_space=pltpu.VMEM),
        out_shape=jax.ShapeDtypeStruct((1, rows), jnp.float32),
        compiler_params=pltpu.CompilerParams(vmem_limit_bytes=VMEM),
        name="reply",
    )(table, cluster.reshape(1, rows), index)
    return best.reshape(rows)


def device(chip, core, column):
    return (chip * 2 + core) * 4 + column


SWAP = [
    (device(chip, core, column), device(chip, 1 - core, column))
    for chip in range(16)
    for core in range(2)
    for column in range(4)
]
LATE_TO_EARLY = [
    (device(chip, core, 2 * pair + 1), device(chip, core, 2 * pair))
    for chip in range(16)
    for core in range(2)
    for pair in range(2)
]


def shards(embeddings, cluster, order):
    message, index = pack(embeddings, cluster, order)
    own = lax.all_to_all(message, AXES, split_axis=0, concat_axis=0, tiled=True)
    other = lax.ppermute(own, AXES, SWAP)
    core = (lax.axis_index("owner") % 2).astype(jnp.int32).reshape(1)
    rows, most = gather_late(jnp.zeros((1,), jnp.int32), own)
    late = lax.ppermute(rows, AXES, LATE_TO_EARLY)
    best = score_pairs(core, own, other)
    table = score_late(core, late, own, other, best)

    def more(state):
        return state[0] * LATE < most[0, 0]

    def one_round(state):
        rows, _ = gather_late(state[0].reshape(1), own)
        late = lax.ppermute(rows, AXES, LATE_TO_EARLY)
        return state[0] + 1, jnp.maximum(state[1], score_late(core, late, own, other, best))

    table = lax.while_loop(more, one_round, (jnp.int32(1), table))[1]
    replies = lax.all_to_all(table, AXES, split_axis=0, concat_axis=0, tiled=True)
    return read_reply(replies, cluster, index)


def solution(mesh):
    placed = (P(AXES, None), P(AXES), P(AXES))
    return jax.shard_map(
        shards, mesh=mesh, in_specs=placed, out_specs=P(AXES), check_vma=False
    )
```

```python
import jax
import jax.numpy as jnp
from jax import lax
from jax.experimental import pallas as pl
from jax.experimental.pallas import tpu as pltpu
from jax.sharding import PartitionSpec as P

D = 768
LANES = 128
BLOCKS = D // LANES
SLOTS = 16
DATA = SLOTS * BLOCKS
MSG = DATA + 8
CLUSTERS = 32
PEERS = 128
ROWS = PEERS * SLOTS
GROUPS = ROWS // LANES
GROUP = LANES // SLOTS
LONE = 256
FACTS = 16
FAR = float(2**20)
BLOCK = 512
AXES = ("owner", "split")
VMEM = 56 * 2**20


def slot_of(index):
    return (index & 31) >> 1


def pair_of(cluster, index):
    return ((cluster >> 1) * 2 + (index & 1)) * 2 + (cluster & 1)


def iota(shape, axis):
    return lax.broadcasted_iota(jnp.int32, shape, axis)


def ones_where(mask):
    return jnp.where(mask, 1.0, 0.0).astype(jnp.bfloat16)


def dot_nt(a, b):
    return lax.dot_general(a, b, (((1,), (1,)), ((), ())), preferred_element_type=jnp.float32)


def dot_nn(a, b):
    return lax.dot_general(a, b, (((1,), (0,)), ((), ())), preferred_element_type=jnp.float32)


def thirds(x):
    first = x.astype(jnp.bfloat16)
    left = x - first.astype(jnp.float32)
    second = left.astype(jnp.bfloat16)
    return first, second, (left - second.astype(jnp.float32)).astype(jnp.bfloat16)


def pack_kernel(emb_ref, cluster_ref, order_ref, out_ref, index_ref, unit_ref, at_ref, some_ref, meta_ref):
    step = pl.program_id(0)
    rows = emb_ref.shape[0]
    pairs = PEERS // 2
    tile = pairs // pl.num_programs(0)

    def some_chosen(chunk):
        return ones_where(iota((LANES, rows), 0) + chunk * LANES == at_ref[1:2, :])

    @pl.when(step == 0)
    def _():
        values = emb_ref[...].astype(jnp.float32)
        total = jnp.sum(values * values, axis=1, keepdims=True)
        unit_ref[...] = (values * lax.rsqrt(total + 1e-06)).astype(jnp.bfloat16)
        cluster = cluster_ref[...]
        rank = order_ref[...]
        hit = iota((CLUSTERS, rows), 0) == cluster
        hits = ones_where(hit)
        upper = ones_where(iota((LANES, LANES), 0) <= iota((LANES, LANES), 1))
        running = jnp.zeros((CLUSTERS, 1), jnp.float32)
        parts = []
        for block in range(rows // LANES):
            part = dot_nn(hits[:, block * LANES:(block + 1) * LANES], upper) + running
            running = part[:, LANES - 1:LANES]
            parts.append(part)
        counted = jnp.concatenate(parts, axis=1)
        counts = jnp.broadcast_to(running, (CLUSTERS, LANES))
        below = ones_where(iota((CLUSTERS, CLUSTERS), 1) < iota((CLUSTERS, CLUSTERS), 0))
        over = jnp.maximum(counts - 32.0, 0.0)
        begin = dot_nn(below, over.astype(jnp.bfloat16))

        def of_row(x):
            return jnp.sum(jnp.where(hit, x, 0.0), axis=0, keepdims=True).astype(jnp.int32)

        index = of_row(counted) - 1
        count = of_row(running)
        index_ref[0:1, :] = index
        index_ref[1:2, :] = count
        slot = slot_of(index)
        pair = pair_of(cluster, index)
        first = index < 32
        last = index + 32 >= count
        at_ref[0:1, :] = jnp.where(first, pair * SLOTS + slot, -1)
        at_ref[1:2, :] = jnp.where(first, -1, of_row(begin[:, :1]) + index - 32)
        at_ref[2:3, :] = pair
        at_ref[3:4, :] = slot
        at_ref[4:5, :] = jnp.broadcast_to(jnp.sum(over[:, :1], axis=0, keepdims=True).astype(jnp.int32), (1, rows))
        sends = iota((pairs, rows), 0) == pair
        sends = jnp.concatenate(
            [jnp.where(sends & first, 1.0, 0.0), jnp.where(sends & last, 1.0, 0.0)], axis=0
        )
        high = ((rank >> 9) + 1).astype(jnp.float32)
        low = ((rank & 511) - 256).astype(jnp.float32)
        at_slot = ones_where((iota((LANES, rows), 0) & (SLOTS - 1)) == slot)
        meta_ref[0] = dot_nt((sends * high).astype(jnp.bfloat16), at_slot)
        meta_ref[1] = dot_nt((sends * low).astype(jnp.bfloat16), at_slot)
        spread = jnp.where(iota((CLUSTERS, LANES), 0) == iota((CLUSTERS, LANES), 1), counts, 0.0)
        meta_ref[2] = jnp.broadcast_to(jnp.sum(spread, axis=0, keepdims=True), (PEERS, LANES))
        place = iota((PEERS, CLUSTERS), 0) & (pairs - 1)
        theirs = ones_where((place >> 2) * 2 + (place & 1) == iota((PEERS, CLUSTERS), 1))
        meta_ref[3] = dot_nn(theirs, counts.astype(jnp.bfloat16))

    chunks = (jnp.max(at_ref[4:5, 0:LANES]) + LANES - 1) // LANES
    places = jnp.concatenate([at_ref[2:4, :], jnp.zeros((6, rows), jnp.int32)], axis=0)
    places = places.astype(jnp.float32) + jnp.where(iota((8, rows), 0) == 0, 1.0, 0.0)
    places = places.astype(jnp.bfloat16)

    @pl.when(step == 0)
    def _():
        def bring(chunk, _):
            start = pl.multiple_of(chunk * LANES, LANES)
            some_ref[pl.ds(start, LANES), :] = dot_nn(some_chosen(chunk), unit_ref[...]).astype(jnp.bfloat16)
            return 0

        lax.fori_loop(0, chunks, bring, 0)

    size = tile * SLOTS
    chosen = ones_where(iota((size, rows), 0) + step * size == at_ref[0:1, :])
    early = dot_nn(chosen, unit_ref[...])

    def spread_some(chunk, late):
        place = dot_nt(places, some_chosen(chunk))
        target = ((place[0:1, :] - 1.0) * SLOTS + place[1:2, :] + 0.5).astype(jnp.int32)
        target = jnp.where(place[0:1, :] > 0.5, target, -1)
        here = iota((size, LANES), 0) + step * size == target
        start = pl.multiple_of(chunk * LANES, LANES)
        some = dot_nn(ones_where(here), some_ref[pl.ds(start, LANES), :])
        taken = jnp.sum(jnp.where(here, 1.0, 0.0), axis=1, keepdims=True)
        return jnp.where(taken > 0.5, some, late)

    late = lax.fori_loop(0, chunks, spread_some, early)
    start = pl.multiple_of(step * tile, tile)
    at = iota((tile, 8, LANES), 1)
    for half, rows_at in ((0, early), (1, late)):
        packed = rows_at.astype(jnp.bfloat16)
        for block in range(BLOCKS):
            out_ref[:, half, block * SLOTS:(block + 1) * SLOTS, :] = packed[
                :, block * LANES:(block + 1) * LANES
            ].reshape(tile, SLOTS, LANES)
        parts = [meta_ref[i, pl.ds(start + half * pairs, tile), :][:, None, :] for i in range(4)]
        meta = jnp.zeros((tile, 8, LANES), jnp.float32)
        for i, part in enumerate(parts):
            meta = jnp.where(at == i, part, meta)
        out_ref[:, half, DATA:MSG, :] = meta.astype(jnp.bfloat16)


def pack(embeddings, cluster, order):
    rows = embeddings.shape[0]
    steps = 4
    message, index = pl.pallas_call(
        pack_kernel,
        grid=(steps,),
        in_specs=[
            pl.BlockSpec((rows, D), lambda i: (0, 0)),
            pl.BlockSpec((1, rows), lambda i: (0, 0)),
            pl.BlockSpec((1, rows), lambda i: (0, 0)),
        ],
        out_specs=[
            pl.BlockSpec((PEERS // 2 // steps, 2, MSG, LANES), lambda i: (i, 0, 0, 0)),
            pl.BlockSpec((2, rows), lambda i: (0, 0)),
        ],
        out_shape=[
            jax.ShapeDtypeStruct((PEERS // 2, 2, MSG, LANES), jnp.bfloat16),
            jax.ShapeDtypeStruct((2, rows), jnp.int32),
        ],
        scratch_shapes=[
            pltpu.VMEM((rows, D), jnp.bfloat16),
            pltpu.VMEM((8, rows), jnp.int32),
            pltpu.VMEM((rows, D), jnp.bfloat16),
            pltpu.VMEM((4, PEERS, LANES), jnp.float32),
        ],
        compiler_params=pltpu.CompilerParams(vmem_limit_bytes=VMEM),
        name="pack",
    )(embeddings, cluster.reshape(1, rows), order.reshape(1, rows))
    return message.reshape(PEERS, MSG, LANES), index


def units_of(ref, start, count):
    first, peers = start // SLOTS, count // SLOTS
    return jnp.concatenate(
        [
            ref[first:first + peers, b * SLOTS:(b + 1) * SLOTS, :].reshape(count, LANES)
            for b in range(BLOCKS)
        ],
        axis=1,
    )


def meta_of(ref):
    meta = ref[:, DATA:MSG, :].astype(jnp.float32).reshape(GROUPS, GROUP, 8, LANES)
    mine = iota((1, GROUP, 8, LANES), 3) >> 4 == iota((1, GROUP, 8, LANES), 1)
    return jnp.sum(jnp.where(mine, meta, 0.0), axis=1), meta


def rank_from(high, low):
    return jnp.where(high > 0.5, high * 512.0 + low, FAR)


def ranks_of(ref):
    held, _ = meta_of(ref)
    return rank_from(held[:, 0:1, :], held[:, 1:2, :])


def as_row(blocks):
    return jnp.concatenate([blocks[b] for b in range(GROUPS)], axis=1)


def as_columns(blocks, out_ref):
    for b in range(GROUPS):
        out_ref[b * LANES:(b + 1) * LANES, :] = jnp.broadcast_to(blocks[b], (LANES, LANES)).T


def row_of_best(ref):
    return jnp.concatenate(
        [
            jnp.max(ref[b * LANES:(b + 1) * LANES, :].T, axis=0, keepdims=True)
            for b in range(ref.shape[0] // LANES)
        ],
        axis=1,
    )


def lone_kernel(at_ref, msg_ref, out_ref, most_ref):
    core, first = at_ref[0], at_ref[1] * LONE
    held, meta = meta_of(msg_ref)
    high, low, count = (held[:, i:i + 1, :] for i in (0, 1, 3))
    half = jnp.floor((jnp.maximum(meta[:, :, 2, :] - 32.0, 0.0) + 1.0) * 0.5)
    most = jnp.sum(jnp.sum(half, axis=0), axis=0, keepdims=True)
    most_ref[...] = jnp.max(most, axis=1, keepdims=True).astype(jnp.int32)

    index = (2 * (iota((GROUPS, 1, LANES), 2) & 15) + core + 32).astype(jnp.float32)
    lone = jnp.where(index < count, 1.0, 0.0)
    lone = jnp.concatenate([lone[b] for b in range(GROUPS)], axis=0).astype(jnp.bfloat16)
    upper = ones_where(iota((LANES, LANES), 0) <= iota((LANES, LANES), 1))
    counted = dot_nn(lone, upper)
    whole = jnp.broadcast_to(counted[:, LANES - 1:LANES], (GROUPS, LANES)).astype(jnp.bfloat16)
    below = ones_where(iota((GROUPS, GROUPS), 1) < iota((GROUPS, GROUPS), 0))
    position = (counted + dot_nn(below, whole)).astype(jnp.int32) - 1 - first
    position = jnp.where(lone > 0.5, position, -1)
    position = jnp.concatenate([position[b:b + 1, :] for b in range(GROUPS)], axis=1)
    chosen = ones_where(iota((LONE, ROWS), 0) == position)
    out_ref[:LONE, :] = dot_nn(chosen, units_of(msg_ref, 0, ROWS)).astype(jnp.bfloat16)
    at = iota((FACTS, ROWS), 0)
    row = iota((FACTS, ROWS), 1)
    facts = jnp.where(at == 2, row >> 4, jnp.where(at == 3, row & 15, 0)).astype(jnp.float32)
    facts = jnp.where(at == 0, as_row(high), jnp.where(at == 1, as_row(low), facts))
    facts = dot_nt(facts.astype(jnp.bfloat16), chosen).astype(jnp.bfloat16)
    out_ref[LONE:, :LONE] = facts
    out_ref[LONE:, LONE:] = jnp.zeros((FACTS, D - LONE), jnp.bfloat16)


def gather_lone(core, round_at, msg):
    return pl.pallas_call(
        lone_kernel,
        in_specs=[
            pl.BlockSpec(memory_space=pltpu.SMEM),
            pl.BlockSpec(memory_space=pltpu.VMEM),
        ],
        out_specs=[pl.BlockSpec(memory_space=pltpu.VMEM)] * 2,
        out_shape=[
            jax.ShapeDtypeStruct((LONE + FACTS, D), jnp.bfloat16),
            jax.ShapeDtypeStruct((1, 1), jnp.int32),
        ],
        compiler_params=pltpu.CompilerParams(vmem_limit_bytes=VMEM),
        name="lone",
    )(jnp.stack([core, round_at]), msg)


def narrow_rows(x):
    best = x[:, :LANES]
    for b in range(1, x.shape[1] // LANES):
        best = jnp.maximum(best, x[:, b * LANES:(b + 1) * LANES])
    return best


def narrow_cols(x):
    return jnp.max(x.reshape(x.shape[0] // 8, 8, x.shape[1]), axis=0)


def wide(column, count):
    return jnp.concatenate([column] * (count // LANES), axis=1)


def span(i):
    return slice(i * BLOCK, (i + 1) * BLOCK)


def lone_facts(ref):
    facts = ref[LONE:, :LONE].astype(jnp.float32)
    peer = jnp.where(facts[0:1, :] > 0.5, facts[2:3, :].astype(jnp.int32), -1)
    return rank_from(facts[0:1, :], facts[1:2, :]), peer, facts[3:4, :].astype(jnp.int32)


def pairs_kernel(
    at_ref, own_ref, other_ref, lone_ref, beside_ref, out_ref, found_ref, rank_ref, rows_ref, cols_ref, some_ref
):
    core, late = at_ref[0], at_ref[1]
    own_ranks = ranks_of(own_ref)
    count = ROWS // BLOCK
    own_row = pl.ds(core, 1)
    other_row = pl.ds(1 - core, 1)

    def score(left, right, left_rank, right_rank, rows_at, cols_at, both):
        scores = dot_nt(left, right)
        earlier = right_rank < wide(left_rank, BLOCK)
        kept = narrow_rows(jnp.where(earlier, scores, -1.0))
        rows_ref[rows_at, :] = jnp.maximum(rows_ref[rows_at, :], kept)
        if both:
            kept = narrow_cols(jnp.where(earlier, -1.0, scores))
            cols_ref[:, cols_at] = jnp.maximum(cols_ref[:, cols_at], kept)

    rows_ref[...] = jnp.full((ROWS, LANES), -1.0, jnp.float32)
    cols_ref[...] = jnp.full((8, ROWS), -1.0, jnp.float32)

    @pl.when(late == 0)
    def _():
        as_columns(own_ranks, rank_ref)
        row = as_row(own_ranks)
        for i in range(count):
            left = units_of(own_ref, i * BLOCK, BLOCK)
            for j in range(i, count):
                right = units_of(own_ref, j * BLOCK, BLOCK)
                score(left, right, rank_ref[span(i), :], row[:, span(j)], span(i), span(j), i != j)
        some_ref[...] = beside_ref[...]
        best = jnp.maximum(row_of_best(rows_ref), jnp.max(cols_ref[...], axis=0, keepdims=True))
        out_ref[own_row, :] = best
        out_ref[other_row, :] = jnp.full((1, ROWS), -1.0, jnp.float32)

    def across(big_ref, small_ref, big_ranks, small_ranks, half):
        as_columns(big_ranks, rank_ref)
        row = as_row(small_ranks)
        for j in range(half * count // 2, (half + 1) * count // 2):
            right = units_of(small_ref, j * BLOCK, BLOCK)
            for i in range(count):
                left = units_of(big_ref, i * BLOCK, BLOCK)
                score(left, right, rank_ref[span(i), :], row[:, span(j)], span(i), span(j), True)
        out_ref[0:1, :] = row_of_best(rows_ref)
        out_ref[1:2, :] = jnp.max(cols_ref[...], axis=0, keepdims=True)
        some_ref[...] = lone_ref[...]

    @pl.when((late == 1) & (core == 0))
    def _():
        across(own_ref, other_ref, own_ranks, ranks_of(other_ref), 0)

    @pl.when((late == 1) & (core == 1))
    def _():
        across(other_ref, own_ref, ranks_of(other_ref), own_ranks, 1)
        as_columns(own_ranks, rank_ref)

    some = some_ref[:LONE, :]
    some_rank, _, _ = lone_facts(some_ref)
    found = jnp.full((8, LONE), -1.0, jnp.float32)
    for i in range(count):
        scores = dot_nt(units_of(own_ref, i * BLOCK, BLOCK), some)
        rank = wide(rank_ref[span(i), :], LONE)
        rows_ref[span(i), :] = narrow_rows(jnp.where(some_rank < rank, scores, -1.0))
        found = jnp.maximum(found, narrow_cols(jnp.where(rank < some_rank, scores, -1.0)))
    found_ref[...] = jnp.max(found, axis=0, keepdims=True)
    out_ref[own_row, :] = jnp.maximum(out_ref[own_row, :], row_of_best(rows_ref))


def score_pairs(core, late, own, other, lone, beside):
    return pl.pallas_call(
        pairs_kernel,
        in_specs=[pl.BlockSpec(memory_space=pltpu.SMEM)] + [pl.BlockSpec(memory_space=pltpu.VMEM)] * 4,
        out_specs=[pl.BlockSpec(memory_space=pltpu.VMEM)] * 2,
        out_shape=[
            jax.ShapeDtypeStruct((2, ROWS), jnp.float32),
            jax.ShapeDtypeStruct((1, LONE), jnp.float32),
        ],
        scratch_shapes=[
            pltpu.VMEM((ROWS, LANES), jnp.float32),
            pltpu.VMEM((ROWS, LANES), jnp.float32),
            pltpu.VMEM((8, ROWS), jnp.float32),
            pltpu.VMEM((LONE + FACTS, D), jnp.bfloat16),
        ],
        compiler_params=pltpu.CompilerParams(vmem_limit_bytes=VMEM),
        name="pairs",
    )(jnp.stack([core, late]), own, other, lone, beside)


def as_table(row):
    mine = iota((GROUP, LANES), 1) >> 4 == iota((GROUP, LANES), 0)
    parts = []
    for b in range(GROUPS):
        part = jnp.where(mine, row[:, b * LANES:(b + 1) * LANES], 0.0)
        for shift in (64, 32, 16):
            part = part + pltpu.roll(part, shift, 1)
        parts.append(part)
    return jnp.concatenate(parts, axis=0)


def finish_kernel(at_ref, lone_ref, beside_ref, late_ref, best_ref, found_ref, out_ref):
    core, late = at_ref[0], at_ref[1]
    late_rank, late_peer, late_slot = lone_facts(late_ref)
    late_column = jnp.broadcast_to(late_rank, (LANES, LONE))
    late_column = jnp.concatenate(
        [late_column[:, b * LANES:(b + 1) * LANES].T for b in range(LONE // LANES)], axis=0
    )
    late_column = wide(late_column, LONE)
    late_best = jnp.full((LONE, LANES), -1.0, jnp.float32)
    found = []
    for ref in (lone_ref, beside_ref):
        rank, peer, slot = lone_facts(ref)
        scores = dot_nt(late_ref[:LONE, :], ref[:LONE, :])
        late_best = jnp.maximum(late_best, narrow_rows(jnp.where(rank < late_column, scores, -1.0)))
        best = jnp.max(jnp.where(late_column < rank, scores, -1.0), axis=0, keepdims=True)
        found.append((best, peer, slot))
    late_best = jnp.concatenate(
        [
            jnp.max(late_best[b * LANES:(b + 1) * LANES, :].T, axis=0, keepdims=True)
            for b in range(LONE // LANES)
        ],
        axis=1,
    )
    earlier_found = found_ref[...]
    own = jnp.maximum(found[0][0], jnp.where(late == 1, earlier_found, -1.0))
    other = jnp.maximum(found[1][0], jnp.where(late == 0, earlier_found, -1.0))
    best = jnp.concatenate([own, other, late_best], axis=1)
    peer = jnp.concatenate([found[0][1], found[1][1], late_peer], axis=1)
    slot = jnp.concatenate(
        [found[0][2] + SLOTS * core, found[1][2] + SLOTS * (1 - core), late_slot + 2 * SLOTS], axis=1
    )
    at_peer = ones_where(iota((PEERS, 3 * LONE), 0) == peer)
    at_slot = iota((LANES, 3 * LONE), 0) == slot
    placed = dot_nt(at_peer, ones_where(at_slot))
    value = jnp.where(at_slot, best, 0.0)
    value = sum(dot_nt(at_peer, part) for part in thirds(value))
    table = jnp.where(placed > 0.5, value, -1.0)
    lane = iota((PEERS, LANES), 1)
    rest = jnp.where(
        lane < SLOTS,
        as_table(best_ref[0:1, :]),
        jnp.where(lane < 2 * SLOTS, as_table(best_ref[1:2, :]), -1.0),
    )
    out_ref[...] = jnp.maximum(table, rest)


def finish(core, late, lone, beside, late_rows, best, found):
    return pl.pallas_call(
        finish_kernel,
        in_specs=[pl.BlockSpec(memory_space=pltpu.SMEM)] + [pl.BlockSpec(memory_space=pltpu.VMEM)] * 5,
        out_specs=pl.BlockSpec(memory_space=pltpu.VMEM),
        out_shape=jax.ShapeDtypeStruct((PEERS, LANES), jnp.float32),
        compiler_params=pltpu.CompilerParams(vmem_limit_bytes=VMEM),
        name="finish",
    )(jnp.stack([core, late]), lone, beside, late_rows, best, found)


def reply_kernel(table_ref, cluster_ref, index_ref, out_ref):
    cluster = cluster_ref[...]
    index = index_ref[0:1, :]
    count = index_ref[1:2, :]
    rows = cluster.shape[1]
    table = table_ref[...]
    lane = iota((PEERS, LANES), 1)
    early = jnp.maximum(table, pltpu.roll(table, PEERS - 4, 0))
    beside = jnp.where(
        lane < SLOTS,
        pltpu.roll(table, LANES - 2 * SLOTS, 1),
        pltpu.roll(pltpu.roll(table, PEERS - 4, 0), LANES - SLOTS, 1),
    )
    late = jnp.maximum(pltpu.roll(early, PEERS - 1, 0), beside)
    both = jnp.concatenate([early.T[:2 * SLOTS, :], late.T[:2 * SLOTS, :]], axis=0)
    chosen = ones_where(iota((PEERS, rows), 0) == pair_of(cluster, jnp.zeros_like(index)) * 2)
    picked = sum(dot_nn(part, chosen) for part in thirds(both))
    at = (index & 1) * SLOTS + slot_of(index)
    here = iota((4 * SLOTS, rows), 0)
    here = ((here == at) & (index < 32)) | ((here == at + 2 * SLOTS) & (index + 32 >= count))
    out_ref[...] = jnp.max(jnp.where(here, picked, -1.0), axis=0, keepdims=True)


def read_reply(table, cluster, index):
    rows = cluster.shape[0]
    best = pl.pallas_call(
        reply_kernel,
        in_specs=[pl.BlockSpec(memory_space=pltpu.VMEM)] * 3,
        out_specs=pl.BlockSpec(memory_space=pltpu.VMEM),
        out_shape=jax.ShapeDtypeStruct((1, rows), jnp.float32),
        compiler_params=pltpu.CompilerParams(vmem_limit_bytes=VMEM),
        name="reply",
    )(table, cluster.reshape(1, rows), index)
    return best.reshape(rows)


def device(chip, core, column):
    return (chip * 2 + core) * 4 + column


SWAP = [
    (device(chip, core, column), device(chip, 1 - core, column))
    for chip in range(16)
    for core in range(2)
    for column in range(4)
]
LATE_SWAP = [(a, b) for a, b in SWAP if a % 2 == 1]
LATE_TO_EARLY = [
    (device(chip, core, 2 * pair + 1), device(chip, core, 2 * pair))
    for chip in range(16)
    for core in range(2)
    for pair in range(2)
]


def shards(embeddings, cluster, order):
    message, index = pack(embeddings, cluster, order)
    own = lax.all_to_all(message, AXES, split_axis=0, concat_axis=0, tiled=True)
    core = (lax.axis_index("owner") % 2).astype(jnp.int32)
    late = (lax.axis_index("split") % 2).astype(jnp.int32)
    other = lax.ppermute(own, AXES, LATE_SWAP)

    def score(lone, late_rows):
        beside = lax.ppermute(lone, AXES, SWAP)
        late_rows = lax.ppermute(late_rows, AXES, LATE_TO_EARLY)
        best, found = score_pairs(core, late, own, other, lone, beside)
        return finish(core, late, lone, beside, late_rows, best, found)

    lone, most = gather_lone(core, jnp.int32(0), own)
    table = score(lone, lone)
    rounds = (most[0, 0] + LONE - 1) // LONE

    def one_round(state):
        at, table = state
        lone, _ = gather_lone(core, at // rounds, own)
        late_rows, _ = gather_lone(core, at % rounds, own)
        return at + 1, jnp.maximum(table, score(lone, late_rows))

    table = lax.while_loop(lambda state: state[0] < rounds * rounds, one_round, (jnp.int32(1), table))[1]
    replies = lax.all_to_all(table, AXES, split_axis=0, concat_axis=0, tiled=True)
    return read_reply(replies, cluster, index)


def solution(mesh):
    placed = (P(AXES, None), P(AXES), P(AXES))
    return jax.shard_map(
        shards, mesh=mesh, in_specs=placed, out_specs=P(AXES), check_vma=False
    )
```

```python
import functools

import jax
import jax.numpy as jnp
from jax import lax
from jax.experimental import pallas as pl
from jax.experimental.pallas import tpu as pltpu
from jax.sharding import PartitionSpec as P

D = 768
LANES = 128
BLOCKS = D // LANES
SLOTS = 16
DATA = SLOTS * BLOCKS
MSG = DATA + 8
CLUSTERS = 32
PEERS = 128
ROWS = PEERS * SLOTS
GROUPS = ROWS // LANES
GROUP = LANES // SLOTS
LONE = 256
FACTS = 16
FAR = float(2**20)
BLOCK = 512
AXES = ("owner", "split")
VMEM = 56 * 2**20


def slot_of(index):
    return (index & 31) >> 1


def pair_of(cluster, index):
    return ((cluster >> 1) * 2 + (index & 1)) * 2 + (cluster & 1)


def my_core():
    return lax.axis_index("owner") % 2


def my_late():
    return lax.axis_index("split") % 2


def iota(shape, axis):
    return lax.broadcasted_iota(jnp.int32, shape, axis)


def ones_where(mask):
    return jnp.where(mask, 1.0, 0.0).astype(jnp.bfloat16)


def dot_nt(a, b):
    return lax.dot_general(a, b, (((1,), (1,)), ((), ())), preferred_element_type=jnp.float32)


def dot_nn(a, b):
    return lax.dot_general(a, b, (((1,), (0,)), ((), ())), preferred_element_type=jnp.float32)


def thirds(x):
    first = x.astype(jnp.bfloat16)
    left = x - first.astype(jnp.float32)
    second = left.astype(jnp.bfloat16)
    return first, second, (left - second.astype(jnp.float32)).astype(jnp.bfloat16)


def pack_kernel(emb_ref, cluster_ref, order_ref, out_ref, index_ref, unit_ref, at_ref, some_ref, some_at_ref, late_ref, meta_ref, past_ref):
    step = pl.program_id(0)
    rows = emb_ref.shape[0]
    pairs = PEERS // 2
    tile = pairs // pl.num_programs(0)

    @pl.when(step == 0)
    def _():
        values = emb_ref[...].astype(jnp.float32)
        total = jnp.sum(values * values, axis=1, keepdims=True)
        unit_ref[...] = (values * lax.rsqrt(total + 1e-06)).astype(jnp.bfloat16)
        cluster = cluster_ref[...]
        rank = order_ref[...]
        hit = iota((CLUSTERS, rows), 0) == cluster
        hits = ones_where(hit)
        upper = ones_where(iota((LANES, LANES), 0) <= iota((LANES, LANES), 1))
        blocks = rows // LANES
        ahead = dot_nn(hits, ones_where(iota((rows, LANES), 0) >> 7 < iota((rows, LANES), 1)))
        counted = jnp.concatenate(
            [
                dot_nn(hits[:, b * LANES:(b + 1) * LANES], upper) + ahead[:, b:b + 1]
                for b in range(blocks)
            ],
            axis=1,
        )
        counts = jnp.broadcast_to(ahead[:, blocks:blocks + 1], (CLUSTERS, LANES))
        below = ones_where(iota((CLUSTERS, CLUSTERS), 1) < iota((CLUSTERS, CLUSTERS), 0))
        over = jnp.maximum(counts - 32.0, 0.0)
        begin = dot_nn(below, over.astype(jnp.bfloat16))

        def of_row(x):
            return jnp.sum(jnp.where(hit, x, 0.0), axis=0, keepdims=True).astype(jnp.int32)

        index = of_row(counted) - 1
        count = of_row(counts[:, :1])
        index_ref[0:1, :] = index
        index_ref[1:2, :] = count
        slot = slot_of(index)
        pair = pair_of(cluster, index)
        first = index < 32
        last = index + 32 >= count
        at_ref[0:1, :] = jnp.where(first, pair * SLOTS + slot, -1)
        at_ref[1:2, :] = jnp.where(first, -1, of_row(begin[:, :1]) + index - 32)
        at_ref[2:3, :] = pair
        at_ref[3:4, :] = slot
        past_ref[0] = jnp.sum(over[:, :1]).astype(jnp.int32)
        sends = iota((pairs, rows), 0) == pair
        sends = jnp.concatenate(
            [jnp.where(sends & first, 1.0, 0.0), jnp.where(sends & last, 1.0, 0.0)], axis=0
        )
        high = ((rank >> 9) + 1).astype(jnp.float32)
        low = ((rank & 511) - 256).astype(jnp.float32)
        at_slot = ones_where((iota((LANES, rows), 0) & (SLOTS - 1)) == slot)
        meta_ref[0] = dot_nt((sends * high).astype(jnp.bfloat16), at_slot)
        meta_ref[1] = dot_nt((sends * low).astype(jnp.bfloat16), at_slot)
        spread = jnp.where(iota((CLUSTERS, LANES), 0) == iota((CLUSTERS, LANES), 1), counts, 0.0)
        meta_ref[2] = jnp.broadcast_to(jnp.sum(spread, axis=0, keepdims=True), (PEERS, LANES))
        place = iota((PEERS, CLUSTERS), 0) & (pairs - 1)
        theirs = ones_where((place >> 2) * 2 + (place & 1) == iota((PEERS, CLUSTERS), 1))
        meta_ref[3] = dot_nn(theirs, counts.astype(jnp.bfloat16))

    def bring(chunk):
        start = chunk * LANES
        chosen = ones_where(iota((LANES, rows), 0) + start == at_ref[1:2, :])
        some_ref[pl.ds(start, LANES), :] = dot_nn(chosen, unit_ref[...]).astype(jnp.bfloat16)
        places = jnp.where(iota((8, rows), 0) == 0, at_ref[2:3, :] + 1, at_ref[3:4, :])
        place = dot_nt(places.astype(jnp.float32).astype(jnp.bfloat16), chosen)
        target = ((place[0:1, :] - 1.0) * SLOTS + place[1:2, :]).astype(jnp.int32)
        some_at_ref[chunk] = jnp.broadcast_to(jnp.where(place[0:1, :] > 0.5, target, -1), (8, LANES))

    @pl.when(step == 0)
    def _():
        bring(0)

    size = tile * SLOTS
    chosen = ones_where(iota((size, rows), 0) + step * size == at_ref[0:1, :])
    early = dot_nn(chosen, unit_ref[...])

    def spread_some(chunk, late):
        here = iota((size, LANES), 0) + step * size == some_at_ref[chunk][0:1, :]
        some = dot_nn(ones_where(here), some_ref[chunk * LANES:(chunk + 1) * LANES, :])
        taken = jnp.sum(jnp.where(here, 1.0, 0.0), axis=1, keepdims=True)
        return jnp.where(taken > 0.5, some, late)

    late = spread_some(0, early)
    start = pl.multiple_of(step * tile, tile)

    def put(half, rows_at):
        packed = rows_at.astype(jnp.bfloat16)
        for block in range(BLOCKS):
            out_ref[:, half, block * SLOTS:(block + 1) * SLOTS, :] = packed[
                :, block * LANES:(block + 1) * LANES
            ].reshape(tile, SLOTS, LANES)

    put(0, early)
    put(1, late)
    late_ref[...] = late
    at = iota((tile, 8, LANES), 1)
    for half in range(2):
        meta = jnp.zeros((tile, 8, LANES), jnp.float32)
        for i in range(4):
            meta = jnp.where(at == i, meta_ref[i, pl.ds(start + half * pairs, tile), :][:, None, :], meta)
        out_ref[:, half, DATA:MSG, :] = meta.astype(jnp.bfloat16)

    @pl.when(past_ref[0] > LANES)
    def _():
        for chunk in range(1, rows // LANES // 2):
            bring(chunk)
            late_ref[...] = spread_some(chunk, late_ref[...])
        put(1, late_ref[...])


def pack(embeddings, cluster, order):
    rows = embeddings.shape[0]
    steps = 2
    message, index = pl.pallas_call(
        pack_kernel,
        grid=(steps,),
        in_specs=[
            pl.BlockSpec((rows, D), lambda i: (0, 0)),
            pl.BlockSpec((1, rows), lambda i: (0, 0)),
            pl.BlockSpec((1, rows), lambda i: (0, 0)),
        ],
        out_specs=[
            pl.BlockSpec((PEERS // 2 // steps, 2, MSG, LANES), lambda i: (i, 0, 0, 0)),
            pl.BlockSpec((2, rows), lambda i: (0, 0)),
        ],
        out_shape=[
            jax.ShapeDtypeStruct((PEERS // 2, 2, MSG, LANES), jnp.bfloat16),
            jax.ShapeDtypeStruct((2, rows), jnp.int32),
        ],
        scratch_shapes=[
            pltpu.VMEM((rows, D), jnp.bfloat16),
            pltpu.VMEM((8, rows), jnp.int32),
            pltpu.VMEM((rows // 2, D), jnp.bfloat16),
            pltpu.VMEM((rows // LANES // 2, 8, LANES), jnp.int32),
            pltpu.VMEM((rows // steps, D), jnp.float32),
            pltpu.VMEM((4, PEERS, LANES), jnp.float32),
            pltpu.SMEM((1,), jnp.int32),
        ],
        compiler_params=pltpu.CompilerParams(vmem_limit_bytes=VMEM),
        name="pack",
    )(embeddings, cluster.reshape(1, rows), order.reshape(1, rows))
    return message.reshape(PEERS, MSG, LANES), index


def units_of(ref, start, count):
    first, peers = start // SLOTS, count // SLOTS
    return jnp.concatenate(
        [
            ref[first:first + peers, b * SLOTS:(b + 1) * SLOTS, :].reshape(count, LANES)
            for b in range(BLOCKS)
        ],
        axis=1,
    )


def meta_of(ref):
    meta = ref[:, DATA:MSG, :].astype(jnp.float32).reshape(GROUPS, GROUP, 8, LANES)
    mine = iota((1, GROUP, 8, LANES), 3) >> 4 == iota((1, GROUP, 8, LANES), 1)
    return jnp.sum(jnp.where(mine, meta, 0.0), axis=1), meta


def rank_from(high, low):
    return jnp.where(high > 0.5, high * 512.0 + low, FAR)


def ranks_of(ref):
    held, _ = meta_of(ref)
    return rank_from(held[:, 0:1, :], held[:, 1:2, :])


def as_row(blocks):
    return jnp.concatenate([blocks[b] for b in range(GROUPS)], axis=1)


def as_columns(blocks, out_ref):
    for b in range(GROUPS):
        out_ref[b * LANES:(b + 1) * LANES, :] = jnp.broadcast_to(blocks[b], (LANES, LANES)).T


def row_of_best(ref):
    return jnp.concatenate(
        [
            jnp.max(ref[b * LANES:(b + 1) * LANES, :].T, axis=0, keepdims=True)
            for b in range(ref.shape[0] // LANES)
        ],
        axis=1,
    )


def lone_kernel(round_ref, msg_ref, out_ref, most_ref):
    core = my_core()
    first = 0 if round_ref is None else round_ref[0] * LONE
    held, meta = meta_of(msg_ref)
    high, low, count = (held[:, i:i + 1, :] for i in (0, 1, 3))
    half = jnp.floor((jnp.maximum(meta[:, :, 2, :] - 32.0, 0.0) + 1.0) * 0.5)
    most = jnp.sum(jnp.sum(half, axis=0), axis=0, keepdims=True)
    most_ref[...] = jnp.max(most, axis=1, keepdims=True).astype(jnp.int32)

    index = (2 * (iota((GROUPS, 1, LANES), 2) & 15) + core + 32).astype(jnp.float32)
    lone = jnp.where(index < count, 1.0, 0.0)
    lone = jnp.concatenate([lone[b] for b in range(GROUPS)], axis=0).astype(jnp.bfloat16)
    upper = ones_where(iota((LANES, LANES), 0) <= iota((LANES, LANES), 1))
    counted = dot_nn(lone, upper)
    whole = jnp.broadcast_to(counted[:, LANES - 1:LANES], (GROUPS, LANES)).astype(jnp.bfloat16)
    below = ones_where(iota((GROUPS, GROUPS), 1) < iota((GROUPS, GROUPS), 0))
    position = (counted + dot_nn(below, whole)).astype(jnp.int32) - 1 - first
    position = jnp.where(lone > 0.5, position, -1)
    position = jnp.concatenate([position[b:b + 1, :] for b in range(GROUPS)], axis=1)
    chosen = ones_where(iota((LONE, ROWS), 0) == position)
    out_ref[:LONE, :] = dot_nn(chosen, units_of(msg_ref, 0, ROWS)).astype(jnp.bfloat16)
    at = iota((FACTS, ROWS), 0)
    row = iota((FACTS, ROWS), 1)
    facts = jnp.where(at == 2, row >> 4, jnp.where(at == 3, row & 15, 0)).astype(jnp.float32)
    facts = jnp.where(at == 0, as_row(high), jnp.where(at == 1, as_row(low), facts))
    facts = dot_nt(facts.astype(jnp.bfloat16), chosen).astype(jnp.bfloat16)
    out_ref[LONE:, :LONE] = facts
    out_ref[LONE:, LONE:] = jnp.zeros((FACTS, D - LONE), jnp.bfloat16)


def gather_lone(msg, round_at=None):
    some = [] if round_at is None else [round_at.reshape(1)]
    return pl.pallas_call(
        lone_kernel if some else functools.partial(lone_kernel, None),
        in_specs=[pl.BlockSpec(memory_space=pltpu.SMEM)] * len(some)
        + [pl.BlockSpec(memory_space=pltpu.VMEM)],
        out_specs=[pl.BlockSpec(memory_space=pltpu.VMEM)] * 2,
        out_shape=[
            jax.ShapeDtypeStruct((LONE + FACTS, D), jnp.bfloat16),
            jax.ShapeDtypeStruct((1, 1), jnp.int32),
        ],
        compiler_params=pltpu.CompilerParams(vmem_limit_bytes=VMEM),
        name="lone",
    )(*some, msg)


def narrow_rows(x):
    best = x[:, :LANES]
    for b in range(1, x.shape[1] // LANES):
        best = jnp.maximum(best, x[:, b * LANES:(b + 1) * LANES])
    return best


def narrow_cols(x):
    return jnp.max(x.reshape(x.shape[0] // 8, 8, x.shape[1]), axis=0)


def wide(column, count):
    return jnp.concatenate([column] * (count // LANES), axis=1)


def span(i):
    return slice(i * BLOCK, (i + 1) * BLOCK)


def lone_facts(ref):
    facts = ref[LONE:, :LONE].astype(jnp.float32)
    peer = jnp.where(facts[0:1, :] > 0.5, facts[2:3, :].astype(jnp.int32), -1)
    return rank_from(facts[0:1, :], facts[1:2, :]), peer, facts[3:4, :].astype(jnp.int32)


def pairs_kernel(own_ref, other_ref, lone_ref, beside_ref, out_ref, found_ref, rank_ref, rows_ref, cols_ref, some_ref):
    core, late = my_core(), my_late()
    own_ranks = ranks_of(own_ref)
    as_columns(own_ranks, rank_ref)
    count = ROWS // BLOCK
    rows_ref[...] = jnp.full((ROWS, LANES), -1.0, jnp.float32)
    cols_ref[...] = jnp.full((8, ROWS), -1.0, jnp.float32)

    def score(right_ref, row, i, j, both):
        scores = dot_nt(units_of(own_ref, i * BLOCK, BLOCK), units_of(right_ref, j * BLOCK, BLOCK))
        earlier = row[:, span(j)] < wide(rank_ref[span(i), :], BLOCK)
        kept = narrow_rows(jnp.where(earlier, scores, -1.0))
        rows_ref[span(i), :] = jnp.maximum(rows_ref[span(i), :], kept)
        if both:
            kept = narrow_cols(jnp.where(earlier, -1.0, scores))
            cols_ref[:, span(j)] = jnp.maximum(cols_ref[:, span(j)], kept)

    @pl.when(late == 0)
    def _():
        row = as_row(own_ranks)
        for i in range(count):
            for j in range(i, count):
                score(own_ref, row, i, j, i != j)
        some_ref[...] = beside_ref[...]

    def across(firsts, seconds):
        row = as_row(ranks_of(other_ref))
        for i in firsts:
            for j in seconds:
                score(other_ref, row, i, j, True)
        some_ref[...] = lone_ref[...]

    @pl.when((late == 1) & (core == 0))
    def _():
        across(range(count), range(count // 2))

    @pl.when((late == 1) & (core == 1))
    def _():
        across(range(count // 2, count), range(count))

    some = some_ref[:LONE, :]
    some_rank, _, _ = lone_facts(some_ref)
    found = jnp.full((8, LONE), -1.0, jnp.float32)
    for i in range(count):
        scores = dot_nt(units_of(own_ref, i * BLOCK, BLOCK), some)
        rank = wide(rank_ref[span(i), :], LONE)
        kept = narrow_rows(jnp.where(some_rank < rank, scores, -1.0))
        rows_ref[span(i), :] = jnp.maximum(rows_ref[span(i), :], kept)
        found = jnp.maximum(found, narrow_cols(jnp.where(rank < some_rank, scores, -1.0)))
    found_ref[...] = jnp.max(found, axis=0, keepdims=True)
    own_best = row_of_best(rows_ref)
    cols_best = jnp.max(cols_ref[...], axis=0, keepdims=True)
    out_ref[0:1, :] = jnp.where(late == 0, jnp.maximum(own_best, cols_best), own_best)
    out_ref[1:2, :] = jnp.where(late == 0, -1.0, cols_best)


def score_pairs(own, other, lone, beside):
    return pl.pallas_call(
        pairs_kernel,
        in_specs=[pl.BlockSpec(memory_space=pltpu.VMEM)] * 4,
        out_specs=[pl.BlockSpec(memory_space=pltpu.VMEM)] * 2,
        out_shape=[
            jax.ShapeDtypeStruct((2, ROWS), jnp.float32),
            jax.ShapeDtypeStruct((1, LONE), jnp.float32),
        ],
        scratch_shapes=[
            pltpu.VMEM((ROWS, LANES), jnp.float32),
            pltpu.VMEM((ROWS, LANES), jnp.float32),
            pltpu.VMEM((8, ROWS), jnp.float32),
            pltpu.VMEM((LONE + FACTS, D), jnp.bfloat16),
        ],
        compiler_params=pltpu.CompilerParams(vmem_limit_bytes=VMEM),
        name="pairs",
    )(own, other, lone, beside)


def as_table(row):
    mine = iota((GROUP, LANES), 1) >> 4 == iota((GROUP, LANES), 0)
    parts = []
    for b in range(GROUPS):
        part = jnp.where(mine, row[:, b * LANES:(b + 1) * LANES], 0.0)
        for shift in (64, 32, 16):
            part = part + pltpu.roll(part, shift, 1)
        parts.append(part)
    return jnp.concatenate(parts, axis=0)


def finish_kernel(lone_ref, beside_ref, late_ref, best_ref, found_ref, out_ref):
    core, late = my_core(), my_late()
    late_rank, late_peer, late_slot = lone_facts(late_ref)
    late_column = jnp.broadcast_to(late_rank, (LANES, LONE))
    late_column = jnp.concatenate(
        [late_column[:, b * LANES:(b + 1) * LANES].T for b in range(LONE // LANES)], axis=0
    )
    late_column = wide(late_column, LONE)
    late_best = jnp.full((LONE, LANES), -1.0, jnp.float32)
    found = []
    for ref in (lone_ref, beside_ref):
        rank, peer, slot = lone_facts(ref)
        scores = dot_nt(late_ref[:LONE, :], ref[:LONE, :])
        late_best = jnp.maximum(late_best, narrow_rows(jnp.where(rank < late_column, scores, -1.0)))
        best = jnp.max(jnp.where(late_column < rank, scores, -1.0), axis=0, keepdims=True)
        found.append((best, peer, slot))
    late_best = jnp.concatenate(
        [
            jnp.max(late_best[b * LANES:(b + 1) * LANES, :].T, axis=0, keepdims=True)
            for b in range(LONE // LANES)
        ],
        axis=1,
    )
    earlier_found = found_ref[...]
    own = jnp.maximum(found[0][0], jnp.where(late == 1, earlier_found, -1.0))
    other = jnp.maximum(found[1][0], jnp.where(late == 0, earlier_found, -1.0))
    best = jnp.concatenate([own, other, late_best], axis=1)
    peer = jnp.concatenate([found[0][1], found[1][1], late_peer], axis=1)
    slot = jnp.concatenate(
        [found[0][2] + SLOTS * core, found[1][2] + SLOTS * (1 - core), late_slot + 2 * SLOTS], axis=1
    )
    at_peer = ones_where(iota((PEERS, 3 * LONE), 0) == peer)
    at_slot = iota((LANES, 3 * LONE), 0) == slot
    placed = dot_nt(at_peer, ones_where(at_slot))
    value = jnp.where(at_slot, best, 0.0)
    value = sum(dot_nt(at_peer, part) for part in thirds(value))
    table = jnp.where(placed > 0.5, value, -1.0)
    lane = iota((PEERS, LANES), 1)
    rest = jnp.where(
        lane >> 4 == core,
        as_table(best_ref[0:1, :]),
        jnp.where(lane < 2 * SLOTS, as_table(best_ref[1:2, :]), -1.0),
    )
    out_ref[...] = jnp.maximum(table, rest)


def finish(lone, beside, late_rows, best, found):
    return pl.pallas_call(
        finish_kernel,
        in_specs=[pl.BlockSpec(memory_space=pltpu.VMEM)] * 5,
        out_specs=pl.BlockSpec(memory_space=pltpu.VMEM),
        out_shape=jax.ShapeDtypeStruct((PEERS, LANES), jnp.float32),
        compiler_params=pltpu.CompilerParams(vmem_limit_bytes=VMEM),
        name="finish",
    )(lone, beside, late_rows, best, found)


def reply_kernel(table_ref, cluster_ref, index_ref, out_ref):
    cluster = cluster_ref[...]
    index = index_ref[0:1, :]
    count = index_ref[1:2, :]
    rows = cluster.shape[1]
    table = table_ref[...]
    lane = iota((PEERS, LANES), 1)
    early = jnp.maximum(table, pltpu.roll(table, PEERS - 4, 0))
    beside = jnp.where(
        lane < SLOTS,
        pltpu.roll(table, LANES - 2 * SLOTS, 1),
        pltpu.roll(pltpu.roll(table, PEERS - 4, 0), LANES - SLOTS, 1),
    )
    late = jnp.maximum(pltpu.roll(early, PEERS - 1, 0), beside)
    both = jnp.concatenate([early.T[:2 * SLOTS, :], late.T[:2 * SLOTS, :]], axis=0)
    chosen = ones_where(iota((PEERS, rows), 0) == pair_of(cluster, jnp.zeros_like(index)) * 2)
    picked = sum(dot_nn(part, chosen) for part in thirds(both))
    at = (index & 1) * SLOTS + slot_of(index)
    here = iota((4 * SLOTS, rows), 0)
    here = ((here == at) & (index < 32)) | ((here == at + 2 * SLOTS) & (index + 32 >= count))
    out_ref[...] = jnp.max(jnp.where(here, picked, -1.0), axis=0, keepdims=True)


def read_reply(table, cluster, index):
    rows = cluster.shape[0]
    best = pl.pallas_call(
        reply_kernel,
        in_specs=[pl.BlockSpec(memory_space=pltpu.VMEM)] * 3,
        out_specs=pl.BlockSpec(memory_space=pltpu.VMEM),
        out_shape=jax.ShapeDtypeStruct((1, rows), jnp.float32),
        compiler_params=pltpu.CompilerParams(vmem_limit_bytes=VMEM),
        name="reply",
    )(table, cluster.reshape(1, rows), index)
    return best.reshape(rows)


def device(chip, core, column):
    return (chip * 2 + core) * 4 + column


SWAP = [
    (device(chip, core, column), device(chip, 1 - core, column))
    for chip in range(16)
    for core in range(2)
    for column in range(4)
]
OTHER_CHIP = [
    (device(chip, core, column), device(chip, core, column ^ 1))
    for chip in range(16)
    for core in range(2)
    for column in range(4)
]


def shards(embeddings, cluster, order):
    message, index = pack(embeddings, cluster, order)
    own = lax.all_to_all(message, AXES, split_axis=0, concat_axis=0, tiled=True)
    other = lax.ppermute(own, AXES, SWAP)

    def score(lone, far):
        beside = lax.ppermute(lone, AXES, SWAP)
        far = lax.ppermute(far, AXES, OTHER_CHIP)
        best, found = score_pairs(own, other, lone, beside)
        return finish(lone, beside, far, best, found)

    lone, most = gather_lone(own)
    table = score(lone, lone)
    rounds = (most[0, 0] + LONE - 1) // LONE

    def one_round(state):
        at, table = state
        lone, _ = gather_lone(own, at // rounds)
        far, _ = gather_lone(own, at % rounds)
        return at + 1, jnp.maximum(table, score(lone, far))

    table = lax.while_loop(lambda state: state[0] < rounds * rounds, one_round, (jnp.int32(1), table))[1]
    replies = lax.all_to_all(table, AXES, split_axis=0, concat_axis=0, tiled=True)
    return read_reply(replies, cluster, index)


def solution(mesh):
    placed = (P(AXES, None), P(AXES), P(AXES))
    return jax.shard_map(
        shards, mesh=mesh, in_specs=placed, out_specs=P(AXES), check_vma=False
    )
```

```python
import functools

import jax
import jax.numpy as jnp
from jax import lax
from jax.experimental import pallas as pl
from jax.experimental.pallas import tpu as pltpu
from jax.sharding import PartitionSpec as P

D = 768
LANES = 128
HALF = LANES // 2
BLOCKS = D // LANES
SLOTS = 16
DATA = SLOTS * BLOCKS
MSG = DATA + 8
CLUSTERS = 32
PEERS = 128
ROWS = PEERS * SLOTS
GROUPS = ROWS // LANES
GROUP = LANES // SLOTS
LONE = 256
FACTS = 16
FAR = float(2**20)
BLOCK = 512
AXES = ("owner", "split")
MIB = 2**20


def slot_of(index):
    return (index & 31) >> 1


def pair_of(cluster, index):
    return ((cluster >> 1) * 2 + (index & 1)) * 2 + (cluster & 1)


def my_core():
    return lax.axis_index("owner") % 2


def my_late():
    return lax.axis_index("split") % 2


def iota(shape, axis):
    return lax.broadcasted_iota(jnp.int32, shape, axis)


def ones_where(mask):
    return jnp.where(mask, 1.0, 0.0).astype(jnp.bfloat16)


def dot_nt(a, b):
    return lax.dot_general(a, b, (((1,), (1,)), ((), ())), preferred_element_type=jnp.float32)


def dot_nn(a, b):
    return lax.dot_general(a, b, (((1,), (0,)), ((), ())), preferred_element_type=jnp.float32)


def thirds(x):
    first = x.astype(jnp.bfloat16)
    left = x - first.astype(jnp.float32)
    second = left.astype(jnp.bfloat16)
    return first, second, (left - second.astype(jnp.float32)).astype(jnp.bfloat16)


def pack_kernel(emb_ref, cluster_ref, order_ref, out_ref, index_ref, unit_ref, at_ref, some_ref, some_at_ref, late_ref, meta_ref, past_ref):
    step = pl.program_id(0)
    rows = emb_ref.shape[0]
    pairs = PEERS // 2
    tile = pairs // pl.num_programs(0)

    @pl.when(step == 0)
    def _():
        values = emb_ref[...].astype(jnp.float32)
        total = jnp.sum(values * values, axis=1, keepdims=True)
        unit_ref[...] = (values * lax.rsqrt(total + 1e-06)).astype(jnp.bfloat16)
        cluster = cluster_ref[...]
        rank = order_ref[...]
        hit = iota((CLUSTERS, rows), 0) == cluster
        hits = ones_where(hit)
        upper = ones_where(iota((LANES, LANES), 0) <= iota((LANES, LANES), 1))
        blocks = rows // LANES
        ahead = dot_nn(hits, ones_where(iota((rows, LANES), 0) >> 7 < iota((rows, LANES), 1)))
        counted = jnp.concatenate(
            [
                dot_nn(hits[:, b * LANES:(b + 1) * LANES], upper) + ahead[:, b:b + 1]
                for b in range(blocks)
            ],
            axis=1,
        )
        counts = jnp.broadcast_to(ahead[:, blocks:blocks + 1], (CLUSTERS, LANES))
        below = ones_where(iota((CLUSTERS, CLUSTERS), 1) < iota((CLUSTERS, CLUSTERS), 0))
        over = jnp.maximum(counts - 32.0, 0.0)
        begin = dot_nn(below, over.astype(jnp.bfloat16))

        def of_row(x):
            return jnp.sum(jnp.where(hit, x, 0.0), axis=0, keepdims=True).astype(jnp.int32)

        index = of_row(counted) - 1
        count = of_row(counts[:, :1])
        index_ref[0:1, :] = index
        index_ref[1:2, :] = count
        slot = slot_of(index)
        pair = pair_of(cluster, index)
        first = index < 32
        last = index + 32 >= count
        at_ref[0:1, :] = jnp.where(first, pair * SLOTS + slot, -1)
        at_ref[1:2, :] = jnp.where(first, -1, of_row(begin[:, :1]) + index - 32)
        at_ref[2:3, :] = pair
        at_ref[3:4, :] = slot
        past_ref[0] = jnp.sum(over[:, :1]).astype(jnp.int32)
        sends = iota((pairs, rows), 0) == pair
        sends = jnp.concatenate(
            [jnp.where(sends & first, 1.0, 0.0), jnp.where(sends & last, 1.0, 0.0)], axis=0
        )
        high = ((rank >> 9) + 1).astype(jnp.float32)
        low = ((rank & 511) - 256).astype(jnp.float32)
        at_slot = ones_where((iota((LANES, rows), 0) & (SLOTS - 1)) == slot)
        meta_ref[0] = dot_nt((sends * high).astype(jnp.bfloat16), at_slot)
        meta_ref[1] = dot_nt((sends * low).astype(jnp.bfloat16), at_slot)
        spread = jnp.where(iota((CLUSTERS, LANES), 0) == iota((CLUSTERS, LANES), 1), counts, 0.0)
        meta_ref[2] = jnp.broadcast_to(jnp.sum(spread, axis=0, keepdims=True), (PEERS, LANES))
        place = iota((PEERS, CLUSTERS), 0) & (pairs - 1)
        theirs = ones_where((place >> 2) * 2 + (place & 1) == iota((PEERS, CLUSTERS), 1))
        meta_ref[3] = dot_nn(theirs, counts.astype(jnp.bfloat16))

    def bring(chunk):
        start = chunk * LANES
        chosen = ones_where(iota((LANES, rows), 0) + start == at_ref[1:2, :])
        some_ref[pl.ds(start, LANES), :] = dot_nn(chosen, unit_ref[...]).astype(jnp.bfloat16)
        places = jnp.where(iota((8, rows), 0) == 0, at_ref[2:3, :] + 1, at_ref[3:4, :])
        place = dot_nt(places.astype(jnp.float32).astype(jnp.bfloat16), chosen)
        target = ((place[0:1, :] - 1.0) * SLOTS + place[1:2, :]).astype(jnp.int32)
        some_at_ref[chunk] = jnp.broadcast_to(jnp.where(place[0:1, :] > 0.5, target, -1), (8, LANES))

    @pl.when(step == 0)
    def _():
        bring(0)

    size = tile * SLOTS
    chosen = ones_where(iota((size, rows), 0) + step * size == at_ref[0:1, :])
    early = dot_nn(chosen, unit_ref[...])

    def spread_some(chunk, late):
        here = iota((size, LANES), 0) + step * size == some_at_ref[chunk][0:1, :]
        some = dot_nn(ones_where(here), some_ref[chunk * LANES:(chunk + 1) * LANES, :])
        taken = jnp.sum(jnp.where(here, 1.0, 0.0), axis=1, keepdims=True)
        return jnp.where(taken > 0.5, some, late)

    late = spread_some(0, early)
    start = pl.multiple_of(step * tile, tile)

    def put(half, rows_at):
        packed = rows_at.astype(jnp.bfloat16)
        for block in range(BLOCKS):
            out_ref[:, half, block * SLOTS:(block + 1) * SLOTS, :] = packed[
                :, block * LANES:(block + 1) * LANES
            ].reshape(tile, SLOTS, LANES)

    put(0, early)
    put(1, late)
    late_ref[...] = late
    at = iota((tile, 8, LANES), 1)
    for half in range(2):
        meta = jnp.zeros((tile, 8, LANES), jnp.float32)
        for i in range(4):
            meta = jnp.where(at == i, meta_ref[i, pl.ds(start + half * pairs, tile), :][:, None, :], meta)
        out_ref[:, half, DATA:MSG, :] = meta.astype(jnp.bfloat16)

    @pl.when(past_ref[0] > LANES)
    def _():
        for chunk in range(1, rows // LANES // 2):
            bring(chunk)
            late_ref[...] = spread_some(chunk, late_ref[...])
        put(1, late_ref[...])


def pack(embeddings, cluster, order):
    rows = embeddings.shape[0]
    steps = 2
    message, index = pl.pallas_call(
        pack_kernel,
        grid=(steps,),
        in_specs=[
            pl.BlockSpec((rows, D), lambda i: (0, 0)),
            pl.BlockSpec((1, rows), lambda i: (0, 0)),
            pl.BlockSpec((1, rows), lambda i: (0, 0)),
        ],
        out_specs=[
            pl.BlockSpec((PEERS // 2 // steps, 2, MSG, LANES), lambda i: (i, 0, 0, 0)),
            pl.BlockSpec((2, rows), lambda i: (0, 0)),
        ],
        out_shape=[
            jax.ShapeDtypeStruct((PEERS // 2, 2, MSG, LANES), jnp.bfloat16),
            jax.ShapeDtypeStruct((2, rows), jnp.int32),
        ],
        scratch_shapes=[
            pltpu.VMEM((rows, D), jnp.bfloat16),
            pltpu.VMEM((8, rows), jnp.int32),
            pltpu.VMEM((rows // 2, D), jnp.bfloat16),
            pltpu.VMEM((rows // LANES // 2, 8, LANES), jnp.int32),
            pltpu.VMEM((rows // steps, D), jnp.float32),
            pltpu.VMEM((4, PEERS, LANES), jnp.float32),
            pltpu.SMEM((1,), jnp.int32),
        ],
        compiler_params=pltpu.CompilerParams(vmem_limit_bytes=24 * MIB),
        name="pack",
    )(embeddings, cluster.reshape(1, rows), order.reshape(1, rows))
    return message.reshape(PEERS, MSG, LANES), index


def units_of(ref, start, count):
    first, peers = start // SLOTS, count // SLOTS
    return jnp.concatenate(
        [
            ref[first:first + peers, b * SLOTS:(b + 1) * SLOTS, :].reshape(count, LANES)
            for b in range(BLOCKS)
        ],
        axis=1,
    )


def meta_of(ref):
    meta = ref[:, DATA:MSG, :].astype(jnp.float32).reshape(GROUPS, GROUP, 8, LANES)
    mine = iota((1, GROUP, 8, LANES), 3) >> 4 == iota((1, GROUP, 8, LANES), 1)
    return jnp.sum(jnp.where(mine, meta, 0.0), axis=1), meta


def rank_from(high, low):
    return jnp.where(high > 0.5, high * 512.0 + low, FAR)


def ranks_of(ref):
    held, _ = meta_of(ref)
    return rank_from(held[:, 0:1, :], held[:, 1:2, :])


def as_row(blocks):
    return jnp.concatenate([blocks[b] for b in range(GROUPS)], axis=1)


def as_columns(blocks, out_ref):
    for b in range(GROUPS):
        out_ref[b * LANES:(b + 1) * LANES, :] = jnp.broadcast_to(blocks[b], (LANES, LANES)).T


def row_of_best(ref):
    return jnp.concatenate(
        [
            jnp.max(ref[b * LANES:(b + 1) * LANES, :].T, axis=0, keepdims=True)
            for b in range(ref.shape[0] // LANES)
        ],
        axis=1,
    )


def lone_kernel(round_ref, msg_ref, out_ref, most_ref):
    core = my_core()
    first = 0 if round_ref is None else round_ref[0] * LONE
    held, meta = meta_of(msg_ref)
    high, low, count = (held[:, i:i + 1, :] for i in (0, 1, 3))
    half = jnp.floor((jnp.maximum(meta[:, :, 2, :] - 32.0, 0.0) + 1.0) * 0.5)
    most = jnp.sum(jnp.sum(half, axis=0), axis=0, keepdims=True)
    most_ref[...] = jnp.max(most, axis=1, keepdims=True).astype(jnp.int32)

    index = (2 * (iota((GROUPS, 1, LANES), 2) & 15) + core + 32).astype(jnp.float32)
    lone = jnp.where(index < count, 1.0, 0.0)
    lone = jnp.concatenate([lone[b] for b in range(GROUPS)], axis=0).astype(jnp.bfloat16)
    upper = ones_where(iota((LANES, LANES), 0) <= iota((LANES, LANES), 1))
    counted = dot_nn(lone, upper)
    whole = jnp.broadcast_to(counted[:, LANES - 1:LANES], (GROUPS, LANES)).astype(jnp.bfloat16)
    below = ones_where(iota((GROUPS, GROUPS), 1) < iota((GROUPS, GROUPS), 0))
    position = (counted + dot_nn(below, whole)).astype(jnp.int32) - 1 - first
    position = jnp.where(lone > 0.5, position, -1)
    position = jnp.concatenate([position[b:b + 1, :] for b in range(GROUPS)], axis=1)
    chosen = ones_where(iota((LONE, ROWS), 0) == position)
    out_ref[:LONE, :] = dot_nn(chosen, units_of(msg_ref, 0, ROWS)).astype(jnp.bfloat16)
    at = iota((FACTS, ROWS), 0)
    row = iota((FACTS, ROWS), 1)
    facts = jnp.where(at == 2, row >> 4, jnp.where(at == 3, row & 15, 0)).astype(jnp.float32)
    facts = jnp.where(at == 0, as_row(high), jnp.where(at == 1, as_row(low), facts))
    facts = dot_nt(facts.astype(jnp.bfloat16), chosen).astype(jnp.bfloat16)
    out_ref[LONE:, :LONE] = facts
    out_ref[LONE:, LONE:] = jnp.zeros((FACTS, D - LONE), jnp.bfloat16)


def gather_lone(msg, round_at=None):
    some = [] if round_at is None else [round_at.reshape(1)]
    return pl.pallas_call(
        lone_kernel if some else functools.partial(lone_kernel, None),
        in_specs=[pl.BlockSpec(memory_space=pltpu.SMEM)] * len(some)
        + [pl.BlockSpec(memory_space=pltpu.VMEM)],
        out_specs=[pl.BlockSpec(memory_space=pltpu.VMEM)] * 2,
        out_shape=[
            jax.ShapeDtypeStruct((LONE + FACTS, D), jnp.bfloat16),
            jax.ShapeDtypeStruct((1, 1), jnp.int32),
        ],
        compiler_params=pltpu.CompilerParams(vmem_limit_bytes=16 * MIB),
        name="lone",
    )(*some, msg)


def narrow_rows(x):
    best = x[:, :LANES]
    for b in range(1, x.shape[1] // LANES):
        best = jnp.maximum(best, x[:, b * LANES:(b + 1) * LANES])
    return best


def narrow_cols(x):
    return jnp.max(x.reshape(x.shape[0] // 8, 8, x.shape[1]), axis=0)


def wide(column, count):
    return jnp.concatenate([column] * (count // LANES), axis=1)


def span(i):
    return slice(i * BLOCK, (i + 1) * BLOCK)


def lone_facts(ref):
    facts = ref[LONE:, :LONE].astype(jnp.float32)
    peer = jnp.where(facts[0:1, :] > 0.5, facts[2:3, :].astype(jnp.int32), -1)
    return rank_from(facts[0:1, :], facts[1:2, :]), peer, facts[3:4, :].astype(jnp.int32)


def pairs_kernel(
    own_ref, other_ref, lone_ref, beside_ref, out_ref, found_ref, rank_ref, rows_ref, cols_ref, some_ref
):
    core, late = my_core(), my_late()

    @pl.when(late == 1)
    def _():
        some_ref[...] = lone_ref[...]

    @pl.when(late == 0)
    def _():
        some_ref[...] = beside_ref[...]

    own_ranks = ranks_of(own_ref)
    as_columns(own_ranks, rank_ref)
    count = ROWS // BLOCK
    cols_ref[...] = jnp.full((8, ROWS), -1.0, jnp.float32)
    some = some_ref[:LONE, :]
    some_rank, _, _ = lone_facts(some_ref)
    found = jnp.full((8, LONE), -1.0, jnp.float32)
    for i in range(count):
        scores = dot_nt(units_of(own_ref, i * BLOCK, BLOCK), some)
        rank = wide(rank_ref[span(i), :], LONE)
        rows_ref[span(i), :] = narrow_rows(jnp.where(some_rank < rank, scores, -1.0))
        found = jnp.maximum(found, narrow_cols(jnp.where(rank < some_rank, scores, -1.0)))
    found_ref[...] = jnp.max(found, axis=0, keepdims=True)

    def score(right_ref, row, i, j, size, both):
        left_at, right_at = slice(i * size, (i + 1) * size), slice(j * size, (j + 1) * size)
        scores = dot_nt(units_of(own_ref, i * size, size), units_of(right_ref, j * size, size))
        earlier = row[:, right_at] < wide(rank_ref[left_at, :], size)
        kept = narrow_rows(jnp.where(earlier, scores, -1.0))
        rows_ref[left_at, :] = jnp.maximum(rows_ref[left_at, :], kept)
        if both:
            kept = narrow_cols(jnp.where(earlier, -1.0, scores))
            cols_ref[:, right_at] = jnp.maximum(cols_ref[:, right_at], kept)

    @pl.when(late == 0)
    def _():
        row = as_row(own_ranks)
        size = BLOCK // 2
        for i in range(2 * count):
            for j in range(i, 2 * count):
                score(own_ref, row, i, j, size, i != j)

    def across(firsts, seconds):
        row = as_row(ranks_of(other_ref))
        for i in firsts:
            for j in seconds:
                score(other_ref, row, i, j, BLOCK, True)

    @pl.when((late == 1) & (core == 0))
    def _():
        across(range(count), range(count // 2))

    @pl.when((late == 1) & (core == 1))
    def _():
        across(range(count // 2, count), range(count))

    own_best = row_of_best(rows_ref)
    cols_best = jnp.max(cols_ref[...], axis=0, keepdims=True)
    out_ref[0:1, :] = jnp.where(late == 0, jnp.maximum(own_best, cols_best), own_best)
    out_ref[1:2, :] = jnp.where(late == 0, -1.0, cols_best)


def score_pairs(own, other, lone, beside):
    vmem = pl.BlockSpec(memory_space=pltpu.VMEM)
    return pl.pallas_call(
        pairs_kernel,
        in_specs=[vmem] * 4,
        out_specs=[vmem] * 2,
        out_shape=[
            jax.ShapeDtypeStruct((2, ROWS), jnp.float32),
            jax.ShapeDtypeStruct((1, LONE), jnp.float32),
        ],
        scratch_shapes=[
            pltpu.VMEM((ROWS, LANES), jnp.float32),
            pltpu.VMEM((ROWS, LANES), jnp.float32),
            pltpu.VMEM((8, ROWS), jnp.float32),
            pltpu.VMEM((LONE + FACTS, D), jnp.bfloat16),
        ],
        compiler_params=pltpu.CompilerParams(vmem_limit_bytes=20 * MIB),
        name="pairs",
    )(own, other, lone, beside)


def as_table(row):
    mine = iota((GROUP, LANES), 1) >> 4 == iota((GROUP, LANES), 0)
    parts = []
    for b in range(GROUPS):
        part = jnp.where(mine, row[:, b * LANES:(b + 1) * LANES], 0.0)
        for shift in (64, 32, 16):
            part = part + pltpu.roll(part, shift, 1)
        parts.append(part)
    return jnp.concatenate(parts, axis=0)


def finish_kernel(lone_ref, beside_ref, late_ref, best_ref, found_ref, out_ref):
    core, late = my_core(), my_late()
    late_rank, late_peer, late_slot = lone_facts(late_ref)
    late_column = jnp.broadcast_to(late_rank, (LANES, LONE))
    late_column = jnp.concatenate(
        [late_column[:, b * LANES:(b + 1) * LANES].T for b in range(LONE // LANES)], axis=0
    )
    late_column = wide(late_column, LONE)
    late_best = jnp.full((LONE, LANES), -1.0, jnp.float32)
    found = []
    for ref in (lone_ref, beside_ref):
        rank, peer, slot = lone_facts(ref)
        scores = dot_nt(late_ref[:LONE, :], ref[:LONE, :])
        late_best = jnp.maximum(late_best, narrow_rows(jnp.where(rank < late_column, scores, -1.0)))
        best = jnp.max(jnp.where(late_column < rank, scores, -1.0), axis=0, keepdims=True)
        found.append((best, peer, slot))
    late_best = jnp.concatenate(
        [
            jnp.max(late_best[b * LANES:(b + 1) * LANES, :].T, axis=0, keepdims=True)
            for b in range(LONE // LANES)
        ],
        axis=1,
    )
    earlier_found = found_ref[...]
    own = jnp.maximum(found[0][0], jnp.where(late == 1, earlier_found, -1.0))
    other = jnp.maximum(found[1][0], jnp.where(late == 0, earlier_found, -1.0))
    best = jnp.concatenate([own, other, late_best], axis=1)
    peer = jnp.concatenate([found[0][1], found[1][1], late_peer], axis=1)
    slot = jnp.concatenate(
        [found[0][2] + SLOTS * core, found[1][2] + SLOTS * (1 - core), late_slot + 2 * SLOTS], axis=1
    )
    at_peer = ones_where(iota((PEERS, 3 * LONE), 0) == peer)
    at_slot = iota((HALF, 3 * LONE), 0) == slot
    first, second, third = (part.astype(jnp.float32) for part in thirds(best))
    sums = jnp.concatenate([jnp.where(at_slot, part, 0.0) for part in (first, 1.0, second, third)], axis=0)
    sums = dot_nt(at_peer, sums.astype(jnp.bfloat16))
    front, back = sums[:, :LANES], sums[:, LANES:]
    value = front + (back + pltpu.roll(back, HALF, 1))
    table = jnp.where(pltpu.roll(front, HALF, 1) > 0.5, value, -1.0)
    lane = iota((PEERS, LANES), 1)
    rest = jnp.where(
        lane >> 4 == core,
        as_table(best_ref[0:1, :]),
        jnp.where(lane < 2 * SLOTS, as_table(best_ref[1:2, :]), -1.0),
    )
    out_ref[...] = jnp.where(lane < HALF, jnp.maximum(table, rest), -1.0)


def finish(lone, beside, late_rows, best, found):
    return pl.pallas_call(
        finish_kernel,
        in_specs=[pl.BlockSpec(memory_space=pltpu.VMEM)] * 5,
        out_specs=pl.BlockSpec(memory_space=pltpu.VMEM),
        out_shape=jax.ShapeDtypeStruct((PEERS, LANES), jnp.float32),
        compiler_params=pltpu.CompilerParams(vmem_limit_bytes=8 * MIB),
        name="finish",
    )(lone, beside, late_rows, best, found)


def reply_kernel(table_ref, cluster_ref, index_ref, out_ref):
    cluster = cluster_ref[...]
    index = index_ref[0:1, :]
    count = index_ref[1:2, :]
    rows = cluster.shape[1]
    table = table_ref[...]
    lane = iota((PEERS, LANES), 1)
    early = jnp.maximum(table, pltpu.roll(table, PEERS - 4, 0))
    beside = jnp.where(
        lane < SLOTS,
        pltpu.roll(table, LANES - 2 * SLOTS, 1),
        pltpu.roll(pltpu.roll(table, PEERS - 4, 0), LANES - SLOTS, 1),
    )
    late = jnp.maximum(pltpu.roll(early, PEERS - 1, 0), beside)
    both = jnp.concatenate([early.T[:2 * SLOTS, :], late.T[:2 * SLOTS, :]], axis=0)
    chosen = ones_where(iota((PEERS, rows), 0) == pair_of(cluster, jnp.zeros_like(index)) * 2)
    picked = dot_nn(jnp.concatenate(thirds(both), axis=0), chosen)
    size = 4 * SLOTS
    picked = picked[:size, :] + (picked[size:2 * size, :] + picked[2 * size:, :])
    at = (index & 1) * SLOTS + slot_of(index)
    here = iota((4 * SLOTS, rows), 0)
    here = ((here == at) & (index < 32)) | ((here == at + 2 * SLOTS) & (index + 32 >= count))
    out_ref[...] = jnp.max(jnp.where(here, picked, -1.0), axis=0, keepdims=True)


def read_reply(table, cluster, index):
    rows = cluster.shape[0]
    best = pl.pallas_call(
        reply_kernel,
        in_specs=[pl.BlockSpec(memory_space=pltpu.VMEM)] * 3,
        out_specs=pl.BlockSpec(memory_space=pltpu.VMEM),
        out_shape=jax.ShapeDtypeStruct((1, rows), jnp.float32),
        compiler_params=pltpu.CompilerParams(vmem_limit_bytes=8 * MIB),
        name="reply",
    )(table, cluster.reshape(1, rows), index)
    return best.reshape(rows)


def device(chip, core, column):
    return (chip * 2 + core) * 4 + column


SWAP = [
    (device(chip, core, column), device(chip, 1 - core, column))
    for chip in range(16)
    for core in range(2)
    for column in range(4)
]
OTHER_CHIP = [
    (device(chip, core, column), device(chip, core, column ^ 1))
    for chip in range(16)
    for core in range(2)
    for column in range(4)
]


def shards(embeddings, cluster, order):
    message, index = pack(embeddings, cluster, order)
    own = lax.all_to_all(message, AXES, split_axis=0, concat_axis=0, tiled=True)
    other = lax.ppermute(own, AXES, SWAP)

    def score(lone, far):
        beside = lax.ppermute(lone, AXES, SWAP)
        far = lax.ppermute(far, AXES, OTHER_CHIP)
        best, found = score_pairs(own, other, lone, beside)
        return finish(lone, beside, far, best, found)

    lone, most = gather_lone(own)
    table = score(lone, lone)
    rounds = (most[0, 0] + LONE - 1) // LONE

    def one_round(state):
        at, table = state
        lone, _ = gather_lone(own, at // rounds)
        far, _ = gather_lone(own, at % rounds)
        return at + 1, jnp.maximum(table, score(lone, far))

    table = lax.while_loop(lambda state: state[0] < rounds * rounds, one_round, (jnp.int32(1), table))[1]
    replies = lax.all_to_all(table, AXES, split_axis=0, concat_axis=0, tiled=True)
    return read_reply(replies, cluster, index)


def solution(mesh):
    placed = (P(AXES, None), P(AXES), P(AXES))
    return jax.shard_map(
        shards, mesh=mesh, in_specs=placed, out_specs=P(AXES), check_vma=False
    )
```

```python
import functools

import jax
import jax.numpy as jnp
from jax import lax
from jax.experimental import pallas as pl
from jax.experimental.pallas import tpu as pltpu
from jax.sharding import PartitionSpec as P

D = 768
LANES = 128
HALF = LANES // 2
BLOCKS = D // LANES
SLOTS = 16
DATA = SLOTS * BLOCKS
MSG = DATA + 8
CLUSTERS = 32
PEERS = 128
ROWS = PEERS * SLOTS
GROUPS = ROWS // LANES
GROUP = LANES // SLOTS
LONE = 256
FACTS = 16
FAR = float(2**20)
BLOCK = 512
AXES = ("owner", "split")
MIB = 2**20


def slot_of(index):
    return (index & 31) >> 1


def pair_of(cluster, index):
    return ((cluster >> 1) * 2 + (index & 1)) * 2 + (cluster & 1)


def my_core():
    return lax.axis_index("owner") % 2


def my_late():
    return lax.axis_index("split") % 2


def iota(shape, axis):
    return lax.broadcasted_iota(jnp.int32, shape, axis)


def ones_where(mask):
    return jnp.where(mask, 1.0, 0.0).astype(jnp.bfloat16)


def dot_nt(a, b):
    return lax.dot_general(a, b, (((1,), (1,)), ((), ())), preferred_element_type=jnp.float32)


def dot_nn(a, b):
    return lax.dot_general(a, b, (((1,), (0,)), ((), ())), preferred_element_type=jnp.float32)


def thirds(x):
    first = x.astype(jnp.bfloat16)
    left = x - first.astype(jnp.float32)
    second = left.astype(jnp.bfloat16)
    return first, second, (left - second.astype(jnp.float32)).astype(jnp.bfloat16)


def pack_kernel(
    emb_hbm, cluster_hbm, order_hbm, out_ref, index_ref, emb_ref, cluster_ref, order_ref, sems, unit_ref, at_ref,
    some_ref, some_at_ref, late_ref, meta_ref, past_ref
):
    step = pl.program_id(0)
    rows = emb_ref.shape[0]
    pairs = PEERS // 2
    tile = pairs // pl.num_programs(0)

    @pl.when(step == 0)
    def _():
        chunk = rows // 4
        spans = [slice(i * chunk, (i + 1) * chunk) for i in range(4)]
        fetches = [
            pltpu.make_async_copy(cluster_hbm, cluster_ref, sems.at[4]),
            pltpu.make_async_copy(order_hbm, order_ref, sems.at[5]),
        ] + [
            pltpu.make_async_copy(emb_hbm.at[at, :], emb_ref.at[at, :], sems.at[i])
            for i, at in enumerate(spans)
        ]
        for fetch in fetches:
            fetch.start()
        fetches[0].wait()
        fetches[1].wait()
        cluster = cluster_ref[...]
        rank = order_ref[...]
        hit = iota((CLUSTERS, rows), 0) == cluster
        hits = ones_where(hit)
        upper = ones_where(iota((LANES, LANES), 0) <= iota((LANES, LANES), 1))
        blocks = rows // LANES
        ahead = dot_nn(hits, ones_where(iota((rows, LANES), 0) >> 7 < iota((rows, LANES), 1)))
        counted = jnp.concatenate(
            [
                dot_nn(hits[:, b * LANES:(b + 1) * LANES], upper) + ahead[:, b:b + 1]
                for b in range(blocks)
            ],
            axis=1,
        )
        counts = jnp.broadcast_to(ahead[:, blocks:blocks + 1], (CLUSTERS, LANES))
        below = ones_where(iota((CLUSTERS, CLUSTERS), 1) < iota((CLUSTERS, CLUSTERS), 0))
        over = jnp.maximum(counts - 32.0, 0.0)
        begin = dot_nn(below, over.astype(jnp.bfloat16))

        def of_row(x):
            return jnp.sum(jnp.where(hit, x, 0.0), axis=0, keepdims=True).astype(jnp.int32)

        index = of_row(counted) - 1
        count = of_row(counts[:, :1])
        index_ref[0:1, :] = index
        index_ref[1:2, :] = count
        slot = slot_of(index)
        pair = pair_of(cluster, index)
        first = index < 32
        last = index + 32 >= count
        at_ref[0:1, :] = jnp.where(first, pair * SLOTS + slot, -1)
        at_ref[1:2, :] = jnp.where(first, -1, of_row(begin[:, :1]) + index - 32)
        at_ref[2:3, :] = pair
        at_ref[3:4, :] = slot
        past_ref[0] = jnp.sum(over[:, :1]).astype(jnp.int32)
        sends = iota((pairs, rows), 0) == pair
        sends = jnp.concatenate(
            [jnp.where(sends & first, 1.0, 0.0), jnp.where(sends & last, 1.0, 0.0)], axis=0
        )
        high = ((rank >> 9) + 1).astype(jnp.float32)
        low = ((rank & 511) - 256).astype(jnp.float32)
        at_slot = ones_where((iota((LANES, rows), 0) & (SLOTS - 1)) == slot)
        meta_ref[0] = dot_nt((sends * high).astype(jnp.bfloat16), at_slot)
        meta_ref[1] = dot_nt((sends * low).astype(jnp.bfloat16), at_slot)
        spread = jnp.where(iota((CLUSTERS, LANES), 0) == iota((CLUSTERS, LANES), 1), counts, 0.0)
        meta_ref[2] = jnp.broadcast_to(jnp.sum(spread, axis=0, keepdims=True), (PEERS, LANES))
        place = iota((PEERS, CLUSTERS), 0) & (pairs - 1)
        theirs = ones_where((place >> 2) * 2 + (place & 1) == iota((PEERS, CLUSTERS), 1))
        meta_ref[3] = dot_nn(theirs, counts.astype(jnp.bfloat16))
        for fetch, at in zip(fetches[2:], spans):
            fetch.wait()
            values = emb_ref[at, :].astype(jnp.float32)
            total = jnp.sum(values * values, axis=1, keepdims=True)
            unit_ref[at, :] = (values * lax.rsqrt(total + 1e-06)).astype(jnp.bfloat16)

    def bring(chunk):
        start = chunk * LANES
        chosen = ones_where(iota((LANES, rows), 0) + start == at_ref[1:2, :])
        some_ref[pl.ds(start, LANES), :] = dot_nn(chosen, unit_ref[...]).astype(jnp.bfloat16)
        places = jnp.where(iota((8, rows), 0) == 0, at_ref[2:3, :] + 1, at_ref[3:4, :])
        place = dot_nt(places.astype(jnp.float32).astype(jnp.bfloat16), chosen)
        target = ((place[0:1, :] - 1.0) * SLOTS + place[1:2, :]).astype(jnp.int32)
        some_at_ref[chunk] = jnp.broadcast_to(jnp.where(place[0:1, :] > 0.5, target, -1), (8, LANES))

    @pl.when(step == 0)
    def _():
        bring(0)

    size = tile * SLOTS
    chosen = ones_where(iota((size, rows), 0) + step * size == at_ref[0:1, :])
    early = dot_nn(chosen, unit_ref[...])

    def spread_some(chunk, late):
        here = iota((size, LANES), 0) + step * size == some_at_ref[chunk][0:1, :]
        some = dot_nn(ones_where(here), some_ref[chunk * LANES:(chunk + 1) * LANES, :])
        taken = jnp.sum(jnp.where(here, 1.0, 0.0), axis=1, keepdims=True)
        return jnp.where(taken > 0.5, some, late)

    late = spread_some(0, early)
    start = pl.multiple_of(step * tile, tile)

    def put(half, rows_at):
        packed = rows_at.astype(jnp.bfloat16)
        for block in range(BLOCKS):
            out_ref[:, half, block * SLOTS:(block + 1) * SLOTS, :] = packed[
                :, block * LANES:(block + 1) * LANES
            ].reshape(tile, SLOTS, LANES)

    put(0, early)
    put(1, late)
    late_ref[...] = late
    at = iota((tile, 8, LANES), 1)
    for half in range(2):
        meta = jnp.zeros((tile, 8, LANES), jnp.float32)
        for i in range(4):
            meta = jnp.where(at == i, meta_ref[i, pl.ds(start + half * pairs, tile), :][:, None, :], meta)
        out_ref[:, half, DATA:MSG, :] = meta.astype(jnp.bfloat16)

    @pl.when(past_ref[0] > LANES)
    def _():
        for chunk in range(1, rows // LANES // 2):
            bring(chunk)
            late_ref[...] = spread_some(chunk, late_ref[...])
        put(1, late_ref[...])


def pack(embeddings, cluster, order):
    rows = embeddings.shape[0]
    steps = 2
    message, index = pl.pallas_call(
        pack_kernel,
        grid=(steps,),
        in_specs=[pl.BlockSpec(memory_space=pltpu.HBM)] * 3,
        out_specs=[
            pl.BlockSpec((PEERS // 2 // steps, 2, MSG, LANES), lambda i: (i, 0, 0, 0)),
            pl.BlockSpec((2, rows), lambda i: (0, 0)),
        ],
        out_shape=[
            jax.ShapeDtypeStruct((PEERS // 2, 2, MSG, LANES), jnp.bfloat16),
            jax.ShapeDtypeStruct((2, rows), jnp.int32),
        ],
        scratch_shapes=[
            pltpu.VMEM((rows, D), jnp.bfloat16),
            pltpu.VMEM((1, rows), jnp.int32),
            pltpu.VMEM((1, rows), jnp.int32),
            pltpu.SemaphoreType.DMA((6,)),
            pltpu.VMEM((rows, D), jnp.bfloat16),
            pltpu.VMEM((8, rows), jnp.int32),
            pltpu.VMEM((rows // 2, D), jnp.bfloat16),
            pltpu.VMEM((rows // LANES // 2, 8, LANES), jnp.int32),
            pltpu.VMEM((rows // steps, D), jnp.float32),
            pltpu.VMEM((4, PEERS, LANES), jnp.float32),
            pltpu.SMEM((1,), jnp.int32),
        ],
        compiler_params=pltpu.CompilerParams(vmem_limit_bytes=121 * MIB // 2),
        name="pack",
    )(embeddings, cluster.reshape(1, rows), order.reshape(1, rows))
    return message.reshape(PEERS, MSG, LANES), index


def units_of(ref, start, count):
    first, peers = start // SLOTS, count // SLOTS
    return jnp.concatenate(
        [
            ref[first:first + peers, b * SLOTS:(b + 1) * SLOTS, :].reshape(count, LANES)
            for b in range(BLOCKS)
        ],
        axis=1,
    )


def meta_of(ref):
    meta = ref[:, DATA:MSG, :].astype(jnp.float32).reshape(GROUPS, GROUP, 8, LANES)
    mine = iota((1, GROUP, 8, LANES), 3) >> 4 == iota((1, GROUP, 8, LANES), 1)
    return jnp.sum(jnp.where(mine, meta, 0.0), axis=1), meta


def rank_from(high, low):
    return jnp.where(high > 0.5, high * 512.0 + low, FAR)


def ranks_of(ref):
    held, _ = meta_of(ref)
    return rank_from(held[:, 0:1, :], held[:, 1:2, :])


def as_row(blocks):
    return jnp.concatenate([blocks[b] for b in range(GROUPS)], axis=1)


def as_columns(blocks, out_ref):
    for b in range(GROUPS):
        out_ref[b * LANES:(b + 1) * LANES, :] = jnp.broadcast_to(blocks[b], (LANES, LANES)).T


def row_of_best(ref):
    return jnp.concatenate(
        [
            jnp.max(ref[b * LANES:(b + 1) * LANES, :].T, axis=0, keepdims=True)
            for b in range(ref.shape[0] // LANES)
        ],
        axis=1,
    )


def lone_kernel(round_ref, msg_ref, out_ref, rounds_ref, more_ref):
    core = my_core()
    first = 0 if round_ref is None else round_ref[0] * LONE
    held, meta = meta_of(msg_ref)
    high, low, count = (held[:, i:i + 1, :] for i in (0, 1, 3))
    half = jnp.floor((jnp.maximum(meta[:, :, 2, :] - 32.0, 0.0) + 1.0) * 0.5)
    most = jnp.sum(jnp.sum(half, axis=0), axis=0, keepdims=True)
    most = jnp.max(most, axis=1, keepdims=True).astype(jnp.int32)
    rounds = (most + LONE - 1) // LONE
    rounds_ref[...] = rounds
    more_ref[...] = rounds * rounds - 1

    index = (2 * (iota((GROUPS, 1, LANES), 2) & 15) + core + 32).astype(jnp.float32)
    lone = jnp.where(index < count, 1.0, 0.0)
    lone = jnp.concatenate([lone[b] for b in range(GROUPS)], axis=0).astype(jnp.bfloat16)
    upper = ones_where(iota((LANES, LANES), 0) <= iota((LANES, LANES), 1))
    counted = dot_nn(lone, upper)
    whole = jnp.broadcast_to(counted[:, LANES - 1:LANES], (GROUPS, LANES)).astype(jnp.bfloat16)
    below = ones_where(iota((GROUPS, GROUPS), 1) < iota((GROUPS, GROUPS), 0))
    position = (counted + dot_nn(below, whole)).astype(jnp.int32) - 1 - first
    position = jnp.where(lone > 0.5, position, -1)
    position = jnp.concatenate([position[b:b + 1, :] for b in range(GROUPS)], axis=1)
    chosen = ones_where(iota((LONE, ROWS), 0) == position)
    out_ref[:LONE, :] = dot_nn(chosen, units_of(msg_ref, 0, ROWS)).astype(jnp.bfloat16)
    at = iota((FACTS, ROWS), 0)
    row = iota((FACTS, ROWS), 1)
    facts = jnp.where(at == 2, row >> 4, jnp.where(at == 3, row & 15, 0)).astype(jnp.float32)
    facts = jnp.where(at == 0, as_row(high), jnp.where(at == 1, as_row(low), facts))
    facts = dot_nt(facts.astype(jnp.bfloat16), chosen).astype(jnp.bfloat16)
    out_ref[LONE:, :LONE] = facts
    out_ref[LONE:, LONE:] = jnp.zeros((FACTS, D - LONE), jnp.bfloat16)


def gather_lone(msg, round_at=None):
    some = [] if round_at is None else [round_at.reshape(1)]
    return pl.pallas_call(
        lone_kernel if some else functools.partial(lone_kernel, None),
        in_specs=[pl.BlockSpec(memory_space=pltpu.SMEM)] * len(some)
        + [pl.BlockSpec(memory_space=pltpu.VMEM)],
        out_specs=[pl.BlockSpec(memory_space=pltpu.VMEM)] * 3,
        out_shape=[
            jax.ShapeDtypeStruct((LONE + FACTS, D), jnp.bfloat16),
            jax.ShapeDtypeStruct((1, 1), jnp.int32),
            jax.ShapeDtypeStruct((1, 1), jnp.int32),
        ],
        compiler_params=pltpu.CompilerParams(vmem_limit_bytes=16 * MIB),
        name="lone",
    )(*some, msg)


def narrow_rows(x):
    best = x[:, :LANES]
    for b in range(1, x.shape[1] // LANES):
        best = jnp.maximum(best, x[:, b * LANES:(b + 1) * LANES])
    return best


def narrow_cols(x):
    return jnp.max(x.reshape(x.shape[0] // 8, 8, x.shape[1]), axis=0)


def wide(column, count):
    return jnp.concatenate([column] * (count // LANES), axis=1)


def span(i):
    return slice(i * BLOCK, (i + 1) * BLOCK)


def lone_facts(ref):
    facts = ref[LONE:, :LONE].astype(jnp.float32)
    peer = jnp.where(facts[0:1, :] > 0.5, facts[2:3, :].astype(jnp.int32), -1)
    return rank_from(facts[0:1, :], facts[1:2, :]), peer, facts[3:4, :].astype(jnp.int32)


def pairs_kernel(
    own_ref, other_ref, lone_ref, beside_ref, out_ref, found_ref, rank_ref, rows_ref, cols_ref, some_ref
):
    core, late = my_core(), my_late()

    @pl.when(late == 1)
    def _():
        some_ref[...] = lone_ref[...]

    @pl.when(late == 0)
    def _():
        some_ref[...] = beside_ref[...]

    own_ranks = ranks_of(own_ref)
    as_columns(own_ranks, rank_ref)
    count = ROWS // BLOCK
    cols_ref[...] = jnp.full((8, ROWS), -1.0, jnp.float32)
    some = some_ref[:LONE, :]
    some_rank, _, _ = lone_facts(some_ref)
    found = jnp.full((8, LONE), -1.0, jnp.float32)
    for i in range(count):
        scores = dot_nt(units_of(own_ref, i * BLOCK, BLOCK), some)
        rank = wide(rank_ref[span(i), :], LONE)
        rows_ref[span(i), :] = narrow_rows(jnp.where(some_rank < rank, scores, -1.0))
        found = jnp.maximum(found, narrow_cols(jnp.where(rank < some_rank, scores, -1.0)))
    found_ref[...] = jnp.max(found, axis=0, keepdims=True)

    def score(right_ref, row, i, j, size, both):
        left_at, right_at = slice(i * size, (i + 1) * size), slice(j * size, (j + 1) * size)
        scores = dot_nt(units_of(own_ref, i * size, size), units_of(right_ref, j * size, size))
        earlier = row[:, right_at] < wide(rank_ref[left_at, :], size)
        kept = narrow_rows(jnp.where(earlier, scores, -1.0))
        rows_ref[left_at, :] = jnp.maximum(rows_ref[left_at, :], kept)
        if both:
            kept = narrow_cols(jnp.where(earlier, -1.0, scores))
            cols_ref[:, right_at] = jnp.maximum(cols_ref[:, right_at], kept)

    @pl.when(late == 0)
    def _():
        row = as_row(own_ranks)
        size = BLOCK // 2
        for i in range(2 * count):
            for j in range(i, 2 * count):
                score(own_ref, row, i, j, size, i != j)

    def across(firsts, seconds):
        row = as_row(ranks_of(other_ref))
        for i in firsts:
            for j in seconds:
                score(other_ref, row, i, j, BLOCK, True)

    @pl.when((late == 1) & (core == 0))
    def _():
        across(range(count), range(count // 2))

    @pl.when((late == 1) & (core == 1))
    def _():
        across(range(count // 2, count), range(count))

    own_best = row_of_best(rows_ref)
    cols_best = jnp.max(cols_ref[...], axis=0, keepdims=True)
    out_ref[0:1, :] = jnp.where(late == 0, jnp.maximum(own_best, cols_best), own_best)
    out_ref[1:2, :] = jnp.where(late == 0, -1.0, cols_best)


def score_pairs(own, other, lone, beside):
    vmem = pl.BlockSpec(memory_space=pltpu.VMEM)
    return pl.pallas_call(
        pairs_kernel,
        in_specs=[vmem] * 4,
        out_specs=[vmem] * 2,
        out_shape=[
            jax.ShapeDtypeStruct((2, ROWS), jnp.float32),
            jax.ShapeDtypeStruct((1, LONE), jnp.float32),
        ],
        scratch_shapes=[
            pltpu.VMEM((ROWS, LANES), jnp.float32),
            pltpu.VMEM((ROWS, LANES), jnp.float32),
            pltpu.VMEM((8, ROWS), jnp.float32),
            pltpu.VMEM((LONE + FACTS, D), jnp.bfloat16),
        ],
        compiler_params=pltpu.CompilerParams(vmem_limit_bytes=20 * MIB),
        name="pairs",
    )(own, other, lone, beside)


def as_table(row):
    mine = iota((GROUP, LANES), 1) >> 4 == iota((GROUP, LANES), 0)
    parts = []
    for b in range(GROUPS):
        part = jnp.where(mine, row[:, b * LANES:(b + 1) * LANES], 0.0)
        for shift in (64, 32, 16):
            part = part + pltpu.roll(part, shift, 1)
        parts.append(part)
    return jnp.concatenate(parts, axis=0)


def finish_kernel(lone_ref, beside_ref, late_ref, best_ref, found_ref, out_ref):
    core, late = my_core(), my_late()
    late_rank, late_peer, late_slot = lone_facts(late_ref)
    late_column = jnp.broadcast_to(late_rank, (LANES, LONE))
    late_column = jnp.concatenate(
        [late_column[:, b * LANES:(b + 1) * LANES].T for b in range(LONE // LANES)], axis=0
    )
    late_column = wide(late_column, LONE)
    late_best = jnp.full((LONE, LANES), -1.0, jnp.float32)
    found = []
    for ref in (lone_ref, beside_ref):
        rank, peer, slot = lone_facts(ref)
        scores = dot_nt(late_ref[:LONE, :], ref[:LONE, :])
        late_best = jnp.maximum(late_best, narrow_rows(jnp.where(rank < late_column, scores, -1.0)))
        best = jnp.max(jnp.where(late_column < rank, scores, -1.0), axis=0, keepdims=True)
        found.append((best, peer, slot))
    late_best = jnp.concatenate(
        [
            jnp.max(late_best[b * LANES:(b + 1) * LANES, :].T, axis=0, keepdims=True)
            for b in range(LONE // LANES)
        ],
        axis=1,
    )
    earlier_found = found_ref[...]
    own = jnp.maximum(found[0][0], jnp.where(late == 1, earlier_found, -1.0))
    other = jnp.maximum(found[1][0], jnp.where(late == 0, earlier_found, -1.0))
    best = jnp.concatenate([own, other, late_best], axis=1)
    peer = jnp.concatenate([found[0][1], found[1][1], late_peer], axis=1)
    slot = jnp.concatenate(
        [found[0][2] + SLOTS * core, found[1][2] + SLOTS * (1 - core), late_slot + 2 * SLOTS], axis=1
    )
    at_peer = ones_where(iota((PEERS, 3 * LONE), 0) == peer)
    at_slot = iota((HALF, 3 * LONE), 0) == slot
    first, second, third = (part.astype(jnp.float32) for part in thirds(best))
    sums = jnp.concatenate([jnp.where(at_slot, part, 0.0) for part in (first, 1.0, second, third)], axis=0)
    sums = dot_nt(at_peer, sums.astype(jnp.bfloat16))
    front, back = sums[:, :LANES], sums[:, LANES:]
    value = front + (back + pltpu.roll(back, HALF, 1))
    table = jnp.where(pltpu.roll(front, HALF, 1) > 0.5, value, -1.0)
    lane = iota((PEERS, LANES), 1)
    rest = jnp.where(
        lane >> 4 == core,
        as_table(best_ref[0:1, :]),
        jnp.where(lane < 2 * SLOTS, as_table(best_ref[1:2, :]), -1.0),
    )
    out_ref[...] = jnp.where(lane < HALF, jnp.maximum(table, rest), -1.0)


def finish(lone, beside, late_rows, best, found):
    return pl.pallas_call(
        finish_kernel,
        in_specs=[pl.BlockSpec(memory_space=pltpu.VMEM)] * 5,
        out_specs=pl.BlockSpec(memory_space=pltpu.VMEM),
        out_shape=jax.ShapeDtypeStruct((PEERS, LANES), jnp.float32),
        compiler_params=pltpu.CompilerParams(vmem_limit_bytes=8 * MIB),
        name="finish",
    )(lone, beside, late_rows, best, found)


def reply_kernel(table_ref, cluster_ref, index_ref, out_ref):
    cluster = cluster_ref[...]
    index = index_ref[0:1, :]
    count = index_ref[1:2, :]
    rows = cluster.shape[1]
    table = table_ref[...]
    lane = iota((PEERS, LANES), 1)
    early = jnp.maximum(table, pltpu.roll(table, PEERS - 4, 0))
    beside = jnp.where(
        lane < SLOTS,
        pltpu.roll(table, LANES - 2 * SLOTS, 1),
        pltpu.roll(pltpu.roll(table, PEERS - 4, 0), LANES - SLOTS, 1),
    )
    late = jnp.maximum(pltpu.roll(early, PEERS - 1, 0), beside)
    both = jnp.concatenate([early.T[:2 * SLOTS, :], late.T[:2 * SLOTS, :]], axis=0)
    chosen = ones_where(iota((PEERS, rows), 0) == pair_of(cluster, jnp.zeros_like(index)) * 2)
    picked = dot_nn(jnp.concatenate(thirds(both), axis=0), chosen)
    size = 4 * SLOTS
    picked = picked[:size, :] + (picked[size:2 * size, :] + picked[2 * size:, :])
    at = (index & 1) * SLOTS + slot_of(index)
    here = iota((4 * SLOTS, rows), 0)
    here = ((here == at) & (index < 32)) | ((here == at + 2 * SLOTS) & (index + 32 >= count))
    out_ref[...] = jnp.max(jnp.where(here, picked, -1.0), axis=0, keepdims=True)


def read_reply(table, cluster, index):
    rows = cluster.shape[0]
    best = pl.pallas_call(
        reply_kernel,
        in_specs=[pl.BlockSpec(memory_space=pltpu.VMEM)] * 3,
        out_specs=pl.BlockSpec(memory_space=pltpu.VMEM),
        out_shape=jax.ShapeDtypeStruct((1, rows), jnp.float32),
        compiler_params=pltpu.CompilerParams(vmem_limit_bytes=8 * MIB),
        name="reply",
    )(table, cluster.reshape(1, rows), index)
    return best.reshape(rows)


def device(chip, core, column):
    return (chip * 2 + core) * 4 + column


SWAP = [
    (device(chip, core, column), device(chip, 1 - core, column))
    for chip in range(16)
    for core in range(2)
    for column in range(4)
]
OTHER_CHIP = [
    (device(chip, core, column), device(chip, core, column ^ 1))
    for chip in range(16)
    for core in range(2)
    for column in range(4)
]


def shards(embeddings, cluster, order):
    message, index = pack(embeddings, cluster, order)
    own = lax.all_to_all(message, AXES, split_axis=0, concat_axis=0, tiled=True)

    def score(other, lone, far):
        beside = lax.ppermute(lone, AXES, SWAP)
        far = lax.ppermute(far, AXES, OTHER_CHIP)
        best, found = score_pairs(own, other, lone, beside)
        return finish(lone, beside, far, best, found)

    other = lax.ppermute(own, AXES, SWAP)
    lone, rounds, more = gather_lone(own)
    table = score(other, lone, lone)

    def one_round(state):
        left, table = state
        other = lax.ppermute(own, AXES, SWAP)
        lone = gather_lone(own, lax.div(left, rounds[0, 0]))[0]
        far = gather_lone(own, lax.rem(left, rounds[0, 0]))[0]
        return left - 1, jnp.maximum(table, score(other, lone, far))

    table = lax.while_loop(lambda state: state[0] > 0, one_round, (more[0, 0], table))[1]
    replies = lax.all_to_all(table, AXES, split_axis=0, concat_axis=0, tiled=True)
    return read_reply(replies, cluster, index)


def solution(mesh):
    placed = (P(AXES, None), P(AXES), P(AXES))
    return jax.shard_map(
        shards, mesh=mesh, in_specs=placed, out_specs=P(AXES), check_vma=False
    )
```

```python
import functools

import jax
import jax.numpy as jnp
from jax import lax
from jax.experimental import pallas as pl
from jax.experimental.pallas import tpu as pltpu
from jax.sharding import PartitionSpec as P

D = 768
LANES = 128
HALF = LANES // 2
BLOCKS = D // LANES
SLOTS = 16
DATA = SLOTS * BLOCKS
MSG = DATA + 8
CLUSTERS = 32
PEERS = 128
ROWS = PEERS * SLOTS
GROUPS = ROWS // LANES
GROUP = LANES // SLOTS
LONE = 256
FACTS = 16
FAR = float(2**20)
BLOCK = 512
AXES = ("owner", "split")
MIB = 2**20


def slot_of(index):
    return (index & 31) >> 1


def pair_of(cluster, index):
    return ((cluster >> 1) * 2 + (index & 1)) * 2 + (cluster & 1)


def my_core():
    return lax.axis_index("owner") % 2


def my_late():
    return lax.axis_index("split") % 2


def iota(shape, axis):
    return lax.broadcasted_iota(jnp.int32, shape, axis)


def ones_where(mask):
    return jnp.where(mask, 1.0, 0.0).astype(jnp.bfloat16)


def dot_nt(a, b):
    return lax.dot_general(a, b, (((1,), (1,)), ((), ())), preferred_element_type=jnp.float32)


def dot_nn(a, b):
    return lax.dot_general(a, b, (((1,), (0,)), ((), ())), preferred_element_type=jnp.float32)


def thirds(x):
    first = x.astype(jnp.bfloat16)
    left = x - first.astype(jnp.float32)
    second = left.astype(jnp.bfloat16)
    return first, second, (left - second.astype(jnp.float32)).astype(jnp.bfloat16)


def pack_kernel(
    emb_hbm, cluster_hbm, order_hbm, out_hbm, index_ref, out_ref, emb_ref, cluster_ref, order_ref, sems, unit_ref, at_ref,
    some_ref, some_at_ref, meta_ref, past_ref
):
    rows = emb_ref.shape[0]
    pairs = PEERS // 2
    steps = 4
    tile = pairs // steps
    size = tile * SLOTS
    chunk = rows // 2
    spans = [slice(i * chunk, (i + 1) * chunk) for i in range(2)]
    fetches = [
        pltpu.make_async_copy(cluster_hbm, cluster_ref, sems.at[4]),
        pltpu.make_async_copy(order_hbm, order_ref, sems.at[5]),
    ] + [
        pltpu.make_async_copy(emb_hbm.at[at, :], emb_ref.at[at, :], sems.at[i])
        for i, at in enumerate(spans)
    ]
    for fetch in fetches:
        fetch.start()
    fetches[0].wait()
    fetches[1].wait()
    cluster = cluster_ref[...]
    rank = order_ref[...]
    hit = iota((CLUSTERS, rows), 0) == cluster
    hits = ones_where(hit)
    upper = ones_where(iota((LANES, LANES), 0) <= iota((LANES, LANES), 1))
    blocks = rows // LANES
    ahead = dot_nn(hits, ones_where(iota((rows, LANES), 0) >> 7 < iota((rows, LANES), 1)))
    counted = jnp.concatenate(
        [
            dot_nn(hits[:, b * LANES:(b + 1) * LANES], upper) + ahead[:, b:b + 1]
            for b in range(blocks)
        ],
        axis=1,
    )
    counts = jnp.broadcast_to(ahead[:, blocks:blocks + 1], (CLUSTERS, LANES))
    below = ones_where(iota((CLUSTERS, CLUSTERS), 1) < iota((CLUSTERS, CLUSTERS), 0))
    over = jnp.maximum(counts - 32.0, 0.0)
    begin = dot_nn(below, over.astype(jnp.bfloat16))

    def of_row(x):
        return jnp.sum(jnp.where(hit, x, 0.0), axis=0, keepdims=True).astype(jnp.int32)

    index = of_row(counted) - 1
    count = of_row(counts[:, :1])
    index_ref[0:1, :] = index
    index_ref[1:2, :] = count
    slot = slot_of(index)
    pair = pair_of(cluster, index)
    first = index < 32
    last = index + 32 >= count
    at_ref[0:1, :] = jnp.where(first, pair * SLOTS + slot, -1)
    at_ref[1:2, :] = jnp.where(first, -1, of_row(begin[:, :1]) + index - 32)
    at_ref[2:3, :] = pair
    at_ref[3:4, :] = slot
    past_ref[0] = jnp.sum(over[:, :1]).astype(jnp.int32)
    sends = iota((pairs, rows), 0) == pair
    sends = jnp.concatenate(
        [jnp.where(sends & first, 1.0, 0.0), jnp.where(sends & last, 1.0, 0.0)], axis=0
    )
    high = ((rank >> 9) + 1).astype(jnp.float32)
    low = ((rank & 511) - 256).astype(jnp.float32)
    at_slot = ones_where((iota((LANES, rows), 0) & (SLOTS - 1)) == slot)
    meta_ref[0] = dot_nt((sends * high).astype(jnp.bfloat16), at_slot)
    meta_ref[1] = dot_nt((sends * low).astype(jnp.bfloat16), at_slot)
    spread = jnp.where(iota((CLUSTERS, LANES), 0) == iota((CLUSTERS, LANES), 1), counts, 0.0)
    meta_ref[2] = jnp.broadcast_to(jnp.sum(spread, axis=0, keepdims=True), (PEERS, LANES))
    place = iota((PEERS, CLUSTERS), 0) & (pairs - 1)
    theirs = ones_where((place >> 2) * 2 + (place & 1) == iota((PEERS, CLUSTERS), 1))
    meta_ref[3] = dot_nn(theirs, counts.astype(jnp.bfloat16))
    for fetch, at in zip(fetches[2:], spans):
        fetch.wait()
        values = emb_ref[at, :].astype(jnp.float32)
        total = jnp.sum(values * values, axis=1, keepdims=True)
        unit_ref[at, :] = (values * lax.rsqrt(total + 1e-06)).astype(jnp.bfloat16)

    def bring(chunk):
        start = chunk * LANES
        chosen = ones_where(iota((LANES, rows), 0) + start == at_ref[1:2, :])
        some_ref[pl.ds(start, LANES), :] = dot_nn(chosen, unit_ref[...]).astype(jnp.bfloat16)
        places = jnp.where(iota((8, rows), 0) == 0, at_ref[2:3, :] + 1, at_ref[3:4, :])
        place = dot_nt(places.astype(jnp.float32).astype(jnp.bfloat16), chosen)
        target = ((place[0:1, :] - 1.0) * SLOTS + place[1:2, :]).astype(jnp.int32)
        some_at_ref[chunk] = jnp.broadcast_to(jnp.where(place[0:1, :] > 0.5, target, -1), (8, LANES))

    bring(0)

    def early_rows(step):
        return dot_nn(ones_where(iota((size, rows), 0) + step * size == at_ref[0:1, :]), unit_ref[...])

    def spread_some(step, chunk, late):
        here = iota((size, LANES), 0) + step * size == some_at_ref[chunk][0:1, :]
        some = dot_nn(ones_where(here), some_ref[chunk * LANES:(chunk + 1) * LANES, :])
        taken = jnp.sum(jnp.where(here, 1.0, 0.0), axis=1, keepdims=True)
        return jnp.where(taken > 0.5, some, late)

    def put(step, half, rows_at):
        packed = rows_at.astype(jnp.bfloat16)
        peers = pl.ds(step * tile, tile)
        for block in range(BLOCKS):
            out_ref[peers, half, block * SLOTS:(block + 1) * SLOTS, :] = packed[
                :, block * LANES:(block + 1) * LANES
            ].reshape(tile, SLOTS, LANES)

    def send(step):
        peers = pl.ds(step * tile, tile)
        return pltpu.make_async_copy(out_ref.at[peers], out_hbm.at[peers], sems.at[step])

    at = iota((tile, 8, LANES), 1)
    for step in range(steps):
        early = early_rows(step)
        put(step, 0, early)
        put(step, 1, spread_some(step, 0, early))
        for half in range(2):
            meta = jnp.zeros((tile, 8, LANES), jnp.float32)
            first = half * pairs + step * tile
            for i in range(4):
                meta = jnp.where(at == i, meta_ref[i, first:first + tile, :][:, None, :], meta)
            out_ref[step * tile:(step + 1) * tile, half, DATA:MSG, :] = meta.astype(jnp.bfloat16)
        send(step).start()
    for step in range(steps):
        send(step).wait()

    @pl.when(past_ref[0] > LANES)
    def _():
        for chunk in range(1, rows // LANES // 2):
            bring(chunk)

        def again(step, _):
            late = early_rows(step)
            for chunk in range(rows // LANES // 2):
                late = spread_some(step, chunk, late)
            put(step, 1, late)
            send(step).start()
            send(step).wait()
            return 0

        lax.fori_loop(0, steps, again, 0)


def pack(embeddings, cluster, order):
    rows = embeddings.shape[0]
    message, index = pl.pallas_call(
        pack_kernel,
        in_specs=[pl.BlockSpec(memory_space=pltpu.HBM)] * 3,
        out_specs=[
            pl.BlockSpec(memory_space=pltpu.HBM),
            pl.BlockSpec(memory_space=pltpu.VMEM),
        ],
        out_shape=[
            jax.ShapeDtypeStruct((PEERS // 2, 2, MSG, LANES), jnp.bfloat16),
            jax.ShapeDtypeStruct((2, rows), jnp.int32),
        ],
        scratch_shapes=[
            pltpu.VMEM((PEERS // 2, 2, MSG, LANES), jnp.bfloat16),
            pltpu.VMEM((rows, D), jnp.bfloat16),
            pltpu.VMEM((1, rows), jnp.int32),
            pltpu.VMEM((1, rows), jnp.int32),
            pltpu.SemaphoreType.DMA((6,)),
            pltpu.VMEM((rows, D), jnp.bfloat16),
            pltpu.VMEM((8, rows), jnp.int32),
            pltpu.VMEM((rows // 2, D), jnp.bfloat16),
            pltpu.VMEM((rows // LANES // 2, 8, LANES), jnp.int32),
            pltpu.VMEM((4, PEERS, LANES), jnp.float32),
            pltpu.SMEM((1,), jnp.int32),
        ],
        compiler_params=pltpu.CompilerParams(vmem_limit_bytes=121 * MIB // 2),
        name="pack",
    )(embeddings, cluster.reshape(1, rows), order.reshape(1, rows))
    return message.reshape(PEERS, MSG, LANES), index


def units_of(ref, start, count):
    first, peers = start // SLOTS, count // SLOTS
    return jnp.concatenate(
        [
            ref[first:first + peers, b * SLOTS:(b + 1) * SLOTS, :].reshape(count, LANES)
            for b in range(BLOCKS)
        ],
        axis=1,
    )


def meta_of(ref):
    meta = ref[:, DATA:MSG, :].astype(jnp.float32).reshape(GROUPS, GROUP, 8, LANES)
    mine = iota((1, GROUP, 8, LANES), 3) >> 4 == iota((1, GROUP, 8, LANES), 1)
    return jnp.sum(jnp.where(mine, meta, 0.0), axis=1), meta


def rank_from(high, low):
    return jnp.where(high > 0.5, high * 512.0 + low, FAR)


def ranks_of(ref):
    held, _ = meta_of(ref)
    return rank_from(held[:, 0:1, :], held[:, 1:2, :])


def as_row(blocks):
    return jnp.concatenate([blocks[b] for b in range(GROUPS)], axis=1)


def as_columns(blocks, out_ref):
    for b in range(GROUPS):
        out_ref[b * LANES:(b + 1) * LANES, :] = jnp.broadcast_to(blocks[b], (LANES, LANES)).T


def row_of_best(ref):
    return jnp.concatenate(
        [
            jnp.max(ref[b * LANES:(b + 1) * LANES, :].T, axis=0, keepdims=True)
            for b in range(ref.shape[0] // LANES)
        ],
        axis=1,
    )


def lone_kernel(round_ref, msg_ref, out_ref, more_ref):
    core = my_core()
    first = 0 if round_ref is None else round_ref[0] * LONE
    held, meta = meta_of(msg_ref)
    high, low, count = (held[:, i:i + 1, :] for i in (0, 1, 3))
    half = jnp.floor((jnp.maximum(meta[:, :, 2, :] - 32.0, 0.0) + 1.0) * 0.5)
    most = jnp.sum(jnp.sum(half, axis=0), axis=0, keepdims=True)
    most = jnp.max(most, axis=1, keepdims=True).astype(jnp.int32)
    more_ref[...] = (most + LONE - 1) // LONE - 1

    index = (2 * (iota((GROUPS, 1, LANES), 2) & 15) + core + 32).astype(jnp.float32)
    lone = jnp.where(index < count, 1.0, 0.0)
    lone = jnp.concatenate([lone[b] for b in range(GROUPS)], axis=0).astype(jnp.bfloat16)
    upper = ones_where(iota((LANES, LANES), 0) <= iota((LANES, LANES), 1))
    counted = dot_nn(lone, upper)
    whole = jnp.broadcast_to(counted[:, LANES - 1:LANES], (GROUPS, LANES)).astype(jnp.bfloat16)
    below = ones_where(iota((GROUPS, GROUPS), 1) < iota((GROUPS, GROUPS), 0))
    position = (counted + dot_nn(below, whole)).astype(jnp.int32) - 1 - first
    position = jnp.where(lone > 0.5, position, -1)
    position = jnp.concatenate([position[b:b + 1, :] for b in range(GROUPS)], axis=1)
    chosen = ones_where(iota((LONE, ROWS), 0) == position)
    out_ref[:LONE, :] = dot_nn(chosen, units_of(msg_ref, 0, ROWS)).astype(jnp.bfloat16)
    at = iota((FACTS, ROWS), 0)
    row = iota((FACTS, ROWS), 1)
    facts = jnp.where(at == 2, row >> 4, jnp.where(at == 3, row & 15, 0)).astype(jnp.float32)
    facts = jnp.where(at == 0, as_row(high), jnp.where(at == 1, as_row(low), facts))
    facts = dot_nt(facts.astype(jnp.bfloat16), chosen).astype(jnp.bfloat16)
    out_ref[LONE:, :LONE] = facts
    out_ref[LONE:, LONE:] = jnp.zeros((FACTS, D - LONE), jnp.bfloat16)


def gather_lone(msg, round_at=None):
    some = [] if round_at is None else [round_at.reshape(1)]
    return pl.pallas_call(
        lone_kernel if some else functools.partial(lone_kernel, None),
        in_specs=[pl.BlockSpec(memory_space=pltpu.SMEM)] * len(some)
        + [pl.BlockSpec(memory_space=pltpu.VMEM)],
        out_specs=[pl.BlockSpec(memory_space=pltpu.VMEM)] * 2,
        out_shape=[
            jax.ShapeDtypeStruct((LONE + FACTS, D), jnp.bfloat16),
            jax.ShapeDtypeStruct((1, 1), jnp.int32),
        ],
        compiler_params=pltpu.CompilerParams(vmem_limit_bytes=16 * MIB),
        name="lone",
    )(*some, msg)


def narrow_rows(x):
    best = x[:, :LANES]
    for b in range(1, x.shape[1] // LANES):
        best = jnp.maximum(best, x[:, b * LANES:(b + 1) * LANES])
    return best


def narrow_cols(x):
    return jnp.max(x.reshape(x.shape[0] // 8, 8, x.shape[1]), axis=0)


def wide(column, count):
    return jnp.concatenate([column] * (count // LANES), axis=1)


def span(i):
    return slice(i * BLOCK, (i + 1) * BLOCK)


def lone_facts(ref):
    facts = ref[LONE:, :LONE].astype(jnp.float32)
    peer = jnp.where(facts[0:1, :] > 0.5, facts[2:3, :].astype(jnp.int32), -1)
    return rank_from(facts[0:1, :], facts[1:2, :]), peer, facts[3:4, :].astype(jnp.int32)


def pairs_kernel(
    own_ref, other_ref, lone_ref, beside_ref, out_ref, found_ref, rank_ref, rows_ref, cols_ref, some_ref
):
    core, late = my_core(), my_late()

    @pl.when(late == 1)
    def _():
        some_ref[...] = lone_ref[...]

    @pl.when(late == 0)
    def _():
        some_ref[...] = beside_ref[...]

    own_ranks = ranks_of(own_ref)
    as_columns(own_ranks, rank_ref)
    count = ROWS // BLOCK
    cols_ref[...] = jnp.full((8, ROWS), -1.0, jnp.float32)
    some = some_ref[:LONE, :]
    some_rank, _, _ = lone_facts(some_ref)
    found = jnp.full((8, LONE), -1.0, jnp.float32)
    for i in range(count):
        scores = dot_nt(units_of(own_ref, i * BLOCK, BLOCK), some)
        rank = wide(rank_ref[span(i), :], LONE)
        rows_ref[span(i), :] = narrow_rows(jnp.where(some_rank < rank, scores, -1.0))
        found = jnp.maximum(found, narrow_cols(jnp.where(rank < some_rank, scores, -1.0)))
    found_ref[...] = jnp.max(found, axis=0, keepdims=True)

    def score(right_ref, row, i, j, size, both):
        left_at, right_at = slice(i * size, (i + 1) * size), slice(j * size, (j + 1) * size)
        scores = dot_nt(units_of(own_ref, i * size, size), units_of(right_ref, j * size, size))
        earlier = row[:, right_at] < wide(rank_ref[left_at, :], size)
        kept = narrow_rows(jnp.where(earlier, scores, -1.0))
        rows_ref[left_at, :] = jnp.maximum(rows_ref[left_at, :], kept)
        if both:
            kept = narrow_cols(jnp.where(earlier, -1.0, scores))
            cols_ref[:, right_at] = jnp.maximum(cols_ref[:, right_at], kept)

    @pl.when(late == 0)
    def _():
        row = as_row(own_ranks)
        size = BLOCK // 2
        for i in range(2 * count):
            for j in range(i, 2 * count):
                score(own_ref, row, i, j, size, i != j)

    def across(firsts, seconds):
        row = as_row(ranks_of(other_ref))
        for i in firsts:
            for j in seconds:
                score(other_ref, row, i, j, BLOCK, True)

    @pl.when((late == 1) & (core == 0))
    def _():
        across(range(count), range(count // 2))

    @pl.when((late == 1) & (core == 1))
    def _():
        across(range(count // 2, count), range(count))

    own_best = row_of_best(rows_ref)
    cols_best = jnp.max(cols_ref[...], axis=0, keepdims=True)
    out_ref[0:1, :] = jnp.where(late == 0, jnp.maximum(own_best, cols_best), own_best)
    out_ref[1:2, :] = jnp.where(late == 0, -1.0, cols_best)


def score_pairs(own, other, lone, beside):
    vmem = pl.BlockSpec(memory_space=pltpu.VMEM)
    return pl.pallas_call(
        pairs_kernel,
        in_specs=[vmem] * 4,
        out_specs=[vmem] * 2,
        out_shape=[
            jax.ShapeDtypeStruct((2, ROWS), jnp.float32),
            jax.ShapeDtypeStruct((1, LONE), jnp.float32),
        ],
        scratch_shapes=[
            pltpu.VMEM((ROWS, LANES), jnp.float32),
            pltpu.VMEM((ROWS, LANES), jnp.float32),
            pltpu.VMEM((8, ROWS), jnp.float32),
            pltpu.VMEM((LONE + FACTS, D), jnp.bfloat16),
        ],
        compiler_params=pltpu.CompilerParams(vmem_limit_bytes=20 * MIB),
        name="pairs",
    )(own, other, lone, beside)


def as_table(row):
    mine = iota((GROUP, LANES), 1) >> 4 == iota((GROUP, LANES), 0)
    parts = []
    for b in range(GROUPS):
        part = jnp.where(mine, row[:, b * LANES:(b + 1) * LANES], 0.0)
        for shift in (64, 32, 16):
            part = part + pltpu.roll(part, shift, 1)
        parts.append(part)
    return jnp.concatenate(parts, axis=0)


def placed_by_peer(best, peer, lane):
    count = best.shape[1]
    at_peer = ones_where(iota((PEERS, count), 0) == peer)
    at_lane = iota((HALF, count), 0) == lane
    first, second, third = (part.astype(jnp.float32) for part in thirds(best))
    sums = jnp.concatenate([jnp.where(at_lane, part, 0.0) for part in (first, 1.0, second, third)], axis=0)
    sums = dot_nt(at_peer, sums.astype(jnp.bfloat16))
    front, back = sums[:, :LANES], sums[:, LANES:]
    value = front + (back + pltpu.roll(back, HALF, 1))
    return jnp.where(pltpu.roll(front, HALF, 1) > 0.5, value, -1.0)


def finish_kernel(lone_ref, beside_ref, late_ref, best_ref, found_ref, out_ref):
    core, late = my_core(), my_late()
    late_rank, late_peer, late_slot = lone_facts(late_ref)
    late_column = jnp.broadcast_to(late_rank, (LANES, LONE))
    late_column = jnp.concatenate(
        [late_column[:, b * LANES:(b + 1) * LANES].T for b in range(LONE // LANES)], axis=0
    )
    late_column = wide(late_column, LONE)
    late_best = jnp.full((LONE, LANES), -1.0, jnp.float32)
    found = []
    for ref in (lone_ref, beside_ref):
        rank, peer, slot = lone_facts(ref)
        scores = dot_nt(late_ref[:LONE, :], ref[:LONE, :])
        late_best = jnp.maximum(late_best, narrow_rows(jnp.where(rank < late_column, scores, -1.0)))
        best = jnp.max(jnp.where(late_column < rank, scores, -1.0), axis=0, keepdims=True)
        found.append((best, peer, slot))
    late_best = jnp.concatenate(
        [
            jnp.max(late_best[b * LANES:(b + 1) * LANES, :].T, axis=0, keepdims=True)
            for b in range(LONE // LANES)
        ],
        axis=1,
    )
    earlier_found = found_ref[...]
    own = jnp.maximum(found[0][0], jnp.where(late == 1, earlier_found, -1.0))
    other = jnp.maximum(found[1][0], jnp.where(late == 0, earlier_found, -1.0))
    best = jnp.concatenate([own, other, late_best], axis=1)
    peer = jnp.concatenate([found[0][1], found[1][1], late_peer], axis=1)
    slot = jnp.concatenate(
        [found[0][2] + SLOTS * core, found[1][2] + SLOTS * (1 - core), late_slot + 2 * SLOTS], axis=1
    )
    table = placed_by_peer(best, peer, slot)
    lane = iota((PEERS, LANES), 1)
    rest = jnp.where(
        lane >> 4 == core,
        as_table(best_ref[0:1, :]),
        jnp.where(lane < 2 * SLOTS, as_table(best_ref[1:2, :]), -1.0),
    )
    out_ref[...] = jnp.where(lane < HALF, jnp.maximum(table, rest), -1.0)


def finish(lone, beside, late_rows, best, found):
    return pl.pallas_call(
        finish_kernel,
        in_specs=[pl.BlockSpec(memory_space=pltpu.VMEM)] * 5,
        out_specs=pl.BlockSpec(memory_space=pltpu.VMEM),
        out_shape=jax.ShapeDtypeStruct((PEERS, LANES), jnp.float32),
        compiler_params=pltpu.CompilerParams(vmem_limit_bytes=8 * MIB),
        name="finish",
    )(lone, beside, late_rows, best, found)


def rest_kernel(own_ref, other_ref, late_ref, table_ref, out_ref, rank_ref, rows_ref):
    core = my_core()
    some = late_ref[:LONE, :]
    some_rank, peer, slot = lone_facts(late_ref)
    found = jnp.full((8, LONE), -1.0, jnp.float32)
    best = []
    for ref in (own_ref, other_ref):
        as_columns(ranks_of(ref), rank_ref)
        for i in range(ROWS // BLOCK):
            scores = dot_nt(units_of(ref, i * BLOCK, BLOCK), some)
            rank = wide(rank_ref[span(i), :], LONE)
            rows_ref[span(i), :] = narrow_rows(jnp.where(some_rank < rank, scores, -1.0))
            found = jnp.maximum(found, narrow_cols(jnp.where(rank < some_rank, scores, -1.0)))
        best.append(as_table(row_of_best(rows_ref)))
    table = placed_by_peer(jnp.max(found, axis=0, keepdims=True), peer, slot + 2 * SLOTS)
    lane = iota((PEERS, LANES), 1)
    rest = jnp.where(lane >> 4 == core, best[0], jnp.where(lane < 2 * SLOTS, best[1], table))
    out_ref[...] = jnp.maximum(table_ref[...], jnp.where(lane < HALF, rest, -1.0))


def score_rest(own, other, late_rows, table):
    return pl.pallas_call(
        rest_kernel,
        in_specs=[pl.BlockSpec(memory_space=pltpu.VMEM)] * 4,
        out_specs=pl.BlockSpec(memory_space=pltpu.VMEM),
        out_shape=jax.ShapeDtypeStruct((PEERS, LANES), jnp.float32),
        scratch_shapes=[
            pltpu.VMEM((ROWS, LANES), jnp.float32),
            pltpu.VMEM((ROWS, LANES), jnp.float32),
        ],
        compiler_params=pltpu.CompilerParams(vmem_limit_bytes=20 * MIB),
        name="rest",
    )(own, other, late_rows, table)


def reply_kernel(table_ref, cluster_ref, index_ref, out_ref):
    cluster = cluster_ref[...]
    index = index_ref[0:1, :]
    count = index_ref[1:2, :]
    rows = cluster.shape[1]
    table = table_ref[...]
    lane = iota((PEERS, LANES), 1)
    early = jnp.maximum(table, pltpu.roll(table, PEERS - 4, 0))
    beside = jnp.where(
        lane < SLOTS,
        pltpu.roll(table, LANES - 2 * SLOTS, 1),
        pltpu.roll(pltpu.roll(table, PEERS - 4, 0), LANES - SLOTS, 1),
    )
    late = jnp.maximum(pltpu.roll(early, PEERS - 1, 0), beside)
    early = jnp.maximum(early, pltpu.roll(beside, PEERS - 1, 0))
    both = jnp.concatenate([early.T[:2 * SLOTS, :], late.T[:2 * SLOTS, :]], axis=0)
    chosen = ones_where(iota((PEERS, rows), 0) == pair_of(cluster, jnp.zeros_like(index)) * 2)
    picked = dot_nn(jnp.concatenate(thirds(both), axis=0), chosen)
    size = 4 * SLOTS
    picked = picked[:size, :] + (picked[size:2 * size, :] + picked[2 * size:, :])
    at = (index & 1) * SLOTS + slot_of(index)
    here = iota((4 * SLOTS, rows), 0)
    here = ((here == at) & (index < 32)) | ((here == at + 2 * SLOTS) & (index + 32 >= count))
    out_ref[...] = jnp.max(jnp.where(here, picked, -1.0), axis=0, keepdims=True)


def read_reply(table, cluster, index):
    rows = cluster.shape[0]
    best = pl.pallas_call(
        reply_kernel,
        in_specs=[pl.BlockSpec(memory_space=pltpu.VMEM)] * 3,
        out_specs=pl.BlockSpec(memory_space=pltpu.VMEM),
        out_shape=jax.ShapeDtypeStruct((1, rows), jnp.float32),
        compiler_params=pltpu.CompilerParams(vmem_limit_bytes=8 * MIB),
        name="reply",
    )(table, cluster.reshape(1, rows), index)
    return best.reshape(rows)


def device(chip, core, column):
    return (chip * 2 + core) * 4 + column


SWAP = [
    (device(chip, core, column), device(chip, 1 - core, column))
    for chip in range(16)
    for core in range(2)
    for column in range(4)
]
OTHER_CHIP = [
    (device(chip, core, column), device(chip, core, column ^ 1))
    for chip in range(16)
    for core in range(2)
    for column in range(4)
]


def shards(embeddings, cluster, order):
    message, index = pack(embeddings, cluster, order)
    own = lax.all_to_all(message, AXES, split_axis=0, concat_axis=0, tiled=True)

    other = lax.ppermute(own, AXES, SWAP)

    def score(lone):
        beside = lax.ppermute(lone, AXES, SWAP)
        far = lax.ppermute(lone, AXES, OTHER_CHIP)
        best, found = score_pairs(own, other, lone, beside)
        return far, finish(lone, beside, far, best, found)

    def one_round(state):
        left, table = state
        far, again = score(gather_lone(own, left)[0])
        return left - 1, score_rest(own, other, far, jnp.maximum(table, again))

    lone, more = gather_lone(own)
    table = score(lone)[1]
    table = lax.while_loop(lambda state: state[0] > 0, one_round, (more[0, 0], table))[1]
    replies = lax.all_to_all(table, AXES, split_axis=0, concat_axis=0, tiled=True)
    return read_reply(replies, cluster, index)


def solution(mesh):
    placed = (P(AXES, None), P(AXES), P(AXES))
    return jax.shard_map(
        shards, mesh=mesh, in_specs=placed, out_specs=P(AXES), check_vma=False
    )
```

```python
import functools

import jax
import jax.numpy as jnp
from jax import lax
from jax.experimental import pallas as pl
from jax.experimental.pallas import tpu as pltpu
from jax.sharding import PartitionSpec as P

D = 768
LANES = 128
HALF = LANES // 2
BLOCKS = D // LANES
SLOTS = 16
DATA = SLOTS * BLOCKS
MSG = DATA + 8
CLUSTERS = 32
PEERS = 128
ROWS = PEERS * SLOTS
GROUPS = ROWS // LANES
GROUP = LANES // SLOTS
LONE = 256
FACTS = 16
FAR = float(2**20)
BLOCK = 512
AXES = ("owner", "split")
MIB = 2**20


def slot_of(index):
    return (index & 31) >> 1


def pair_of(cluster, index):
    return ((cluster >> 1) * 2 + (index & 1)) * 2 + (cluster & 1)


def my_core():
    return lax.axis_index("owner") % 2


def my_late():
    return lax.axis_index("split") % 2


def iota(shape, axis):
    return lax.broadcasted_iota(jnp.int32, shape, axis)


def ones_where(mask):
    return jnp.where(mask, 1.0, 0.0).astype(jnp.bfloat16)


def dot_nt(a, b):
    return lax.dot_general(a, b, (((1,), (1,)), ((), ())), preferred_element_type=jnp.float32)


def dot_nn(a, b):
    return lax.dot_general(a, b, (((1,), (0,)), ((), ())), preferred_element_type=jnp.float32)


def thirds(x):
    first = x.astype(jnp.bfloat16)
    left = x - first.astype(jnp.float32)
    second = left.astype(jnp.bfloat16)
    return first, second, (left - second.astype(jnp.float32)).astype(jnp.bfloat16)


def pack_kernel(
    emb_hbm, cluster_hbm, order_hbm, out_hbm, index_ref, out_ref, emb_ref, cluster_ref, order_ref, sems, unit_ref, at_ref,
    some_ref, some_at_ref, meta_ref, past_ref
):
    rows = emb_ref.shape[0]
    pairs = PEERS // 2
    steps = 4
    tile = pairs // steps
    size = tile * SLOTS
    chunk = rows // 2
    spans = [slice(i * chunk, (i + 1) * chunk) for i in range(2)]
    fetches = [
        pltpu.make_async_copy(cluster_hbm, cluster_ref, sems.at[0, 0]),
        pltpu.make_async_copy(order_hbm, order_ref, sems.at[0, 1]),
    ] + [
        pltpu.make_async_copy(emb_hbm.at[at, :], emb_ref.at[at, :], sems.at[1, i])
        for i, at in enumerate(spans)
    ]
    for fetch in fetches:
        fetch.start()
    fetches[0].wait()
    fetches[1].wait()
    cluster = cluster_ref[...]
    rank = order_ref[...]
    hit = iota((CLUSTERS, rows), 0) == cluster
    hits = ones_where(hit)
    upper = ones_where(iota((LANES, LANES), 0) <= iota((LANES, LANES), 1))
    blocks = rows // LANES
    ahead = dot_nn(hits, ones_where(iota((rows, LANES), 0) >> 7 < iota((rows, LANES), 1)))
    counted = jnp.concatenate(
        [
            dot_nn(hits[:, b * LANES:(b + 1) * LANES], upper) + ahead[:, b:b + 1]
            for b in range(blocks)
        ],
        axis=1,
    )
    counts = jnp.broadcast_to(ahead[:, blocks:blocks + 1], (CLUSTERS, LANES))
    below = ones_where(iota((CLUSTERS, CLUSTERS), 1) < iota((CLUSTERS, CLUSTERS), 0))
    over = jnp.maximum(counts - 32.0, 0.0)
    begin = dot_nn(below, over.astype(jnp.bfloat16))

    def of_row(x):
        return jnp.sum(jnp.where(hit, x, 0.0), axis=0, keepdims=True).astype(jnp.int32)

    index = of_row(counted) - 1
    count = of_row(counts[:, :1])
    index_ref[0:1, :] = index
    index_ref[1:2, :] = count
    slot = slot_of(index)
    pair = pair_of(cluster, index)
    first = index < 32
    last = index + 32 >= count
    at_ref[0:1, :] = jnp.where(first, pair * SLOTS + slot, -1)
    at_ref[1:2, :] = jnp.where(first, -1, of_row(begin[:, :1]) + index - 32)
    at_ref[2:3, :] = pair
    at_ref[3:4, :] = slot
    past_ref[0] = jnp.sum(over[:, :1]).astype(jnp.int32)
    sends = iota((pairs, rows), 0) == pair
    sends = jnp.concatenate(
        [jnp.where(sends & first, 1.0, 0.0), jnp.where(sends & last, 1.0, 0.0)], axis=0
    )
    high = ((rank >> 9) + 1).astype(jnp.float32)
    low = ((rank & 511) - 256).astype(jnp.float32)
    at_slot = ones_where((iota((LANES, rows), 0) & (SLOTS - 1)) == slot)
    meta_ref[0] = dot_nt((sends * high).astype(jnp.bfloat16), at_slot)
    meta_ref[1] = dot_nt((sends * low).astype(jnp.bfloat16), at_slot)
    spread = jnp.where(iota((CLUSTERS, LANES), 0) == iota((CLUSTERS, LANES), 1), counts, 0.0)
    meta_ref[2] = jnp.broadcast_to(jnp.sum(spread, axis=0, keepdims=True), (PEERS, LANES))
    place = iota((PEERS, CLUSTERS), 0) & (pairs - 1)
    theirs = ones_where((place >> 2) * 2 + (place & 1) == iota((PEERS, CLUSTERS), 1))
    meta_ref[3] = dot_nn(theirs, counts.astype(jnp.bfloat16))
    for fetch, at in zip(fetches[2:], spans):
        fetch.wait()
        values = emb_ref[at, :].astype(jnp.float32)
        total = jnp.sum(values * values, axis=1, keepdims=True)
        unit_ref[at, :] = (values * lax.rsqrt(total + 1e-06)).astype(jnp.bfloat16)

    def bring(chunk):
        start = chunk * LANES
        chosen = ones_where(iota((LANES, rows), 0) + start == at_ref[1:2, :])
        some_ref[pl.ds(start, LANES), :] = dot_nn(chosen, unit_ref[...]).astype(jnp.bfloat16)
        places = jnp.where(iota((8, rows), 0) == 0, at_ref[2:3, :] + 1, at_ref[3:4, :])
        place = dot_nt(places.astype(jnp.float32).astype(jnp.bfloat16), chosen)
        target = ((place[0:1, :] - 1.0) * SLOTS + place[1:2, :]).astype(jnp.int32)
        some_at_ref[chunk] = jnp.broadcast_to(jnp.where(place[0:1, :] > 0.5, target, -1), (8, LANES))

    def early_rows(step):
        return dot_nn(ones_where(iota((size, rows), 0) + step * size == at_ref[0:1, :]), unit_ref[...])

    def spread_some(step, chunk, late):
        here = iota((size, LANES), 0) + step * size == some_at_ref[chunk][0:1, :]
        some = dot_nn(ones_where(here), some_ref[chunk * LANES:(chunk + 1) * LANES, :])
        taken = jnp.sum(jnp.where(here, 1.0, 0.0), axis=1, keepdims=True)
        return jnp.where(taken > 0.5, some, late)

    def put(step, half, rows_at):
        packed = rows_at.astype(jnp.bfloat16)
        peers = pl.ds(step * tile, tile)
        for block in range(BLOCKS):
            out_ref[peers, half, block * SLOTS:(block + 1) * SLOTS, :] = packed[
                :, block * LANES:(block + 1) * LANES
            ].reshape(tile, SLOTS, LANES)

    def send(step, half):
        peers = pl.ds(step * tile, tile)
        return pltpu.make_async_copy(out_ref.at[peers, half], out_hbm.at[peers, half], sems.at[half, step])

    at = iota((tile, 8, LANES), 1)

    def finish_tile(step, half, rows_at):
        put(step, half, rows_at)
        meta = jnp.zeros((tile, 8, LANES), jnp.float32)
        first = half * pairs + step * tile
        for i in range(4):
            meta = jnp.where(at == i, meta_ref[i, first:first + tile, :][:, None, :], meta)
        out_ref[step * tile:(step + 1) * tile, half, DATA:MSG, :] = meta.astype(jnp.bfloat16)
        send(step, half).start()

    early = []
    for step in range(steps):
        early.append(early_rows(step))
        finish_tile(step, 0, early[step])
        if step == 1:
            bring(0)
    for step in range(steps):
        finish_tile(step, 1, spread_some(step, 0, early[step]))
    for half in range(2):
        for step in range(steps):
            send(step, half).wait()

    @pl.when(past_ref[0] > LANES)
    def _():
        for chunk in range(1, rows // LANES // 2):
            bring(chunk)

        def again(step, _):
            late = early_rows(step)
            for chunk in range(rows // LANES // 2):
                late = spread_some(step, chunk, late)
            put(step, 1, late)
            send(step, 1).start()
            send(step, 1).wait()
            return 0

        lax.fori_loop(0, steps, again, 0)


def pack(embeddings, cluster, order):
    rows = embeddings.shape[0]
    message, index = pl.pallas_call(
        pack_kernel,
        in_specs=[pl.BlockSpec(memory_space=pltpu.HBM)] * 3,
        out_specs=[
            pl.BlockSpec(memory_space=pltpu.HBM),
            pl.BlockSpec(memory_space=pltpu.VMEM),
        ],
        out_shape=[
            jax.ShapeDtypeStruct((PEERS // 2, 2, MSG, LANES), jnp.bfloat16),
            jax.ShapeDtypeStruct((2, rows), jnp.int32),
        ],
        scratch_shapes=[
            pltpu.VMEM((PEERS // 2, 2, MSG, LANES), jnp.bfloat16),
            pltpu.VMEM((rows, D), jnp.bfloat16),
            pltpu.VMEM((1, rows), jnp.int32),
            pltpu.VMEM((1, rows), jnp.int32),
            pltpu.SemaphoreType.DMA((2, 4)),
            pltpu.VMEM((rows, D), jnp.bfloat16),
            pltpu.VMEM((8, rows), jnp.int32),
            pltpu.VMEM((rows // 2, D), jnp.bfloat16),
            pltpu.VMEM((rows // LANES // 2, 8, LANES), jnp.int32),
            pltpu.VMEM((4, PEERS, LANES), jnp.float32),
            pltpu.SMEM((1,), jnp.int32),
        ],
        compiler_params=pltpu.CompilerParams(vmem_limit_bytes=121 * MIB // 2),
        name="pack",
    )(embeddings, cluster.reshape(1, rows), order.reshape(1, rows))
    return message.reshape(PEERS, MSG, LANES), index


def units_of(ref, start, count):
    first, peers = start // SLOTS, count // SLOTS
    return jnp.concatenate(
        [
            ref[first:first + peers, b * SLOTS:(b + 1) * SLOTS, :].reshape(count, LANES)
            for b in range(BLOCKS)
        ],
        axis=1,
    )


def meta_of(ref):
    meta = ref[:, DATA:MSG, :].astype(jnp.float32).reshape(GROUPS, GROUP, 8, LANES)
    mine = iota((1, GROUP, 8, LANES), 3) >> 4 == iota((1, GROUP, 8, LANES), 1)
    return jnp.sum(jnp.where(mine, meta, 0.0), axis=1), meta


def rank_from(high, low):
    return jnp.where(high > 0.5, high * 512.0 + low, FAR)


def ranks_of(ref):
    held, _ = meta_of(ref)
    return rank_from(held[:, 0:1, :], held[:, 1:2, :])


def as_row(blocks):
    return jnp.concatenate([blocks[b] for b in range(GROUPS)], axis=1)


def as_columns(blocks, out_ref):
    for b in range(GROUPS):
        out_ref[b * LANES:(b + 1) * LANES, :] = jnp.broadcast_to(blocks[b], (LANES, LANES)).T


def row_of_best(ref):
    return jnp.concatenate(
        [
            jnp.max(ref[b * LANES:(b + 1) * LANES, :].T, axis=0, keepdims=True)
            for b in range(ref.shape[0] // LANES)
        ],
        axis=1,
    )


def lone_kernel(round_ref, msg_ref, out_ref, more_ref):
    core = my_core()
    first = 0 if round_ref is None else round_ref[0] * LONE
    held, meta = meta_of(msg_ref)
    high, low, count = (held[:, i:i + 1, :] for i in (0, 1, 3))
    half = jnp.floor((jnp.maximum(meta[:, :, 2, :] - 32.0, 0.0) + 1.0) * 0.5)
    most = jnp.sum(jnp.sum(half, axis=0), axis=0, keepdims=True)
    most = jnp.max(most, axis=1, keepdims=True).astype(jnp.int32)
    more_ref[...] = (most + LONE - 1) // LONE - 1

    index = (2 * (iota((GROUPS, 1, LANES), 2) & 15) + core + 32).astype(jnp.float32)
    lone = jnp.where(index < count, 1.0, 0.0)
    lone = jnp.concatenate([lone[b] for b in range(GROUPS)], axis=0).astype(jnp.bfloat16)
    upper = ones_where(iota((LANES, LANES), 0) <= iota((LANES, LANES), 1))
    counted = dot_nn(lone, upper)
    whole = jnp.broadcast_to(counted[:, LANES - 1:LANES], (GROUPS, LANES)).astype(jnp.bfloat16)
    below = ones_where(iota((GROUPS, GROUPS), 1) < iota((GROUPS, GROUPS), 0))
    position = (counted + dot_nn(below, whole)).astype(jnp.int32) - 1 - first
    position = jnp.where(lone > 0.5, position, -1)
    position = jnp.concatenate([position[b:b + 1, :] for b in range(GROUPS)], axis=1)
    chosen = ones_where(iota((LONE, ROWS), 0) == position)
    out_ref[:LONE, :] = dot_nn(chosen, units_of(msg_ref, 0, ROWS)).astype(jnp.bfloat16)
    at = iota((FACTS, ROWS), 0)
    row = iota((FACTS, ROWS), 1)
    facts = jnp.where(at == 2, row >> 4, jnp.where(at == 3, row & 15, 0)).astype(jnp.float32)
    facts = jnp.where(at == 0, as_row(high), jnp.where(at == 1, as_row(low), facts))
    facts = dot_nt(facts.astype(jnp.bfloat16), chosen).astype(jnp.bfloat16)
    out_ref[LONE:, :LONE] = facts
    out_ref[LONE:, LONE:] = jnp.zeros((FACTS, D - LONE), jnp.bfloat16)


def gather_lone(msg, round_at=None):
    some = [] if round_at is None else [round_at.reshape(1)]
    return pl.pallas_call(
        lone_kernel if some else functools.partial(lone_kernel, None),
        in_specs=[pl.BlockSpec(memory_space=pltpu.SMEM)] * len(some)
        + [pl.BlockSpec(memory_space=pltpu.VMEM)],
        out_specs=[pl.BlockSpec(memory_space=pltpu.VMEM)] * 2,
        out_shape=[
            jax.ShapeDtypeStruct((LONE + FACTS, D), jnp.bfloat16),
            jax.ShapeDtypeStruct((1, 1), jnp.int32),
        ],
        compiler_params=pltpu.CompilerParams(vmem_limit_bytes=16 * MIB),
        name="lone",
    )(*some, msg)


def narrow_rows(x):
    best = x[:, :LANES]
    for b in range(1, x.shape[1] // LANES):
        best = jnp.maximum(best, x[:, b * LANES:(b + 1) * LANES])
    return best


def narrow_cols(x):
    return jnp.max(x.reshape(x.shape[0] // 8, 8, x.shape[1]), axis=0)


def wide(column, count):
    return jnp.concatenate([column] * (count // LANES), axis=1)


def span(i):
    return slice(i * BLOCK, (i + 1) * BLOCK)


def lone_facts(ref):
    facts = ref[LONE:, :LONE].astype(jnp.float32)
    peer = jnp.where(facts[0:1, :] > 0.5, facts[2:3, :].astype(jnp.int32), -1)
    return rank_from(facts[0:1, :], facts[1:2, :]), peer, facts[3:4, :].astype(jnp.int32)


def pairs_kernel(
    own_ref, other_ref, lone_ref, beside_ref, out_ref, found_ref, rank_ref, rows_ref, cols_ref, some_ref
):
    core, late = my_core(), my_late()

    @pl.when(late == 1)
    def _():
        some_ref[...] = lone_ref[...]

    @pl.when(late == 0)
    def _():
        some_ref[...] = beside_ref[...]

    own_ranks = ranks_of(own_ref)
    as_columns(own_ranks, rank_ref)
    count = ROWS // BLOCK
    cols_ref[...] = jnp.full((8, ROWS), -1.0, jnp.float32)
    some = some_ref[:LONE, :]
    some_rank, _, _ = lone_facts(some_ref)
    found = jnp.full((8, LONE), -1.0, jnp.float32)
    for i in range(count):
        scores = dot_nt(units_of(own_ref, i * BLOCK, BLOCK), some)
        rank = wide(rank_ref[span(i), :], LONE)
        rows_ref[span(i), :] = narrow_rows(jnp.where(some_rank < rank, scores, -1.0))
        found = jnp.maximum(found, narrow_cols(jnp.where(rank < some_rank, scores, -1.0)))
    found_ref[...] = jnp.max(found, axis=0, keepdims=True)

    def score(right_ref, row, i, j, size, both):
        left_at, right_at = slice(i * size, (i + 1) * size), slice(j * size, (j + 1) * size)
        scores = dot_nt(units_of(own_ref, i * size, size), units_of(right_ref, j * size, size))
        earlier = row[:, right_at] < wide(rank_ref[left_at, :], size)
        kept = narrow_rows(jnp.where(earlier, scores, -1.0))
        rows_ref[left_at, :] = jnp.maximum(rows_ref[left_at, :], kept)
        if both:
            kept = narrow_cols(jnp.where(earlier, -1.0, scores))
            cols_ref[:, right_at] = jnp.maximum(cols_ref[:, right_at], kept)

    @pl.when(late == 0)
    def _():
        row = as_row(own_ranks)
        size = BLOCK // 2
        for i in range(2 * count):
            for j in range(i, 2 * count):
                score(own_ref, row, i, j, size, i != j)

    def across(firsts, seconds):
        row = as_row(ranks_of(other_ref))
        for i in firsts:
            for j in seconds:
                score(other_ref, row, i, j, BLOCK, True)

    @pl.when((late == 1) & (core == 0))
    def _():
        across(range(count), range(count // 2))

    @pl.when((late == 1) & (core == 1))
    def _():
        across(range(count // 2, count), range(count))

    own_best = row_of_best(rows_ref)
    cols_best = jnp.max(cols_ref[...], axis=0, keepdims=True)
    out_ref[0:1, :] = jnp.where(late == 0, jnp.maximum(own_best, cols_best), own_best)
    out_ref[1:2, :] = jnp.where(late == 0, -1.0, cols_best)


def score_pairs(own, other, lone, beside):
    vmem = pl.BlockSpec(memory_space=pltpu.VMEM)
    return pl.pallas_call(
        pairs_kernel,
        in_specs=[vmem] * 4,
        out_specs=[vmem] * 2,
        out_shape=[
            jax.ShapeDtypeStruct((2, ROWS), jnp.float32),
            jax.ShapeDtypeStruct((1, LONE), jnp.float32),
        ],
        scratch_shapes=[
            pltpu.VMEM((ROWS, LANES), jnp.float32),
            pltpu.VMEM((ROWS, LANES), jnp.float32),
            pltpu.VMEM((8, ROWS), jnp.float32),
            pltpu.VMEM((LONE + FACTS, D), jnp.bfloat16),
        ],
        compiler_params=pltpu.CompilerParams(vmem_limit_bytes=20 * MIB),
        name="pairs",
    )(own, other, lone, beside)


def as_table(row):
    mine = iota((GROUP, LANES), 1) >> 4 == iota((GROUP, LANES), 0)
    parts = []
    for b in range(GROUPS):
        part = jnp.where(mine, row[:, b * LANES:(b + 1) * LANES], 0.0)
        for shift in (64, 32, 16):
            part = part + pltpu.roll(part, shift, 1)
        parts.append(part)
    return jnp.concatenate(parts, axis=0)


def placed_by_peer(best, peer, lane):
    count = best.shape[1]
    at_peer = ones_where(iota((PEERS, count), 0) == peer)
    at_lane = iota((HALF, count), 0) == lane
    first, second, third = (part.astype(jnp.float32) for part in thirds(best))
    sums = jnp.concatenate([jnp.where(at_lane, part, 0.0) for part in (first, 1.0, second, third)], axis=0)
    sums = dot_nt(at_peer, sums.astype(jnp.bfloat16))
    front, back = sums[:, :LANES], sums[:, LANES:]
    value = front + (back + pltpu.roll(back, HALF, 1))
    return jnp.where(pltpu.roll(front, HALF, 1) > 0.5, value, -1.0)


def finish_kernel(lone_ref, beside_ref, late_ref, best_ref, found_ref, out_ref):
    core, late = my_core(), my_late()
    late_rank, late_peer, late_slot = lone_facts(late_ref)
    late_column = jnp.broadcast_to(late_rank, (LANES, LONE))
    late_column = jnp.concatenate(
        [late_column[:, b * LANES:(b + 1) * LANES].T for b in range(LONE // LANES)], axis=0
    )
    late_column = wide(late_column, LONE)
    late_best = jnp.full((LONE, LANES), -1.0, jnp.float32)
    _, own_peer, own_slot = lone_facts(lone_ref)
    _, other_peer, other_slot = lone_facts(beside_ref)
    facts = jnp.where(late == 0, lone_ref[LONE:, :], beside_ref[LONE:, :])[:, :LONE].astype(jnp.float32)
    rank = rank_from(facts[0:1, :], facts[1:2, :])
    scores = dot_nt(late_ref[:LONE, :], jnp.where(late == 0, lone_ref[:LONE, :], beside_ref[:LONE, :]))
    late_best = jnp.maximum(late_best, narrow_rows(jnp.where(rank < late_column, scores, -1.0)))
    seen = jnp.max(jnp.where(late_column < rank, scores, -1.0), axis=0, keepdims=True)
    late_best = jnp.concatenate(
        [
            jnp.max(late_best[b * LANES:(b + 1) * LANES, :].T, axis=0, keepdims=True)
            for b in range(LONE // LANES)
        ],
        axis=1,
    )
    earlier_found = found_ref[...]
    own = jnp.where(late == 0, seen, earlier_found)
    other = jnp.where(late == 0, earlier_found, seen)
    best = jnp.concatenate([own, other, late_best], axis=1)
    peer = jnp.concatenate([own_peer, other_peer, late_peer], axis=1)
    slot = jnp.concatenate(
        [own_slot + SLOTS * core, other_slot + SLOTS * (1 - core), late_slot + 2 * SLOTS], axis=1
    )
    table = placed_by_peer(best, peer, slot)
    lane = iota((PEERS, LANES), 1)
    rest = jnp.where(
        lane >> 4 == core,
        as_table(best_ref[0:1, :]),
        jnp.where(lane < 2 * SLOTS, as_table(best_ref[1:2, :]), -1.0),
    )
    out_ref[...] = jnp.where(lane < HALF, jnp.maximum(table, rest), -1.0)


def finish(lone, beside, late_rows, best, found):
    return pl.pallas_call(
        finish_kernel,
        in_specs=[pl.BlockSpec(memory_space=pltpu.VMEM)] * 5,
        out_specs=pl.BlockSpec(memory_space=pltpu.VMEM),
        out_shape=jax.ShapeDtypeStruct((PEERS, LANES), jnp.float32),
        compiler_params=pltpu.CompilerParams(vmem_limit_bytes=8 * MIB),
        name="finish",
    )(lone, beside, late_rows, best, found)


def rest_kernel(own_ref, other_ref, late_ref, table_ref, out_ref, rank_ref, rows_ref):
    core = my_core()
    some = late_ref[:LONE, :]
    some_rank, peer, slot = lone_facts(late_ref)
    found = jnp.full((8, LONE), -1.0, jnp.float32)
    best = []
    for ref in (own_ref, other_ref):
        as_columns(ranks_of(ref), rank_ref)
        for i in range(ROWS // BLOCK):
            scores = dot_nt(units_of(ref, i * BLOCK, BLOCK), some)
            rank = wide(rank_ref[span(i), :], LONE)
            rows_ref[span(i), :] = narrow_rows(jnp.where(some_rank < rank, scores, -1.0))
            found = jnp.maximum(found, narrow_cols(jnp.where(rank < some_rank, scores, -1.0)))
        best.append(as_table(row_of_best(rows_ref)))
    table = placed_by_peer(jnp.max(found, axis=0, keepdims=True), peer, slot + 2 * SLOTS)
    lane = iota((PEERS, LANES), 1)
    rest = jnp.where(lane >> 4 == core, best[0], jnp.where(lane < 2 * SLOTS, best[1], table))
    out_ref[...] = jnp.maximum(table_ref[...], jnp.where(lane < HALF, rest, -1.0))


def score_rest(own, other, late_rows, table):
    return pl.pallas_call(
        rest_kernel,
        in_specs=[pl.BlockSpec(memory_space=pltpu.VMEM)] * 4,
        out_specs=pl.BlockSpec(memory_space=pltpu.VMEM),
        out_shape=jax.ShapeDtypeStruct((PEERS, LANES), jnp.float32),
        scratch_shapes=[
            pltpu.VMEM((ROWS, LANES), jnp.float32),
            pltpu.VMEM((ROWS, LANES), jnp.float32),
        ],
        compiler_params=pltpu.CompilerParams(vmem_limit_bytes=20 * MIB),
        name="rest",
    )(own, other, late_rows, table)


def reply_kernel(table_ref, cluster_ref, index_ref, out_ref):
    cluster = cluster_ref[...]
    index = index_ref[0:1, :]
    count = index_ref[1:2, :]
    rows = cluster.shape[1]
    table = table_ref[...]
    lane = iota((PEERS, LANES), 1)
    early = jnp.maximum(table, pltpu.roll(table, PEERS - 4, 0))
    beside = jnp.where(
        lane < SLOTS,
        pltpu.roll(table, LANES - 2 * SLOTS, 1),
        pltpu.roll(pltpu.roll(table, PEERS - 4, 0), LANES - SLOTS, 1),
    )
    late = jnp.maximum(pltpu.roll(early, PEERS - 1, 0), beside)
    early = jnp.maximum(early, pltpu.roll(beside, PEERS - 1, 0))
    both = jnp.concatenate([early.T[:2 * SLOTS, :], late.T[:2 * SLOTS, :]], axis=0)
    chosen = ones_where(iota((PEERS, rows), 0) == pair_of(cluster, jnp.zeros_like(index)) * 2)
    picked = dot_nn(jnp.concatenate(thirds(both), axis=0), chosen)
    size = 4 * SLOTS
    picked = picked[:size, :] + (picked[size:2 * size, :] + picked[2 * size:, :])
    at = (index & 1) * SLOTS + slot_of(index)
    here = iota((4 * SLOTS, rows), 0)
    here = ((here == at) & (index < 32)) | ((here == at + 2 * SLOTS) & (index + 32 >= count))
    out_ref[...] = jnp.max(jnp.where(here, picked, -1.0), axis=0, keepdims=True)


def read_reply(table, cluster, index):
    rows = cluster.shape[0]
    best = pl.pallas_call(
        reply_kernel,
        in_specs=[pl.BlockSpec(memory_space=pltpu.VMEM)] * 3,
        out_specs=pl.BlockSpec(memory_space=pltpu.VMEM),
        out_shape=jax.ShapeDtypeStruct((1, rows), jnp.float32),
        compiler_params=pltpu.CompilerParams(vmem_limit_bytes=8 * MIB),
        name="reply",
    )(table, cluster.reshape(1, rows), index)
    return best.reshape(rows)


def device(chip, core, column):
    return (chip * 2 + core) * 4 + column


SWAP = [
    (device(chip, core, column), device(chip, 1 - core, column))
    for chip in range(16)
    for core in range(2)
    for column in range(4)
]
OTHER_CHIP = [
    (device(chip, core, column), device(chip, core, column ^ 1))
    for chip in range(16)
    for core in range(2)
    for column in range(4)
]


def shards(embeddings, cluster, order):
    message, index = pack(embeddings, cluster, order)
    own = lax.all_to_all(message, AXES, split_axis=0, concat_axis=0, tiled=True)

    other = lax.ppermute(own, AXES, SWAP)

    def score(lone):
        beside = lax.ppermute(lone, AXES, SWAP)
        far = lax.ppermute(lone, AXES, OTHER_CHIP)
        best, found = score_pairs(own, other, lone, beside)
        return far, finish(lone, beside, far, best, found)

    def one_round(state):
        left, table = state
        far, again = score(gather_lone(own, left[0, 0])[0])
        return left - 1, score_rest(own, other, far, jnp.maximum(table, again))

    lone, more = gather_lone(own)
    table = score(lone)[1]
    table = lax.while_loop(lambda state: state[0][0, 0] > 0, one_round, (more, table))[1]
    replies = lax.all_to_all(table, AXES, split_axis=0, concat_axis=0, tiled=True)
    return read_reply(replies, cluster, index)


def solution(mesh):
    placed = (P(AXES, None), P(AXES), P(AXES))
    return jax.shard_map(
        shards, mesh=mesh, in_specs=placed, out_specs=P(AXES), check_vma=False
    )
```

```python
import functools

import jax
import jax.numpy as jnp
from jax import lax
from jax.experimental import pallas as pl
from jax.experimental.pallas import tpu as pltpu
from jax.sharding import PartitionSpec as P

D = 768
LANES = 128
HALF = LANES // 2
BLOCKS = D // LANES
SLOTS = 16
DATA = SLOTS * BLOCKS
MSG = DATA + 8
CLUSTERS = 32
PEERS = 128
ROWS = PEERS * SLOTS
GROUPS = ROWS // LANES
GROUP = LANES // SLOTS
LONE = 256
FACTS = 16
FAR = float(2**20)
BLOCK = 512
AXES = ("owner", "split")
MIB = 2**20


def slot_of(index):
    return (index & 31) >> 1


def pair_of(cluster, index):
    return ((cluster >> 1) * 2 + (index & 1)) * 2 + (cluster & 1)


def my_core():
    return lax.axis_index("owner") % 2


def my_late():
    return lax.axis_index("split") % 2


def iota(shape, axis):
    return lax.broadcasted_iota(jnp.int32, shape, axis)


def ones_where(mask):
    return jnp.where(mask, 1.0, 0.0).astype(jnp.bfloat16)


def dot_nt(a, b):
    return lax.dot_general(a, b, (((1,), (1,)), ((), ())), preferred_element_type=jnp.float32)


def dot_nn(a, b):
    return lax.dot_general(a, b, (((1,), (0,)), ((), ())), preferred_element_type=jnp.float32)


def thirds(x):
    first = x.astype(jnp.bfloat16)
    left = x - first.astype(jnp.float32)
    second = left.astype(jnp.bfloat16)
    return first, second, (left - second.astype(jnp.float32)).astype(jnp.bfloat16)


def pack_kernel(
    emb_hbm, cluster_hbm, order_hbm, out_hbm, index_ref, out_ref, emb_ref, cluster_ref, order_ref, sems, unit_ref, at_ref,
    some_ref, some_at_ref, meta_ref, past_ref
):
    rows = emb_ref.shape[0]
    pairs = PEERS // 2
    steps = 8
    tile = pairs // steps
    size = tile * SLOTS
    chunk = rows // 2
    spans = [slice(i * chunk, (i + 1) * chunk) for i in range(2)]
    fetches = [
        pltpu.make_async_copy(cluster_hbm, cluster_ref, sems.at[4]),
        pltpu.make_async_copy(order_hbm, order_ref, sems.at[5]),
    ] + [
        pltpu.make_async_copy(emb_hbm.at[at, :], emb_ref.at[at, :], sems.at[i])
        for i, at in enumerate(spans)
    ]
    for fetch in fetches:
        fetch.start()
    fetches[0].wait()
    fetches[1].wait()
    cluster = cluster_ref[...]
    rank = order_ref[...]
    hit = iota((CLUSTERS, rows), 0) == cluster
    hits = ones_where(hit)
    upper = ones_where(iota((LANES, LANES), 0) <= iota((LANES, LANES), 1))
    blocks = rows // LANES
    ahead = dot_nn(hits, ones_where(iota((rows, LANES), 0) >> 7 < iota((rows, LANES), 1)))
    counted = jnp.concatenate(
        [
            dot_nn(hits[:, b * LANES:(b + 1) * LANES], upper) + ahead[:, b:b + 1]
            for b in range(blocks)
        ],
        axis=1,
    )
    counts = jnp.broadcast_to(ahead[:, blocks:blocks + 1], (CLUSTERS, LANES))
    below = ones_where(iota((CLUSTERS, CLUSTERS), 1) < iota((CLUSTERS, CLUSTERS), 0))
    over = jnp.maximum(counts - 32.0, 0.0)
    begin = dot_nn(below, over.astype(jnp.bfloat16))

    def of_row(x):
        return jnp.sum(jnp.where(hit, x, 0.0), axis=0, keepdims=True).astype(jnp.int32)

    index = of_row(counted) - 1
    count = of_row(counts[:, :1])
    index_ref[0:1, :] = index
    index_ref[1:2, :] = count
    slot = slot_of(index)
    pair = pair_of(cluster, index)
    first = index < 32
    last = index + 32 >= count
    at_ref[0:1, :] = jnp.where(first, pair * SLOTS + slot, -1)
    at_ref[1:2, :] = jnp.where(first, -1, of_row(begin[:, :1]) + index - 32)
    at_ref[2:3, :] = pair
    at_ref[3:4, :] = slot
    past_ref[0] = jnp.sum(over[:, :1]).astype(jnp.int32)
    sends = iota((pairs, rows), 0) == pair
    sends = jnp.concatenate(
        [jnp.where(sends & first, 1.0, 0.0), jnp.where(sends & last, 1.0, 0.0)], axis=0
    )
    high = ((rank >> 9) + 1).astype(jnp.float32)
    low = ((rank & 511) - 256).astype(jnp.float32)
    at_slot = ones_where((iota((LANES, rows), 0) & (SLOTS - 1)) == slot)
    meta_ref[0] = dot_nt((sends * high).astype(jnp.bfloat16), at_slot)
    meta_ref[1] = dot_nt((sends * low).astype(jnp.bfloat16), at_slot)
    spread = jnp.where(iota((CLUSTERS, LANES), 0) == iota((CLUSTERS, LANES), 1), counts, 0.0)
    meta_ref[2] = jnp.broadcast_to(jnp.sum(spread, axis=0, keepdims=True), (PEERS, LANES))
    place = iota((PEERS, CLUSTERS), 0) & (pairs - 1)
    theirs = ones_where((place >> 2) * 2 + (place & 1) == iota((PEERS, CLUSTERS), 1))
    meta_ref[3] = dot_nn(theirs, counts.astype(jnp.bfloat16))
    for fetch, at in zip(fetches[2:], spans):
        fetch.wait()
        values = emb_ref[at, :].astype(jnp.float32)
        total = jnp.sum(values * values, axis=1, keepdims=True)
        unit_ref[at, :] = (values * lax.rsqrt(total + 1e-06)).astype(jnp.bfloat16)

    def bring(chunk):
        start = chunk * LANES
        chosen = ones_where(iota((LANES, rows), 0) + start == at_ref[1:2, :])
        some_ref[pl.ds(start, LANES), :] = dot_nn(chosen, unit_ref[...]).astype(jnp.bfloat16)
        places = jnp.where(iota((8, rows), 0) == 0, at_ref[2:3, :] + 1, at_ref[3:4, :])
        place = dot_nt(places.astype(jnp.float32).astype(jnp.bfloat16), chosen)
        target = ((place[0:1, :] - 1.0) * SLOTS + place[1:2, :]).astype(jnp.int32)
        some_at_ref[chunk] = jnp.broadcast_to(jnp.where(place[0:1, :] > 0.5, target, -1), (8, LANES))

    bring(0)

    def early_rows(step):
        return dot_nn(ones_where(iota((size, rows), 0) + step * size == at_ref[0:1, :]), unit_ref[...])

    def spread_some(step, chunk, late):
        here = iota((size, LANES), 0) + step * size == some_at_ref[chunk][0:1, :]
        some = dot_nn(ones_where(here), some_ref[chunk * LANES:(chunk + 1) * LANES, :])
        taken = jnp.sum(jnp.where(here, 1.0, 0.0), axis=1, keepdims=True)
        return jnp.where(taken > 0.5, some, late)

    def put(step, half, rows_at):
        packed = rows_at.astype(jnp.bfloat16)
        peers = pl.ds(step * tile, tile)
        for block in range(BLOCKS):
            out_ref[peers, half, block * SLOTS:(block + 1) * SLOTS, :] = packed[
                :, block * LANES:(block + 1) * LANES
            ].reshape(tile, SLOTS, LANES)

    def send(step):
        peers = pl.ds(step * tile, tile)
        return pltpu.make_async_copy(out_ref.at[peers], out_hbm.at[peers], sems.at[step])

    at = iota((tile, 8, LANES), 1)
    for step in range(steps):
        early = early_rows(step)
        put(step, 0, early)
        put(step, 1, spread_some(step, 0, early))
        for half in range(2):
            meta = jnp.zeros((tile, 8, LANES), jnp.float32)
            first = half * pairs + step * tile
            for i in range(4):
                meta = jnp.where(at == i, meta_ref[i, first:first + tile, :][:, None, :], meta)
            out_ref[step * tile:(step + 1) * tile, half, DATA:MSG, :] = meta.astype(jnp.bfloat16)
        send(step).start()
    for step in range(steps):
        send(step).wait()

    @pl.when(past_ref[0] > LANES)
    def _():
        for chunk in range(1, rows // LANES // 2):
            bring(chunk)

        def again(step, _):
            late = early_rows(step)
            for chunk in range(rows // LANES // 2):
                late = spread_some(step, chunk, late)
            put(step, 1, late)
            send(step).start()
            send(step).wait()
            return 0

        lax.fori_loop(0, steps, again, 0)


def pack(embeddings, cluster, order):
    rows = embeddings.shape[0]
    message, index = pl.pallas_call(
        pack_kernel,
        in_specs=[pl.BlockSpec(memory_space=pltpu.HBM)] * 3,
        out_specs=[
            pl.BlockSpec(memory_space=pltpu.HBM),
            pl.BlockSpec(memory_space=pltpu.VMEM),
        ],
        out_shape=[
            jax.ShapeDtypeStruct((PEERS // 2, 2, MSG, LANES), jnp.bfloat16),
            jax.ShapeDtypeStruct((2, rows), jnp.int32),
        ],
        scratch_shapes=[
            pltpu.VMEM((PEERS // 2, 2, MSG, LANES), jnp.bfloat16),
            pltpu.VMEM((rows, D), jnp.bfloat16),
            pltpu.VMEM((1, rows), jnp.int32),
            pltpu.VMEM((1, rows), jnp.int32),
            pltpu.SemaphoreType.DMA((8,)),
            pltpu.VMEM((rows, D), jnp.bfloat16),
            pltpu.VMEM((8, rows), jnp.int32),
            pltpu.VMEM((rows // 2, D), jnp.bfloat16),
            pltpu.VMEM((rows // LANES // 2, 8, LANES), jnp.int32),
            pltpu.VMEM((4, PEERS, LANES), jnp.float32),
            pltpu.SMEM((1,), jnp.int32),
        ],
        compiler_params=pltpu.CompilerParams(vmem_limit_bytes=121 * MIB // 2),
        name="pack",
    )(embeddings, cluster.reshape(1, rows), order.reshape(1, rows))
    return message.reshape(PEERS, MSG, LANES), index


def units_of(ref, start, count):
    first, peers = start // SLOTS, count // SLOTS
    return jnp.concatenate(
        [
            ref[first:first + peers, b * SLOTS:(b + 1) * SLOTS, :].reshape(count, LANES)
            for b in range(BLOCKS)
        ],
        axis=1,
    )


def meta_of(ref):
    meta = ref[:, DATA:MSG, :].astype(jnp.float32).reshape(GROUPS, GROUP, 8, LANES)
    mine = iota((1, GROUP, 8, LANES), 3) >> 4 == iota((1, GROUP, 8, LANES), 1)
    return jnp.sum(jnp.where(mine, meta, 0.0), axis=1), meta


def rank_from(high, low):
    return jnp.where(high > 0.5, high * 512.0 + low, FAR)


def ranks_of(ref):
    held, _ = meta_of(ref)
    return rank_from(held[:, 0:1, :], held[:, 1:2, :])


def as_row(blocks):
    return jnp.concatenate([blocks[b] for b in range(GROUPS)], axis=1)


def as_columns(blocks, out_ref):
    for b in range(GROUPS):
        out_ref[b * LANES:(b + 1) * LANES, :] = jnp.broadcast_to(blocks[b], (LANES, LANES)).T


def row_of_best(ref):
    return jnp.concatenate(
        [
            jnp.max(ref[b * LANES:(b + 1) * LANES, :].T, axis=0, keepdims=True)
            for b in range(ref.shape[0] // LANES)
        ],
        axis=1,
    )


def lone_kernel(round_ref, msg_ref, out_ref, more_ref):
    core = my_core()
    first = 0 if round_ref is None else round_ref[0] * LONE
    held, meta = meta_of(msg_ref)
    high, low, count = (held[:, i:i + 1, :] for i in (0, 1, 3))
    half = jnp.floor((jnp.maximum(meta[:, :, 2, :] - 32.0, 0.0) + 1.0) * 0.5)
    most = jnp.sum(jnp.sum(half, axis=0), axis=0, keepdims=True)
    most = jnp.max(most, axis=1, keepdims=True).astype(jnp.int32)
    more_ref[...] = (most + LONE - 1) // LONE - 1

    index = (2 * (iota((GROUPS, 1, LANES), 2) & 15) + core + 32).astype(jnp.float32)
    lone = jnp.where(index < count, 1.0, 0.0)
    lone = jnp.concatenate([lone[b] for b in range(GROUPS)], axis=0).astype(jnp.bfloat16)
    upper = ones_where(iota((LANES, LANES), 0) <= iota((LANES, LANES), 1))
    counted = dot_nn(lone, upper)
    whole = jnp.broadcast_to(counted[:, LANES - 1:LANES], (GROUPS, LANES)).astype(jnp.bfloat16)
    below = ones_where(iota((GROUPS, GROUPS), 1) < iota((GROUPS, GROUPS), 0))
    position = (counted + dot_nn(below, whole)).astype(jnp.int32) - 1 - first
    position = jnp.where(lone > 0.5, position, -1)
    position = jnp.concatenate([position[b:b + 1, :] for b in range(GROUPS)], axis=1)
    chosen = ones_where(iota((LONE, ROWS), 0) == position)
    out_ref[:LONE, :] = dot_nn(chosen, units_of(msg_ref, 0, ROWS)).astype(jnp.bfloat16)
    at = iota((FACTS, ROWS), 0)
    row = iota((FACTS, ROWS), 1)
    facts = jnp.where(at == 2, row >> 4, jnp.where(at == 3, row & 15, 0)).astype(jnp.float32)
    facts = jnp.where(at == 0, as_row(high), jnp.where(at == 1, as_row(low), facts))
    facts = dot_nt(facts.astype(jnp.bfloat16), chosen).astype(jnp.bfloat16)
    out_ref[LONE:, :LONE] = facts
    out_ref[LONE:, LONE:] = jnp.zeros((FACTS, D - LONE), jnp.bfloat16)


def gather_lone(msg, round_at=None):
    some = [] if round_at is None else [round_at.reshape(1)]
    return pl.pallas_call(
        lone_kernel if some else functools.partial(lone_kernel, None),
        in_specs=[pl.BlockSpec(memory_space=pltpu.SMEM)] * len(some)
        + [pl.BlockSpec(memory_space=pltpu.VMEM)],
        out_specs=[pl.BlockSpec(memory_space=pltpu.VMEM)] * 2,
        out_shape=[
            jax.ShapeDtypeStruct((LONE + FACTS, D), jnp.bfloat16),
            jax.ShapeDtypeStruct((1, 1), jnp.int32),
        ],
        compiler_params=pltpu.CompilerParams(vmem_limit_bytes=16 * MIB),
        name="lone",
    )(*some, msg)


def narrow_rows(x):
    best = x[:, :LANES]
    for b in range(1, x.shape[1] // LANES):
        best = jnp.maximum(best, x[:, b * LANES:(b + 1) * LANES])
    return best


def narrow_cols(x):
    return jnp.max(x.reshape(x.shape[0] // 8, 8, x.shape[1]), axis=0)


def wide(column, count):
    return jnp.concatenate([column] * (count // LANES), axis=1)


def span(i):
    return slice(i * BLOCK, (i + 1) * BLOCK)


def lone_facts(ref):
    facts = ref[LONE:, :LONE].astype(jnp.float32)
    peer = jnp.where(facts[0:1, :] > 0.5, facts[2:3, :].astype(jnp.int32), -1)
    return rank_from(facts[0:1, :], facts[1:2, :]), peer, facts[3:4, :].astype(jnp.int32)


def pairs_kernel(
    own_ref, other_ref, lone_ref, beside_ref, out_ref, found_ref, rank_ref, rows_ref, cols_ref, some_ref
):
    core, late = my_core(), my_late()

    @pl.when(late == 1)
    def _():
        some_ref[...] = lone_ref[...]

    @pl.when(late == 0)
    def _():
        some_ref[...] = beside_ref[...]

    own_ranks = ranks_of(own_ref)
    as_columns(own_ranks, rank_ref)
    count = ROWS // BLOCK
    cols_ref[...] = jnp.full((8, ROWS), -1.0, jnp.float32)
    some = some_ref[:LONE, :]
    some_rank, _, _ = lone_facts(some_ref)
    found = jnp.full((8, LONE), -1.0, jnp.float32)
    for i in range(count):
        scores = dot_nt(units_of(own_ref, i * BLOCK, BLOCK), some)
        rank = wide(rank_ref[span(i), :], LONE)
        rows_ref[span(i), :] = narrow_rows(jnp.where(some_rank < rank, scores, -1.0))
        found = jnp.maximum(found, narrow_cols(jnp.where(rank < some_rank, scores, -1.0)))
    found_ref[...] = jnp.max(found, axis=0, keepdims=True)

    def score(right_ref, row, i, j, size, both):
        left_at, right_at = slice(i * size, (i + 1) * size), slice(j * size, (j + 1) * size)
        scores = dot_nt(units_of(own_ref, i * size, size), units_of(right_ref, j * size, size))
        earlier = row[:, right_at] < wide(rank_ref[left_at, :], size)
        kept = narrow_rows(jnp.where(earlier, scores, -1.0))
        rows_ref[left_at, :] = jnp.maximum(rows_ref[left_at, :], kept)
        if both:
            kept = narrow_cols(jnp.where(earlier, -1.0, scores))
            cols_ref[:, right_at] = jnp.maximum(cols_ref[:, right_at], kept)

    @pl.when(late == 0)
    def _():
        row = as_row(own_ranks)
        size = BLOCK // 2
        for i in range(2 * count):
            for j in range(i, 2 * count):
                score(own_ref, row, i, j, size, i != j)

    def across(firsts, seconds):
        row = as_row(ranks_of(other_ref))
        for i in firsts:
            for j in seconds:
                score(other_ref, row, i, j, BLOCK, True)

    @pl.when((late == 1) & (core == 0))
    def _():
        across(range(count), range(count // 2))

    @pl.when((late == 1) & (core == 1))
    def _():
        across(range(count // 2, count), range(count))

    own_best = row_of_best(rows_ref)
    cols_best = jnp.max(cols_ref[...], axis=0, keepdims=True)
    out_ref[0:1, :] = jnp.where(late == 0, jnp.maximum(own_best, cols_best), own_best)
    out_ref[1:2, :] = jnp.where(late == 0, -1.0, cols_best)


def score_pairs(own, other, lone, beside):
    vmem = pl.BlockSpec(memory_space=pltpu.VMEM)
    return pl.pallas_call(
        pairs_kernel,
        in_specs=[vmem] * 4,
        out_specs=[vmem] * 2,
        out_shape=[
            jax.ShapeDtypeStruct((2, ROWS), jnp.float32),
            jax.ShapeDtypeStruct((1, LONE), jnp.float32),
        ],
        scratch_shapes=[
            pltpu.VMEM((ROWS, LANES), jnp.float32),
            pltpu.VMEM((ROWS, LANES), jnp.float32),
            pltpu.VMEM((8, ROWS), jnp.float32),
            pltpu.VMEM((LONE + FACTS, D), jnp.bfloat16),
        ],
        compiler_params=pltpu.CompilerParams(vmem_limit_bytes=20 * MIB),
        name="pairs",
    )(own, other, lone, beside)


def as_table(row):
    mine = iota((GROUP, LANES), 1) >> 4 == iota((GROUP, LANES), 0)
    parts = []
    for b in range(GROUPS):
        part = jnp.where(mine, row[:, b * LANES:(b + 1) * LANES], 0.0)
        for shift in (64, 32, 16):
            part = part + pltpu.roll(part, shift, 1)
        parts.append(part)
    return jnp.concatenate(parts, axis=0)


def placed_by_peer(best, peer, lane):
    count = best.shape[1]
    at_peer = ones_where(iota((PEERS, count), 0) == peer)
    at_lane = iota((HALF, count), 0) == lane
    first, second, third = (part.astype(jnp.float32) for part in thirds(best))
    sums = jnp.concatenate([jnp.where(at_lane, part, 0.0) for part in (first, 1.0, second, third)], axis=0)
    sums = dot_nt(at_peer, sums.astype(jnp.bfloat16))
    front, back = sums[:, :LANES], sums[:, LANES:]
    value = front + (back + pltpu.roll(back, HALF, 1))
    return jnp.where(pltpu.roll(front, HALF, 1) > 0.5, value, -1.0)


def finish_kernel(lone_ref, beside_ref, late_ref, best_ref, found_ref, out_ref):
    core, late = my_core(), my_late()
    late_rank, late_peer, late_slot = lone_facts(late_ref)
    late_column = jnp.broadcast_to(late_rank, (LANES, LONE))
    late_column = jnp.concatenate(
        [late_column[:, b * LANES:(b + 1) * LANES].T for b in range(LONE // LANES)], axis=0
    )
    late_column = wide(late_column, LONE)
    late_best = jnp.full((LONE, LANES), -1.0, jnp.float32)
    found = []
    for ref in (lone_ref, beside_ref):
        rank, peer, slot = lone_facts(ref)
        scores = dot_nt(late_ref[:LONE, :], ref[:LONE, :])
        late_best = jnp.maximum(late_best, narrow_rows(jnp.where(rank < late_column, scores, -1.0)))
        best = jnp.max(jnp.where(late_column < rank, scores, -1.0), axis=0, keepdims=True)
        found.append((best, peer, slot))
    late_best = jnp.concatenate(
        [
            jnp.max(late_best[b * LANES:(b + 1) * LANES, :].T, axis=0, keepdims=True)
            for b in range(LONE // LANES)
        ],
        axis=1,
    )
    earlier_found = found_ref[...]
    own = jnp.maximum(found[0][0], jnp.where(late == 1, earlier_found, -1.0))
    other = jnp.maximum(found[1][0], jnp.where(late == 0, earlier_found, -1.0))
    best = jnp.concatenate([own, other, late_best], axis=1)
    peer = jnp.concatenate([found[0][1], found[1][1], late_peer], axis=1)
    slot = jnp.concatenate(
        [found[0][2] + SLOTS * core, found[1][2] + SLOTS * (1 - core), late_slot + 2 * SLOTS], axis=1
    )
    table = placed_by_peer(best, peer, slot)
    lane = iota((PEERS, LANES), 1)
    rest = jnp.where(
        lane >> 4 == core,
        as_table(best_ref[0:1, :]),
        jnp.where(lane < 2 * SLOTS, as_table(best_ref[1:2, :]), -1.0),
    )
    out_ref[...] = jnp.where(lane < HALF, jnp.maximum(table, rest), -1.0)


def finish(lone, beside, late_rows, best, found):
    return pl.pallas_call(
        finish_kernel,
        in_specs=[pl.BlockSpec(memory_space=pltpu.VMEM)] * 5,
        out_specs=pl.BlockSpec(memory_space=pltpu.VMEM),
        out_shape=jax.ShapeDtypeStruct((PEERS, LANES), jnp.float32),
        compiler_params=pltpu.CompilerParams(vmem_limit_bytes=8 * MIB),
        name="finish",
    )(lone, beside, late_rows, best, found)


def rest_kernel(own_ref, other_ref, late_ref, table_ref, out_ref, rank_ref, rows_ref):
    core = my_core()
    some = late_ref[:LONE, :]
    some_rank, peer, slot = lone_facts(late_ref)
    found = jnp.full((8, LONE), -1.0, jnp.float32)
    best = []
    for ref in (own_ref, other_ref):
        as_columns(ranks_of(ref), rank_ref)
        for i in range(ROWS // BLOCK):
            scores = dot_nt(units_of(ref, i * BLOCK, BLOCK), some)
            rank = wide(rank_ref[span(i), :], LONE)
            rows_ref[span(i), :] = narrow_rows(jnp.where(some_rank < rank, scores, -1.0))
            found = jnp.maximum(found, narrow_cols(jnp.where(rank < some_rank, scores, -1.0)))
        best.append(as_table(row_of_best(rows_ref)))
    table = placed_by_peer(jnp.max(found, axis=0, keepdims=True), peer, slot + 2 * SLOTS)
    lane = iota((PEERS, LANES), 1)
    rest = jnp.where(lane >> 4 == core, best[0], jnp.where(lane < 2 * SLOTS, best[1], table))
    out_ref[...] = jnp.maximum(table_ref[...], jnp.where(lane < HALF, rest, -1.0))


def score_rest(own, other, late_rows, table):
    return pl.pallas_call(
        rest_kernel,
        in_specs=[pl.BlockSpec(memory_space=pltpu.VMEM)] * 4,
        out_specs=pl.BlockSpec(memory_space=pltpu.VMEM),
        out_shape=jax.ShapeDtypeStruct((PEERS, LANES), jnp.float32),
        scratch_shapes=[
            pltpu.VMEM((ROWS, LANES), jnp.float32),
            pltpu.VMEM((ROWS, LANES), jnp.float32),
        ],
        compiler_params=pltpu.CompilerParams(vmem_limit_bytes=20 * MIB),
        name="rest",
    )(own, other, late_rows, table)


def reply_kernel(table_ref, cluster_ref, index_ref, out_ref):
    cluster = cluster_ref[...]
    index = index_ref[0:1, :]
    count = index_ref[1:2, :]
    rows = cluster.shape[1]
    table = table_ref[...]
    lane = iota((PEERS, LANES), 1)
    early = jnp.maximum(table, pltpu.roll(table, PEERS - 4, 0))
    beside = jnp.where(
        lane < SLOTS,
        pltpu.roll(table, LANES - 2 * SLOTS, 1),
        pltpu.roll(pltpu.roll(table, PEERS - 4, 0), LANES - SLOTS, 1),
    )
    late = jnp.maximum(pltpu.roll(early, PEERS - 1, 0), beside)
    early = jnp.maximum(early, pltpu.roll(beside, PEERS - 1, 0))
    both = jnp.concatenate([early.T[:2 * SLOTS, :], late.T[:2 * SLOTS, :]], axis=0)
    chosen = ones_where(iota((PEERS, rows), 0) == pair_of(cluster, jnp.zeros_like(index)) * 2)
    picked = dot_nn(jnp.concatenate(thirds(both), axis=0), chosen)
    size = 4 * SLOTS
    picked = picked[:size, :] + (picked[size:2 * size, :] + picked[2 * size:, :])
    at = (index & 1) * SLOTS + slot_of(index)
    here = iota((4 * SLOTS, rows), 0)
    here = ((here == at) & (index < 32)) | ((here == at + 2 * SLOTS) & (index + 32 >= count))
    out_ref[...] = jnp.max(jnp.where(here, picked, -1.0), axis=0, keepdims=True)


def read_reply(table, cluster, index):
    rows = cluster.shape[0]
    best = pl.pallas_call(
        reply_kernel,
        in_specs=[pl.BlockSpec(memory_space=pltpu.VMEM)] * 3,
        out_specs=pl.BlockSpec(memory_space=pltpu.VMEM),
        out_shape=jax.ShapeDtypeStruct((1, rows), jnp.float32),
        compiler_params=pltpu.CompilerParams(vmem_limit_bytes=8 * MIB),
        name="reply",
    )(table, cluster.reshape(1, rows), index)
    return best.reshape(rows)


def device(chip, core, column):
    return (chip * 2 + core) * 4 + column


SWAP = [
    (device(chip, core, column), device(chip, 1 - core, column))
    for chip in range(16)
    for core in range(2)
    for column in range(4)
]
OTHER_CHIP = [
    (device(chip, core, column), device(chip, core, column ^ 1))
    for chip in range(16)
    for core in range(2)
    for column in range(4)
]


def shards(embeddings, cluster, order):
    message, index = pack(embeddings, cluster, order)
    own = lax.all_to_all(message, AXES, split_axis=0, concat_axis=0, tiled=True)

    other = lax.ppermute(own, AXES, SWAP)

    def score(lone):
        beside = lax.ppermute(lone, AXES, SWAP)
        far = lax.ppermute(lone, AXES, OTHER_CHIP)
        best, found = score_pairs(own, other, lone, beside)
        return far, finish(lone, beside, far, best, found)

    def one_round(state):
        left, table = state
        far, again = score(gather_lone(own, left)[0])
        return left - 1, score_rest(own, other, far, jnp.maximum(table, again))

    lone, more = gather_lone(own)
    table = score(lone)[1]
    table = lax.while_loop(lambda state: state[0] > 0, one_round, (more[0, 0], table))[1]
    replies = lax.all_to_all(table, AXES, split_axis=0, concat_axis=0, tiled=True)
    return read_reply(replies, cluster, index)


def solution(mesh):
    placed = (P(AXES, None), P(AXES), P(AXES))
    return jax.shard_map(
        shards, mesh=mesh, in_specs=placed, out_specs=P(AXES), check_vma=False
    )
```
